32 devices in a mesh: sp: 8 (over y, x, core), dp: 4 (over z).
Axes of the slice: x: 2, y: 2, z: 4, core: 2. Of those that a mesh axis runs over, the one named last changes fastest.
Arguments:
- tokens: bfloat16 [4, 3072, 768], P('dp', 'sp'), may hold values from -6 to 6
- ln1_gain: float32 [768], replicated, may hold values from 0.5 to 1.5
- ln1_shift: float32 [768], replicated, may hold values from -1.2 to 1.2
- w_qkv: bfloat16 [768, 2304], replicated, may hold values from -0.21875 to 0.21875
- w_out: bfloat16 [768, 768], replicated, may hold values from -1.75 to 1.75
- ln2_gain: float32 [768], replicated, may hold values from 0.5 to 1.5
- ln2_shift: float32 [768], replicated, may hold values from -1.2 to 1.2
- w_router: bfloat16 [768, 16], replicated, may hold values from -0.21875 to 0.21875
- train_w1: bfloat16 [8, 768, 3072], P('sp', None, 'dp'), may hold values from -0.21875 to 0.21875
- train_w2: bfloat16 [8, 3072, 768], P('sp', 'dp'), may hold values from -0.109375 to 0.109375
- frozen_w1: bfloat16 [8, 768, 3072], P('sp', None, 'dp'), may hold values from -0.21875 to 0.21875
- frozen_w2: bfloat16 [8, 3072, 768], P('sp', 'dp'), may hold values from -0.109375 to 0.109375
- routes: int32 [4, 3072, 2], P('dp', 'sp'), may hold values from 0 to 15, all different within a row; in each aligned block of 384 rows (0 to 383, 384 to 767, ..., all dimensions but the last counted through in order) at most 96 rows name the same one
- cotangent: bfloat16 [4, 3072, 768], P('dp', 'sp'), may hold values from -6 to 6
Outputs:
- block_out: bfloat16 [4, 3072, 768], P('dp', 'sp')
- tokens_grad: float32 [4, 3072, 768], P('dp', 'sp')
- ln1_gain_grad: float32 [768], replicated
- ln1_shift_grad: float32 [768], replicated
- qkv_grad: float32 [768, 2304], replicated
- out_proj_grad: float32 [768, 768], replicated
- ln2_gain_grad: float32 [768], replicated
- ln2_shift_grad: float32 [768], replicated
- router_grad: float32 [768, 16], replicated
- train_w1_grad: float32 [8, 768, 3072], P('sp', None, 'dp')
- train_w2_grad: float32 [8, 3072, 768], P('sp', 'dp')
The draws below stay inside these ranges and needn't reach their ends.
Inputs may be any that keep to these rules, and one draw needn't show every extreme that they name: `routes`: each token names two different experts. Among the 384 tokens of one device no expert is named more than 96 times, and on some device some expert is named exactly 96 times.
All inputs are finite; a program needn't handle non-finite values.
Results may differ from the reference program's by a relative error of at most 0.025.
Values may be sent and summed in bfloat16 or wider, within the bound.
A program may use at most 384 MiB of HBM per device.

```python
import math
import jax
import jax.numpy as jnp
import numpy as np
from jax import lax

D = 768
HEADS = 12
HEAD_DIM = 64
FF = 3072
SEQ_A = 1
SEQ_B = 1
CA = 128
CB = 256
T_DEV = 384
TRAINED = 8
EXPERTS = 16
CAP = 96
N_SP = 8
N_DP = 4


def steps_of(stream_key, dims, shards, least, largest):
    loudness, own = 1.0, jax.random.fold_in(stream_key, 6)
    for position, parts in shards:
        heights = jnp.exp(jax.random.uniform(jax.random.fold_in(own, position), (parts,), jnp.float32, least / len(shards), largest / len(shards)))
        loudness = loudness * jnp.repeat(heights, dims[position] // parts).reshape([-1 if axis == position else 1 for axis in range(len(dims))])
    return loudness


def deal_out(stream_key, own, number, rows, number_of, top, bound, lean):
    sequence = jax.random.permutation(stream_key, number_of)
    crowded, common = portions_of(number_of, rows * top, bound, lean, True), portions_of(number_of, rows * top, bound, lean, False)
    places = jnp.arange(number_of)

    def named(lengths, offset_by):
        used = int((lengths > 0).sum())
        fixed = max(1, used // 4)
        passed = fixed + (places - fixed + offset_by * (used - fixed)) % max(1, number_of - fixed)
        return jnp.zeros((number_of,), jnp.int32).at[sequence[jnp.where(places < fixed, places, passed)]].set(jnp.asarray(lengths, jnp.int32))

    lengths = jnp.where(number % 4 == 0, named(crowded, number // 4), named(common, number - number // 4 - 1))
    mixed = jax.random.permutation(jax.random.fold_in(own, 3), number_of)
    giver, receiver = mixed[0:number_of // 2 * 2:2], mixed[1:number_of // 2 * 2:2]
    slack = jnp.minimum(lengths[giver] - 1, bound - lengths[receiver]) // 2
    slack = jnp.where((giver == sequence[0]) | (receiver == sequence[0]) | (lengths[receiver] == 0), 0, jnp.maximum(slack, 0))
    passed = jax.random.randint(jax.random.fold_in(own, 4), (number_of // 2,), 0, 1 << 20) % (slack + 1)
    lengths = lengths.at[giver].add(-passed).at[receiver].add(passed)
    members = jnp.searchsorted(jnp.cumsum(lengths), jnp.arange(rows * top), side="right").astype(jnp.int32)
    table = members.reshape(top, rows).T
    table = table[jax.random.permutation(jax.random.fold_in(own, 1), rows)]
    offset_by = jax.random.randint(jax.random.fold_in(own, 2), (rows, 1), 0, top)
    return jnp.take_along_axis(table, (jnp.arange(top)[None, :] + offset_by) % top, axis=1)


def portions_of(number_of, total, limit, skew, full):
    loads = [(1 << 20) // math.isqrt(standing ** skew) + 1 for standing in range(1, number_of + 1)]
    largest = limit if full else min(limit, max(-(-total // number_of), total * loads[0] // sum(loads)))
    least = 1 if total - largest >= number_of - 1 else 0
    holding, surplus = [largest] + [least] * (number_of - 1), total - largest - least * (number_of - 1)
    while surplus > 0:
        free = [i for i in range(1, number_of) if holding[i] < largest] or [i for i in range(1, number_of) if holding[i] < limit]
        whole, remaining = sum([loads[i] for i in free]), surplus
        for i in free:
            addition = min(limit - holding[i], max(1, remaining * loads[i] // whole), surplus)
            holding[i] = holding[i] + addition
            surplus = surplus - addition
    return np.array(holding)


def gaussian(key, dims, deviation, limit, pieces=(), kind=jnp.bfloat16):
    drawn = deviation * jax.random.normal(key, dims, jnp.float32)
    if pieces:
        drawn = drawn * steps_of(key, dims, pieces, -0.22, 0.18)
    return jnp.clip(drawn, -limit, limit).astype(kind)


def setup_inputs(seed: int = 0) -> dict:
    keys = jax.random.split(jax.random.key(seed), 15)
    tokens = gaussian(keys[0], (N_DP, N_SP * T_DEV, D), 1.0, 6.0, ((0, 4), (1, 8)))
    ln1_gain = jnp.clip(1.0 + 0.1 * jax.random.normal(keys[1], (D,), jnp.float32), 0.5, 1.5)
    ln1_shift = gaussian(keys[2], (D,), 0.2, 1.2, (), jnp.float32)
    w_qkv = gaussian(keys[3], (D, 3 * D), D ** -0.5, 0.21875)
    w_out = gaussian(keys[4], (D, D), (D // 64) ** -0.5, 1.75)
    ln2_gain = jnp.clip(1.0 + 0.1 * jax.random.normal(keys[5], (D,), jnp.float32), 0.5, 1.5)
    ln2_shift = gaussian(keys[6], (D,), 0.2, 1.2, (), jnp.float32)
    w_router = gaussian(keys[7], (D, EXPERTS), D ** -0.5, 0.21875)
    train_w1 = gaussian(keys[8], (TRAINED, D, FF), D ** -0.5, 0.21875, ((0, 8), (2, 4)))
    train_w2 = gaussian(keys[9], (TRAINED, FF, D), FF ** -0.5, 0.109375, ((0, 8), (1, 4)))
    frozen_w1 = gaussian(keys[10], (EXPERTS - TRAINED, D, FF), D ** -0.5, 0.21875, ((0, 8), (2, 4)))
    frozen_w2 = gaussian(keys[11], (EXPERTS - TRAINED, FF, D), FF ** -0.5, 0.109375, ((0, 8), (1, 4)))
    routes_keys = jax.random.split(jax.random.fold_in(keys[12], 1), N_DP * (N_SP * T_DEV) // T_DEV)
    routes_turns = jax.random.permutation(jax.random.fold_in(keys[12], 3), N_DP * (N_SP * T_DEV) // T_DEV)
    routes = jax.vmap(lambda own, number: deal_out(jax.random.fold_in(keys[12], 2), own, number, T_DEV, EXPERTS, 2, CAP, 1))(routes_keys, routes_turns).reshape((N_DP, N_SP * T_DEV, 2))
    cotangent = gaussian(keys[13], (N_DP, N_SP * T_DEV, D), 1.0, 6.0, ((0, 4), (1, 8)))
    return {"tokens": tokens, "ln1_gain": ln1_gain, "ln1_shift": ln1_shift, "w_qkv": w_qkv, "w_out": w_out, "ln2_gain": ln2_gain, "ln2_shift": ln2_shift, "w_router": w_router, "train_w1": train_w1, "train_w2": train_w2, "frozen_w1": frozen_w1, "frozen_w2": frozen_w2, "routes": routes, "cotangent": cotangent}


@jax.custom_vjp
def low(v):
    return lax.optimization_barrier(v.astype(jnp.bfloat16)).astype(jnp.float32)

@jax.custom_vjp
def low_back(v):
    return v

def low_keep(v):
    return (low(v), None)

def low_pass(kept, grad):
    return (grad,)

def back_keep(v):
    return (v, None)

def back_low(kept, grad):
    return (low(grad),)
low.defvjp(low_keep, low_pass)
low_back.defvjp(back_keep, back_low)
EPSILON = 1e-05
NEGATIVE = -1e+30
HIGHEST_PRECISION = lax.Precision.HIGHEST

def layer_norm(inputs, gain_vec, shift_vec):
    centre = lax.optimization_barrier(jnp.mean(inputs, axis=-1, keepdims=True))
    centred = inputs - centre
    spread = lax.optimization_barrier(jnp.mean(centred * centred, axis=-1, keepdims=True))
    return centred * lax.rsqrt(spread + EPSILON) * gain_vec + shift_vec

def attend_sequence(packed):
    length = packed.shape[0]
    queries = packed[:, :D].reshape(length, HEADS, HEAD_DIM)
    key_rows = packed[:, D:2 * D].reshape(length, HEADS, HEAD_DIM)
    value_rows = packed[:, 2 * D:].reshape(length, HEADS, HEAD_DIM)
    block_rows = min(512, length)

    def one_block(start):
        block_queries = lax.dynamic_slice_in_dim(queries, start, block_rows, 0)
        scores = jnp.einsum('qhd,khd->hqk', block_queries, key_rows, precision=HIGHEST_PRECISION) * HEAD_DIM ** (-0.5)
        scores = low_back(scores)
        positions = start + jnp.arange(block_rows, dtype=jnp.int32)
        allowed = positions[:, None] >= jnp.arange(length, dtype=jnp.int32)[None, :]
        scores = jnp.where(allowed[None], scores, NEGATIVE)
        top_score = lax.optimization_barrier(jnp.max(scores, axis=-1, keepdims=True))
        exped = jnp.exp(scores - top_score)
        probability = exped / lax.optimization_barrier(jnp.sum(exped, axis=-1, keepdims=True))
        mixed = jnp.einsum('hqk,khd->qhd', low(probability), value_rows, precision=HIGHEST_PRECISION)
        return mixed.reshape(block_rows, D)
    starts = jnp.arange(length // block_rows, dtype=jnp.int32) * block_rows
    blocks = lax.map(jax.checkpoint(one_block), starts)
    return blocks.reshape(length, D)

def to_sequences(grid, offset, count, per_device):
    part = grid[:, :, offset:offset + count * per_device]
    part = part.reshape(N_DP, N_SP, count, per_device, part.shape[-1]).transpose(0, 2, 1, 3, 4)
    return part.reshape(N_DP * count, N_SP * per_device, part.shape[-1])

def from_sequences(sequences, count, per_device):
    part = sequences.reshape(N_DP, count, N_SP, per_device, sequences.shape[-1]).transpose(0, 2, 1, 3, 4)
    return part.reshape(N_DP, N_SP, count * per_device, sequences.shape[-1])

def route_positions(routes):
    expert_ids = routes.reshape(N_DP * N_SP, T_DEV * 2)
    matches = (expert_ids[..., None] == jnp.arange(EXPERTS, dtype=jnp.int32)).astype(jnp.int32)
    before = jnp.cumsum(matches, axis=1) - matches
    slot_index = lax.optimization_barrier(jnp.sum(before * matches, axis=-1))
    device_index = jnp.arange(N_DP * N_SP, dtype=jnp.int32)[:, None]
    positions = expert_ids * (N_DP * N_SP * CAP) + device_index * CAP + slot_index
    return positions.reshape(-1).astype(jnp.int32)

def run_expert(operands):
    rows_in, first_weight, second_weight = operands
    pre_act = low_back(jnp.dot(rows_in, first_weight, precision=HIGHEST_PRECISION))
    hidden = low(jax.nn.gelu(pre_act))
    return low_back(low(jnp.dot(hidden, second_weight, precision=HIGHEST_PRECISION)))

def reference(tokens, ln1_gain, ln1_shift, w_qkv, w_out, ln2_gain, ln2_shift, w_router, train_w1, train_w2, frozen_w1, frozen_w2, routes, cotangent):
    token_total = N_DP * N_SP * T_DEV
    slot_rows = N_DP * N_SP * CAP
    frozen_first = frozen_w1.astype(jnp.float32)
    frozen_second = frozen_w2.astype(jnp.float32)
    positions = route_positions(routes)
    expert_ids = routes.reshape(token_total, 2)
    anchor = jnp.arange(token_total * 2, dtype=jnp.int32) // 2
    source_rows = jnp.full((EXPERTS * slot_rows,), token_total, jnp.int32).at[positions].set(anchor)

    def forward(inputs, gain_one, shift_one, qkv_weight, out_weight, gain_two, shift_two, router_weight, first_train, second_train):
        first_norm = low(layer_norm(inputs, gain_one, shift_one))
        projected = low_back(low(jnp.dot(first_norm, qkv_weight, precision=HIGHEST_PRECISION)))
        grid = projected.reshape(N_DP, N_SP, T_DEV, 3 * D)
        short_out = lax.map(attend_sequence, to_sequences(grid, 0, SEQ_A, CA))
        long_out = lax.map(attend_sequence, to_sequences(grid, SEQ_A * CA, SEQ_B, CB))
        attended = jnp.concatenate([from_sequences(short_out, SEQ_A, CA), from_sequences(long_out, SEQ_B, CB)], axis=2)
        attended = low_back(low(attended.reshape(token_total, D)))
        middle = inputs + low_back(jnp.dot(attended, out_weight, precision=HIGHEST_PRECISION))
        second_norm = low(layer_norm(middle, gain_two, shift_two))
        logits = jnp.dot(second_norm, router_weight, precision=HIGHEST_PRECISION)
        chosen = jnp.take_along_axis(logits, expert_ids, axis=1)
        top_logit = lax.optimization_barrier(jnp.max(chosen, axis=-1, keepdims=True))
        exped = jnp.exp(chosen - top_logit)
        gates = exped / lax.optimization_barrier(jnp.sum(exped, axis=-1, keepdims=True))
        padded = jnp.concatenate([second_norm, jnp.zeros((1, D), jnp.float32)], axis=0)
        expert_in = low_back(padded[source_rows]).reshape(EXPERTS, slot_rows, D)
        first_all = jnp.concatenate([first_train, frozen_first], axis=0)
        second_all = jnp.concatenate([second_train, frozen_second], axis=0)
        expert_flat = lax.map(jax.checkpoint(run_expert), (expert_in, first_all, second_all)).reshape(EXPERTS * slot_rows, D)
        routed = expert_flat[positions].reshape(token_total, 2, D)
        return middle + lax.optimization_barrier(jnp.sum(gates[..., None] * routed, axis=1))
    primals = (tokens.reshape(token_total, D).astype(jnp.float32), ln1_gain, ln1_shift, w_qkv.astype(jnp.float32), w_out.astype(jnp.float32), ln2_gain, ln2_shift, w_router.astype(jnp.float32), train_w1.astype(jnp.float32), train_w2.astype(jnp.float32))
    result, pullback = jax.vjp(forward, *primals)
    grads = pullback(cotangent.reshape(token_total, D).astype(jnp.float32))
    block_out = result.reshape(N_DP, N_SP * T_DEV, D).astype(jnp.bfloat16)
    tokens_grad = grads[0].reshape(N_DP, N_SP * T_DEV, D)
    return (block_out, tokens_grad, grads[1], grads[2], grads[3], grads[4], grads[5], grads[6], grads[7], grads[8], grads[9])
```

```python
import functools

import jax
import jax.numpy as jnp
from jax import lax
from jax.experimental import pallas as pl
from jax.experimental.pallas import tpu as pltpu
from jax.sharding import PartitionSpec as P

HEADS = 12
HEAD_DIM = 64
LEN_A = 1024
LEN_B = 2048
PAIRS = HEADS // 2
WIDE = 2 * HEAD_DIM
UNIT = 3 * LEN_A
BLOCK = 256
EPSILON = 1e-05
NEGATIVE = -1e30
MESH = pl.DeviceIdType.MESH
DMA = pltpu.SemaphoreType.DMA
F32 = jnp.float32
BF16 = jnp.bfloat16
VMEM = pl.BlockSpec(memory_space=pltpu.VMEM)


def dot(a, b):
    return jnp.dot(a, b, preferred_element_type=F32)


def dot_t(a, b):
    return lax.dot_general(a, b, (((1,), (1,)), ((), ())), preferred_element_type=F32)


def t_dot(a, b):
    return lax.dot_general(a, b, (((0,), (0,)), ((), ())), preferred_element_type=F32)


def normed(value):
    centre = jnp.mean(value, axis=-1, keepdims=True)
    centred = value - centre
    spread = jnp.mean(centred * centred, axis=-1, keepdims=True)
    scale = lax.rsqrt(spread + EPSILON)
    return centred * scale, scale


def norm_back(grad, gain, hat, scale):
    scaled = grad * gain
    first = jnp.mean(scaled, axis=-1, keepdims=True)
    second = jnp.mean(scaled * hat, axis=-1, keepdims=True)
    return (scaled - first - hat * second) * scale


class Layout:
    def __init__(self, n_sp):
        self.n = n_sp
        self.sequences = n_sp // 8
        self.short = LEN_A // n_sp
        self.long = LEN_B // n_sp
        self.split = self.sequences * self.short

    def owners(self):
        found = []
        for seq in range(self.sequences):
            for pair in range(PAIRS):
                number = seq * PAIRS + pair
                found.append((number + number // 3 + 1, True, self.split + seq * self.long, self.long, pair, 0))
                found.append((4 * (seq * 2 + pair // 3), False, seq * self.short, self.short, pair, (pair % 3) * LEN_A))
        return found

    def role(self, me):
        is_short = lax.rem(me, 4) == 0
        number = me - me // 4 - 1
        group = me // 4
        seq = jnp.where(is_short, group // 2, number // PAIRS)
        pair = jnp.where(is_short, 3 * lax.rem(group, 2), lax.rem(number, PAIRS))
        return is_short, seq, pair

    def task(self, is_short, index):
        per = LEN_A // BLOCK
        start = jnp.where(is_short, (index // per) * LEN_A, 0)
        block = jnp.where(is_short, lax.rem(index, per), index)
        return pl.multiple_of(start, BLOCK), block

    def tasks(self, is_short):
        return jnp.where(is_short, 3 * LEN_A // BLOCK, LEN_B // BLOCK)


def greet(n):
    me = lax.axis_index("sp")
    barrier = pltpu.get_barrier_semaphore()
    for step in range(1, n):
        pl.semaphore_signal(barrier, inc=1, device_id={"sp": lax.rem(me + step, n)}, device_id_type=MESH)
    pl.semaphore_wait(barrier, n - 1)


def remote(source, target, send_sem, recv_sem, device):
    return pltpu.make_async_remote_copy(
        src_ref=source, dst_ref=target, send_sem=send_sem, recv_sem=recv_sem, device_id={"sp": device}, device_id_type=MESH
    )


def lanes_first():
    return lax.broadcasted_iota(jnp.int32, (1, WIDE), 1) < HEAD_DIM


def halves(value):
    keep = lanes_first()
    zero = jnp.zeros_like(value)
    return jnp.where(keep, value, zero), jnp.where(keep, zero, value)


def causal(rows):
    return lax.broadcasted_iota(jnp.int32, (rows, rows), 0) >= lax.broadcasted_iota(jnp.int32, (rows, rows), 1)


def to_owners(lay, me, cols, slot, source, target, send_sems, recv_sem, local_sem, wanted):
    started = []
    for number, (owner, is_long, start, rows, pair, unit) in enumerate(lay.owners()):
        if pair not in wanted:
            continue
        piece = source.at[pl.ds(start, rows), pl.ds(cols(pair), WIDE)]
        place = target(unit + me * rows, rows)
        far = remote(piece, place, send_sems.at[slot(number)], recv_sem, owner)
        near = pltpu.make_async_copy(piece, place, local_sem)

        @pl.when(me != owner)
        def _():
            far.start()

        @pl.when(me == owner)
        def _():
            near.start()
            near.wait()

        started.append((owner, far))
    return started


def finish_sends(me, started):
    for owner, copy in started:

        @pl.when(me != owner)
        def _():
            copy.wait_send()


def wait_unit(lay, is_short, buffer, sem):
    for short, rows in ((True, 3 * (lay.n - 1) * lay.short), (False, (lay.n - 1) * lay.long)):

        @pl.when(is_short == short)
        def _():
            piece = buffer.at[pl.ds(0, rows)]
            pltpu.make_async_copy(piece, piece, sem).wait()


def send_home(lay, me, is_short, seq, first_pair, base, block, unit_start, source, target, base_col, send_sem, recv_sem, local_sem):
    for short, rows in ((True, lay.short), (False, lay.long)):

        @pl.when(is_short == short)
        def _():
            pair = first_pair + (unit_start // LEN_A if short else 0)
            column = pl.multiple_of(base_col + pair * WIDE, WIDE)
            first = pl.multiple_of(seq * rows + (0 if short else lay.split), 16)
            for part in range(BLOCK // rows):
                home = block * (BLOCK // rows) + part
                piece = source.at[pl.ds(pl.multiple_of(base + part * rows, 16), rows)]
                place = target.at[pl.ds(first, rows), pl.ds(column, WIDE)]

                @pl.when(home != me)
                def _():
                    remote(piece, place, send_sem, recv_sem, home).start()

                @pl.when(home == me)
                def _():
                    near = pltpu.make_async_copy(piece, place, local_sem)
                    near.start()
                    near.wait()


def wait_home(lay, is_short, scratch, sem, tensors, sent):
    for short in (True, False):
        own = 3 * lay.short if short else lay.long
        if sent:
            rows = (3 * LEN_A if short else LEN_B) - own
        else:
            rows = PAIRS * lay.sequences * (lay.short + lay.long) - own

        @pl.when(is_short == short)
        def _():
            for _ in range(tensors):
                piece = scratch.at[pl.ds(0, rows)]
                pltpu.make_async_copy(piece, piece, sem).wait()


def attend_kernel(
    lay, tokens, gain, shift, w_qkv, first_norm, unit, attended, log_total, home, staged, staged_out, send, recv, out_send, home_recv, local
):
    me = lax.axis_index("sp")
    is_short, seq, first_pair = lay.role(me)
    greet(lay.n)
    hat, _ = normed(tokens[...].astype(F32))
    first_norm[...] = (hat * gain[...] + shift[...]).astype(BF16)
    started = []
    for chunk in range(9):
        kind, third = divmod(chunk, 3)
        made = dot(first_norm[...], w_qkv[:, chunk * 2 * WIDE : (chunk + 1) * 2 * WIDE]).astype(BF16)
        staged[chunk] = made * BF16(HEAD_DIM**-0.5) if kind == 0 else made
        count = len(lay.owners())
        started += to_owners(
            lay,
            me,
            lambda pair: (pair % 2) * WIDE,
            lambda number: chunk * count + number,
            staged.at[chunk],
            lambda start, rows: unit.at[kind, pl.ds(pl.multiple_of(start, 16), rows)],
            send,
            recv.at[kind],
            local,
            (2 * third, 2 * third + 1),
        )
    for kind in range(3):
        wait_unit(lay, is_short, unit.at[kind], recv.at[kind])
    keep = lanes_first()
    lower = causal(BLOCK)

    def task(index, carry):
        start, block = lay.task(is_short, index)
        base = pl.multiple_of(start + block * BLOCK, BLOCK)
        queries = halves(unit[0, pl.ds(base, BLOCK)])

        def visit(place, state, diagonal):
            keys = unit[1, pl.ds(place, BLOCK)]
            values = unit[2, pl.ds(place, BLOCK)]
            result = []
            for (peak, total, summed), query in zip(state, queries):
                scores = dot_t(query, keys)
                if diagonal:
                    scores = jnp.where(lower, scores, NEGATIVE)
                new_peak = jnp.maximum(peak, jnp.max(scores, axis=1, keepdims=True))
                factor = jnp.exp(peak - new_peak)
                weight = jnp.exp(scores - new_peak)
                total = total * factor + jnp.sum(weight, axis=1, keepdims=True)
                summed = summed * factor + dot(weight.astype(BF16), values)
                result.append((new_peak, total, summed))
            return tuple(result)

        empty = (jnp.full((BLOCK, 1), NEGATIVE, F32), jnp.zeros((BLOCK, 1), F32), jnp.zeros((BLOCK, WIDE), F32))
        state = lax.fori_loop(
            0, block, lambda j, state: visit(pl.multiple_of(start + j * BLOCK, BLOCK), state, False), (empty, empty)
        )
        (peak_a, total_a, summed_a), (peak_b, total_b, summed_b) = visit(base, state, True)
        result = jnp.where(keep, summed_a / total_a, summed_b / total_b)
        attended[pl.ds(base, BLOCK)] = result
        staged_out[pl.ds(base, BLOCK)] = result.astype(BF16)
        log_total[pl.ds(base, BLOCK)] = jnp.where(keep, peak_a + jnp.log(total_a), peak_b + jnp.log(total_b))
        send_home(
            lay, me, is_short, seq, first_pair, base, block, start, staged_out, home, 0, out_send, home_recv, local
        )
        return carry

    lax.fori_loop(0, lay.tasks(is_short), task, 0)
    finish_sends(me, started)
    wait_home(lay, is_short, staged_out, out_send, 1, True)
    wait_home(lay, is_short, staged_out, home_recv, 1, False)


def attend(lay, tokens, gain, shift, w_qkv):
    count, width = tokens.shape
    owners = len(lay.owners())
    return pl.pallas_call(
        functools.partial(attend_kernel, lay),
        out_shape=(
            jax.ShapeDtypeStruct((count, width), BF16),
            jax.ShapeDtypeStruct((3, UNIT, WIDE), BF16),
            jax.ShapeDtypeStruct((UNIT, WIDE), F32),
            jax.ShapeDtypeStruct((UNIT, WIDE), F32),
            jax.ShapeDtypeStruct((count, width), BF16),
        ),
        in_specs=[VMEM] * 4,
        out_specs=[VMEM] * 5,
        scratch_shapes=[
            pltpu.VMEM((9, count, 2 * WIDE), BF16),
            pltpu.VMEM((UNIT, WIDE), BF16),
            DMA((9 * owners,)),
            DMA((3,)),
            DMA,
            DMA,
            DMA,
        ],
        compiler_params=pltpu.CompilerParams(collective_id=0, has_side_effects=True, vmem_limit_bytes=48 * 2**20),
        cost_estimate=pl.CostEstimate(flops=6 * 10**9, bytes_accessed=20 * 2**20, transcendentals=5 * 10**6),
        name="attend",
    )(tokens, gain, shift, w_qkv)


def one_hot_rows(lay, capacity, routes_t):
    n = lay.n
    experts, count = 2 * n, routes_t.shape[1]
    index = lax.broadcasted_iota(jnp.int32, (experts, count), 0)
    matches = [(index == routes_t[c : c + 1]).astype(F32) for c in range(2)]
    earlier = (
        lax.broadcasted_iota(jnp.int32, (count, count), 0) < lax.broadcasted_iota(jnp.int32, (count, count), 1)
    ).astype(F32)
    rank = dot((matches[0] + matches[1]).astype(BF16), earlier.astype(BF16))
    place = rank + (((index % n) * 2 + index // n) * capacity).astype(F32)
    slots = lax.broadcasted_iota(jnp.int32, (experts * capacity, count), 0)
    return [(slots == jnp.sum(m * place, axis=0, keepdims=True).astype(jnp.int32)).astype(F32).astype(BF16) for m in matches]


def one_hot_columns(lay, capacity, routes):
    n = lay.n
    experts, count = 2 * n, routes.shape[0]
    index = lax.broadcasted_iota(jnp.int32, (count, 128), 1)
    matches = [(index == routes[:, c : c + 1]).astype(F32) for c in range(2)]
    earlier = (
        lax.broadcasted_iota(jnp.int32, (count, count), 0) > lax.broadcasted_iota(jnp.int32, (count, count), 1)
    ).astype(F32)
    rank = dot(earlier.astype(BF16), (matches[0] + matches[1]).astype(BF16))
    place = rank + (((index % n) * 2 + index // n) * capacity).astype(F32)
    slots = lax.broadcasted_iota(jnp.int32, (count, experts * capacity), 1)
    hot = [(slots == jnp.sum(m * place, axis=1, keepdims=True).astype(jnp.int32)).astype(F32).astype(BF16) for m in matches]
    return hot, matches


def dispatch_kernel(
    lay, capacity, tokens, attended, w_out, gain, shift, w_router, routes, routes_t, cotangent,
    middle_out, second_out, gates_out, rows_in, rows_grad, packed, packed_grad, send, recv, local,
):
    n = lay.n
    me = lax.axis_index("sp")
    greet(n)
    middle = tokens[...].astype(F32) + dot(attended[...], w_out[...])
    middle_out[...] = middle
    hat, _ = normed(middle)
    second = (hat * gain[...] + shift[...]).astype(BF16)
    second_out[...] = second
    hot = one_hot_rows(lay, capacity, routes_t[...])
    started = []

    def spread(source, target, which):
        for kind in range(2):
            near = pltpu.make_async_copy(
                source.at[pl.ds(pl.multiple_of((me * 2 + kind) * capacity, 16), capacity)],
                target.at[kind, pl.ds(pl.multiple_of(me * capacity, 16), capacity)],
                local.at[which, kind],
            )
            near.start()
            for step in range(1, n):
                to = lax.rem(me + step, n)
                copy = remote(
                    source.at[pl.ds(pl.multiple_of((to * 2 + kind) * capacity, 16), capacity)],
                    target.at[kind, pl.ds(pl.multiple_of(me * capacity, 16), capacity)],
                    send.at[which, kind, step],
                    recv.at[which, kind, step],
                    to,
                )
                copy.start()
                started.append(copy)
            started.append(near)

    packed[...] = dot(hot[0] + hot[1], second).astype(BF16)
    spread(packed, rows_in, 0)
    logits = dot(second, w_router[...])
    index = lax.broadcasted_iota(jnp.int32, logits.shape, 1)
    chosen = [jnp.sum(jnp.where(index == routes[:, c : c + 1], logits, 0.0), axis=1, keepdims=True) for c in range(2)]
    top = jnp.maximum(chosen[0], chosen[1])
    exped = [jnp.exp(value - top) for value in chosen]
    gates = [value / (exped[0] + exped[1]) for value in exped]
    upstream = cotangent[...].astype(F32)
    lane = lax.broadcasted_iota(jnp.int32, gates_out.shape, 1)
    gates_out[...] = jnp.where(lane == 0, gates[0], gates[1])
    packed_grad[...] = (
        dot(hot[0], (gates[0] * upstream).astype(BF16)) + dot(hot[1], (gates[1] * upstream).astype(BF16))
    ).astype(BF16)
    spread(packed_grad, rows_grad, 1)
    for copy in started:
        copy.wait()


def dispatch(lay, capacity, tokens, attended, w_out, gain, shift, w_router, routes, cotangent):
    count, width = tokens.shape
    n = lay.n
    slots = 2 * n * capacity
    return pl.pallas_call(
        functools.partial(dispatch_kernel, lay, capacity),
        out_shape=(
            jax.ShapeDtypeStruct((count, width), F32),
            jax.ShapeDtypeStruct((count, width), BF16),
            jax.ShapeDtypeStruct((count, 128), F32),
            jax.ShapeDtypeStruct((2, n * capacity, width), BF16),
            jax.ShapeDtypeStruct((2, n * capacity, width), BF16),
        ),
        in_specs=[VMEM] * 9,
        out_specs=[VMEM] * 5,
        scratch_shapes=[
            pltpu.VMEM((slots, width), BF16),
            pltpu.VMEM((slots, width), BF16),
            DMA((2, 2, n)),
            DMA((2, 2, n)),
            DMA((2, 2)),
        ],
        compiler_params=pltpu.CompilerParams(collective_id=1, has_side_effects=True, vmem_limit_bytes=48 * 2**20),
        cost_estimate=pl.CostEstimate(flops=4 * 10**9, bytes_accessed=20 * 2**20, transcendentals=10**4),
        name="dispatch",
    )(tokens, attended, w_out, gain, shift, w_router, routes, routes.T, cotangent)


ROWS = 256


def gelu_parts(value):
    root = 0.7978845608028654
    square = value * value
    bent = jnp.tanh(root * value * (1.0 + 0.044715 * square))
    half = 0.5 + 0.5 * bent
    slope = half + 0.5 * value * (1.0 - bent * bent) * (root + 3.0 * 0.044715 * root * square)
    return value * half, slope


def expert_kernel(trained, rows_ref, grads_ref, first, second, out, grad_in, *rest):
    if trained:
        first_grad, second_grad, out_sum, in_sum, hidden, pre_grad = rest
    else:
        out_sum, in_sum, hidden, pre_grad = rest
    step = pl.program_id(0)
    total = rows_ref.shape[0]
    for start in range(0, total, ROWS):
        part = pl.ds(start, ROWS)
        pre = dot(rows_ref[part], first[0])
        active, slope = gelu_parts(pre)
        active = active.astype(BF16)
        hidden[part] = active
        back = (dot_t(grads_ref[part], second[0]) * slope).astype(BF16)
        pre_grad[part] = back
        produced = dot(active, second[0])
        returned = dot_t(back, first[0])

        @pl.when(step == 0)
        def _():
            out_sum[part] = produced
            in_sum[part] = returned

        @pl.when(step > 0)
        def _():
            out_sum[part] += produced
            in_sum[part] += returned

    if trained:
        first_grad[0] = t_dot(rows_ref[...], pre_grad[...]).astype(BF16)
        second_grad[0] = t_dot(hidden[...], grads_ref[...]).astype(BF16)

    @pl.when(step == pl.num_programs(0) - 1)
    def _():
        out[...] = out_sum[...].astype(BF16)
        grad_in[...] = in_sum[...].astype(BF16)


def expert(trained, rows, grads, first, second):
    slices, width, hidden = first.shape
    total = rows.shape[0]
    whole = pl.BlockSpec((total, width), lambda k: (0, 0))
    first_spec = pl.BlockSpec((1, width, hidden), lambda k: (k, 0, 0))
    second_spec = pl.BlockSpec((1, hidden, width), lambda k: (k, 0, 0))
    out_shape = [jax.ShapeDtypeStruct((total, width), BF16)] * 2
    out_specs = [whole, whole]
    if trained:
        out_shape += [jax.ShapeDtypeStruct(first.shape, BF16), jax.ShapeDtypeStruct(second.shape, BF16)]
        out_specs += [first_spec, second_spec]
    return pl.pallas_call(
        functools.partial(expert_kernel, trained),
        grid=(slices,),
        out_shape=out_shape,
        in_specs=[whole, whole, first_spec, second_spec],
        out_specs=out_specs,
        scratch_shapes=[
            pltpu.VMEM((total, width), F32),
            pltpu.VMEM((total, width), F32),
            pltpu.VMEM((total, hidden), BF16),
            pltpu.VMEM((total, hidden), BF16),
        ],
        compiler_params=pltpu.CompilerParams(vmem_limit_bytes=48 * 2**20),
        cost_estimate=pl.CostEstimate(
            flops=slices * total * width * hidden * (12 if trained else 8), bytes_accessed=20 * 2**20, transcendentals=10**6
        ),
        name="trained_expert" if trained else "frozen_expert",
    )(rows, grads, first, second)


def combine_kernel(
    lay, capacity, out_train, out_frozen, grad_train, grad_frozen, middle, second, gates, attended, w_out, gain, w_router, routes, cotangent,
    block_out, middle_grad, attended_grad, out_proj, router, gain_grad, shift_grad,
    got, got_grad, send, recv, local,
):
    n = lay.n
    me = lax.axis_index("sp")
    greet(n)
    started = [[], []]
    for which, (sources, target) in enumerate((((out_train, out_frozen), got), ((grad_train, grad_frozen), got_grad))):
        for kind, source in enumerate(sources):
            place = target.at[pl.ds(pl.multiple_of((me * 2 + kind) * capacity, 16), capacity)]
            near = pltpu.make_async_copy(
                source.at[pl.ds(pl.multiple_of(me * capacity, 16), capacity)], place, local.at[which, kind]
            )
            near.start()
            for step in range(1, n):
                to = lax.rem(me + step, n)
                copy = remote(
                    source.at[pl.ds(pl.multiple_of(to * capacity, 16), capacity)],
                    place,
                    send.at[which, kind, step],
                    recv.at[which, kind, step],
                    to,
                )
                copy.start()
                started[which].append(copy)
            started[which].append(near)
    hot, matches = one_hot_columns(lay, capacity, routes[...])
    upstream = cotangent[...].astype(F32)
    gate = [gates[:, c : c + 1] for c in range(2)]
    for copy in started[0]:
        copy.wait()
    total = middle[...]
    grad_gate = []
    for c in range(2):
        produced = dot(hot[c], got[...])
        total = total + gate[c] * produced
        grad_gate.append(jnp.sum(upstream * produced, axis=1, keepdims=True))
    block_out[...] = total.astype(BF16)
    mean_grad = gate[0] * grad_gate[0] + gate[1] * grad_gate[1]
    grad_logits = sum(matches[c] * (gate[c] * (grad_gate[c] - mean_grad)) for c in range(2))
    high = grad_logits.astype(BF16)
    low = (grad_logits - high.astype(F32)).astype(BF16)
    router[...] = t_dot(second[...], high) + t_dot(second[...], low)
    grad_second = dot_t(high, w_router[...]) + dot_t(low, w_router[...])
    for copy in started[1]:
        copy.wait()
    grad_second = grad_second + dot(hot[0] + hot[1], got_grad[...])
    hat, scale = normed(middle[...])
    gain_grad[...] = jnp.sum(grad_second * hat, axis=0, keepdims=True)
    shift_grad[...] = jnp.sum(grad_second, axis=0, keepdims=True)
    grad = upstream + norm_back(grad_second, gain[...], hat, scale)
    middle_grad[...] = grad
    branch = grad.astype(BF16)
    attended_grad[...] = dot_t(branch, w_out[...]).astype(BF16)
    out_proj[...] = t_dot(attended[...], branch)


def combine(lay, capacity, outs, grads, middle, second, gates, attended, w_out, gain, w_router, routes, cotangent):
    count, width = middle.shape
    n = lay.n
    slots = 2 * n * capacity
    return pl.pallas_call(
        functools.partial(combine_kernel, lay, capacity),
        out_shape=(
            jax.ShapeDtypeStruct((count, width), BF16),
            jax.ShapeDtypeStruct((count, width), F32),
            jax.ShapeDtypeStruct((count, width), BF16),
            jax.ShapeDtypeStruct((width, width), F32),
            jax.ShapeDtypeStruct((width, 128), F32),
            jax.ShapeDtypeStruct((1, width), F32),
            jax.ShapeDtypeStruct((1, width), F32),
        ),
        in_specs=[VMEM] * 13,
        out_specs=[VMEM] * 7,
        scratch_shapes=[
            pltpu.VMEM((slots, width), BF16),
            pltpu.VMEM((slots, width), BF16),
            DMA((2, 2, n)),
            DMA((2, 2, n)),
            DMA((2, 2)),
        ],
        compiler_params=pltpu.CompilerParams(collective_id=2, has_side_effects=True, vmem_limit_bytes=48 * 2**20),
        cost_estimate=pl.CostEstimate(flops=6 * 10**9, bytes_accessed=30 * 2**20, transcendentals=10**4),
        name="combine",
    )(*outs, *grads, middle, second, gates, attended, w_out, gain, w_router, routes, cotangent)


def attend_back_kernel(
    lay, unit, attended, log_total, grad_attended, first_norm, tokens, gain, w_qkv, middle_grad,
    tokens_grad, qkv_grad, gain_grad, shift_grad,
    grad_out, deltas, query_sum, staged, home, send, recv, out_send, home_recv, local,
):
    me = lax.axis_index("sp")
    is_short, seq, first_pair = lay.role(me)
    greet(lay.n)
    started = to_owners(
        lay,
        me,
        lambda pair: pair * WIDE,
        lambda number: number,
        grad_attended,
        lambda start, rows: grad_out.at[pl.ds(pl.multiple_of(start, 16), rows)],
        send,
        recv,
        local,
        range(PAIRS),
    )
    query_sum[...] = jnp.zeros_like(query_sum)
    keep = lanes_first()
    lower = causal(BLOCK)
    wait_unit(lay, is_short, grad_out, recv)

    def make_delta(index, carry):
        part = pl.ds(pl.multiple_of(index * BLOCK, BLOCK), BLOCK)
        first, second = halves(grad_out[part].astype(F32) * attended[part])
        deltas[part] = jnp.where(
            keep, jnp.sum(first, axis=1, keepdims=True), jnp.sum(second, axis=1, keepdims=True)
        )
        return carry

    lax.fori_loop(0, lay.tasks(is_short), make_delta, 0)
    per = jnp.where(is_short, LEN_A // BLOCK, LEN_B // BLOCK)

    def task(index, carry):
        start, block = lay.task(is_short, index)
        base = pl.multiple_of(start + block * BLOCK, BLOCK)
        keys = unit[1, pl.ds(base, BLOCK)]
        values = unit[2, pl.ds(base, BLOCK)]
        key_both = jnp.concatenate(halves(keys), axis=0)

        def visit(place, state, diagonal):
            part = pl.ds(place, BLOCK)
            grad_key, grad_value = state
            queries = halves(unit[0, part])
            outs = halves(grad_out[part])
            weights, grads = [], []
            for which, (query, out) in enumerate(zip(queries, outs)):
                column = which * HEAD_DIM
                scores = dot_t(query, keys)
                if diagonal:
                    scores = jnp.where(lower, scores, NEGATIVE)
                weight = jnp.exp(scores - log_total[part, column : column + 1])
                grad = weight * (dot_t(out, values) - deltas[part, column : column + 1])
                weights.append(weight.astype(BF16))
                grads.append(grad.astype(BF16))
            grad_value = grad_value + t_dot(jnp.concatenate(weights, axis=0), jnp.concatenate(outs, axis=0))
            grad_key = grad_key + t_dot(jnp.concatenate(grads, axis=0), jnp.concatenate(queries, axis=0))
            query_sum[part] += dot(jnp.concatenate(grads, axis=1), key_both)
            return grad_key, grad_value

        zero = jnp.zeros((BLOCK, WIDE), F32)
        state = visit(base, (zero, zero), True)
        grad_key, grad_value = lax.fori_loop(
            block + 1, per, lambda i, state: visit(pl.multiple_of(start + i * BLOCK, BLOCK), state, False), state
        )
        part = pl.ds(base, BLOCK)
        staged[0, part] = (query_sum[part] * HEAD_DIM**-0.5).astype(BF16)
        staged[1, part] = grad_key.astype(BF16)
        staged[2, part] = grad_value.astype(BF16)
        for kind in range(3):
            send_home(
                lay, me, is_short, seq, first_pair, base, block, start, staged.at[kind], home, kind * PAIRS * WIDE,
                out_send.at[kind], home_recv.at[kind], local,
            )
        return carry

    lax.fori_loop(0, lay.tasks(is_short), task, 0)
    for kind in range(3):
        wait_home(lay, is_short, staged.at[kind], home_recv.at[kind], 1, False)
    grad_first = dot_t(home[...], w_qkv[...])
    hat, scale = normed(tokens[...].astype(F32))
    gain_grad[...] = jnp.sum(grad_first * hat, axis=0, keepdims=True)
    shift_grad[...] = jnp.sum(grad_first, axis=0, keepdims=True)
    tokens_grad[...] = middle_grad[...] + norm_back(grad_first, gain[...], hat, scale)
    for chunk in range(0, 3 * PAIRS * WIDE, 2 * WIDE):
        qkv_grad[:, chunk : chunk + 2 * WIDE] = t_dot(first_norm[...], home[:, chunk : chunk + 2 * WIDE])
    finish_sends(me, started)
    for kind in range(3):
        wait_home(lay, is_short, staged.at[kind], out_send.at[kind], 1, True)


def attend_back(lay, unit, attended, log_total, grad_attended, first_norm, tokens, gain, w_qkv, middle_grad):
    count, width = tokens.shape
    owners = len(lay.owners())
    return pl.pallas_call(
        functools.partial(attend_back_kernel, lay),
        out_shape=(
            jax.ShapeDtypeStruct((count, width), F32),
            jax.ShapeDtypeStruct((width, 3 * width), F32),
            jax.ShapeDtypeStruct((1, width), F32),
            jax.ShapeDtypeStruct((1, width), F32),
        ),
        in_specs=[VMEM] * 9,
        out_specs=[VMEM] * 4,
        scratch_shapes=[
            pltpu.VMEM((UNIT, WIDE), BF16),
            pltpu.VMEM((UNIT, WIDE), F32),
            pltpu.VMEM((UNIT, WIDE), F32),
            pltpu.VMEM((3, UNIT, WIDE), BF16),
            pltpu.VMEM((count, 3 * width), BF16),
            DMA((owners,)),
            DMA,
            DMA((3,)),
            DMA((3,)),
            DMA,
        ],
        compiler_params=pltpu.CompilerParams(collective_id=3, has_side_effects=True, vmem_limit_bytes=48 * 2**20),
        cost_estimate=pl.CostEstimate(flops=10 * 10**9, bytes_accessed=30 * 2**20, transcendentals=5 * 10**6),
        name="attend_back",
    )(unit, attended, log_total, grad_attended, first_norm, tokens, gain, w_qkv, middle_grad)


def shards(
    tokens, ln1_gain, ln1_shift, w_qkv, w_out, ln2_gain, ln2_shift, w_router,
    train_w1, train_w2, frozen_w1, frozen_w2, routes, cotangent,
):
    n = lax.axis_size("sp")
    lay = Layout(n)
    tokens, routes, cotangent = tokens[0], routes[0], cotangent[0]
    count = tokens.shape[0]
    capacity = 2 * count // n
    experts = w_router.shape[1]
    row = lambda vector: vector.reshape(1, -1)
    router_wide = jnp.pad(w_router, ((0, 0), (0, 128 - experts)))
    whole = [lax.all_gather(weight[0], "dp") for weight in (train_w1, train_w2, frozen_w1, frozen_w2)]
    first_norm, unit, attended, log_total, attended_low = attend(lay, tokens, row(ln1_gain), row(ln1_shift), w_qkv)
    middle, second, gates, rows, grads = dispatch(
        lay, capacity, tokens, attended_low, w_out, row(ln2_gain), row(ln2_shift), router_wide, routes, cotangent
    )
    out_train, in_train, first_grad, second_grad = expert(True, rows[0], grads[0], whole[0], whole[1])
    out_frozen, in_frozen = expert(False, rows[1], grads[1], whole[2], whole[3])
    first_grad = lax.psum_scatter(first_grad, "dp", scatter_dimension=0).astype(F32)
    second_grad = lax.psum_scatter(second_grad, "dp", scatter_dimension=0).astype(F32)
    block_out, middle_grad, attended_grad, out_proj, router, gain_two, shift_two = combine(
        lay, capacity, (out_train, out_frozen), (in_train, in_frozen), middle, second, gates, attended_low, w_out,
        row(ln2_gain), router_wide, routes, cotangent,
    )
    tokens_grad, qkv_grad, gain_one, shift_one = attend_back(
        lay, unit, attended, log_total, attended_grad, first_norm, tokens, row(ln1_gain), w_qkv, middle_grad
    )
    small = lax.psum((out_proj, router[:, :experts], gain_two, shift_two), ("sp", "dp"))
    last = lax.psum((qkv_grad, gain_one, shift_one), ("sp", "dp"))
    return (
        block_out[None],
        tokens_grad[None],
        last[1][0],
        last[2][0],
        last[0],
        small[0],
        small[2][0],
        small[3][0],
        small[1],
        first_grad[None],
        second_grad[None],
    )


def solution(mesh):
    in_specs = (
        P("dp", "sp", None), P(), P(), P(), P(), P(), P(), P(),
        P("sp", None, "dp"), P("sp", "dp", None), P("sp", None, "dp"), P("sp", "dp", None),
        P("dp", "sp", None), P("dp", "sp", None),
    )
    out_specs = (
        P("dp", "sp", None), P("dp", "sp", None), P(), P(), P(), P(), P(), P(), P(),
        P("sp", None, "dp"), P("sp", "dp", None),
    )
    return jax.shard_map(shards, mesh=mesh, in_specs=in_specs, out_specs=out_specs, check_vma=False)
```

```python
import functools

import jax
import jax.numpy as jnp
from jax import lax
from jax.experimental import pallas as pl
from jax.experimental.pallas import tpu as pltpu
from jax.sharding import PartitionSpec as P

HEADS = 12
HEAD_DIM = 64
LEN_A = 1024
LEN_B = 2048
PAIRS = HEADS // 2
WIDE = 2 * HEAD_DIM
UNIT = 3 * LEN_A
BLOCK = 256
EPSILON = 1e-05
NEGATIVE = -1e30
MESH = pl.DeviceIdType.MESH
DMA = pltpu.SemaphoreType.DMA
F32 = jnp.float32
BF16 = jnp.bfloat16
VMEM = pl.BlockSpec(memory_space=pltpu.VMEM)


def dot(a, b):
    return jnp.dot(a, b, preferred_element_type=F32)


def dot_t(a, b):
    return lax.dot_general(a, b, (((1,), (1,)), ((), ())), preferred_element_type=F32)


def t_dot(a, b):
    return lax.dot_general(a, b, (((0,), (0,)), ((), ())), preferred_element_type=F32)


def normed(value):
    centre = jnp.mean(value, axis=-1, keepdims=True)
    centred = value - centre
    spread = jnp.mean(centred * centred, axis=-1, keepdims=True)
    scale = lax.rsqrt(spread + EPSILON)
    return centred * scale, scale


def norm_back(grad, gain, hat, scale):
    scaled = grad * gain
    first = jnp.mean(scaled, axis=-1, keepdims=True)
    second = jnp.mean(scaled * hat, axis=-1, keepdims=True)
    return (scaled - first - hat * second) * scale


class Layout:
    def __init__(self, n_sp):
        self.n = n_sp
        self.sequences = n_sp // 8
        self.short = LEN_A // n_sp
        self.long = LEN_B // n_sp
        self.split = self.sequences * self.short

    def owners(self):
        found = []
        for seq in range(self.sequences):
            for pair in range(PAIRS):
                number = seq * PAIRS + pair
                found.append((number + number // 3 + 1, True, self.split + seq * self.long, self.long, pair, 0))
                found.append((4 * (seq * 2 + pair // 3), False, seq * self.short, self.short, pair, (pair % 3) * LEN_A))
        return found

    def role(self, me):
        is_short = lax.rem(me, 4) == 0
        number = me - me // 4 - 1
        group = me // 4
        seq = jnp.where(is_short, group // 2, number // PAIRS)
        pair = jnp.where(is_short, 3 * lax.rem(group, 2), lax.rem(number, PAIRS))
        return is_short, seq, pair

    def task(self, is_short, index):
        per = LEN_A // BLOCK
        start = jnp.where(is_short, (index // per) * LEN_A, 0)
        block = jnp.where(is_short, lax.rem(index, per), index)
        return pl.multiple_of(start, BLOCK), block

    def tasks(self, is_short):
        return jnp.where(is_short, 3 * LEN_A // BLOCK, LEN_B // BLOCK)


def meet(peers):
    barrier = pltpu.get_barrier_semaphore()
    for wanted, device in peers:

        @pl.when(wanted)
        def _():
            pl.semaphore_signal(barrier, inc=1, device_id=device, device_id_type=MESH)

    pl.semaphore_wait(barrier, sum(jnp.asarray(wanted, jnp.int32) for wanted, _ in peers))


def plane_peers(n):
    me = lax.axis_index("sp")
    return [(True, {"sp": lax.rem(me + step, n)}) for step in range(1, n)]


def remote(source, target, send_sem, recv_sem, device):
    device = device if isinstance(device, dict) else {"sp": device}
    return pltpu.make_async_remote_copy(
        src_ref=source, dst_ref=target, send_sem=send_sem, recv_sem=recv_sem, device_id=device, device_id_type=MESH
    )


def lanes_first():
    return lax.broadcasted_iota(jnp.int32, (1, WIDE), 1) < HEAD_DIM


def halves(value):
    keep = lanes_first()
    zero = jnp.zeros_like(value)
    return jnp.where(keep, value, zero), jnp.where(keep, zero, value)


def causal(rows):
    return lax.broadcasted_iota(jnp.int32, (rows, rows), 0) >= lax.broadcasted_iota(jnp.int32, (rows, rows), 1)


def to_owners(lay, me, cols, slot, source, target, send_sems, recv_sem, local_sem, wanted):
    started = []
    for number, (owner, is_long, start, rows, pair, unit) in enumerate(lay.owners()):
        if pair not in wanted:
            continue
        piece = source.at[pl.ds(start, rows), pl.ds(cols(pair), WIDE)]
        place = target(unit + me * rows, rows)
        far = remote(piece, place, send_sems.at[slot(number)], recv_sem, owner)
        near = pltpu.make_async_copy(piece, place, local_sem)

        @pl.when(me != owner)
        def _():
            far.start()

        @pl.when(me == owner)
        def _():
            near.start()
            near.wait()

        started.append((owner, far))
    return started


def finish_sends(me, started):
    for owner, copy in started:

        @pl.when(me != owner)
        def _():
            copy.wait_send()


def wait_unit(lay, is_short, buffer, sem):
    for short, rows in ((True, 3 * (lay.n - 1) * lay.short), (False, (lay.n - 1) * lay.long)):

        @pl.when(is_short == short)
        def _():
            piece = buffer.at[pl.ds(0, rows)]
            pltpu.make_async_copy(piece, piece, sem).wait()


def send_home(lay, me, is_short, seq, first_pair, base, block, unit_start, source, target, base_col, send_sem, recv_sem, local_sem):
    for short, rows in ((True, lay.short), (False, lay.long)):

        @pl.when(is_short == short)
        def _():
            pair = first_pair + (unit_start // LEN_A if short else 0)
            column = pl.multiple_of(base_col + pair * WIDE, WIDE)
            first = pl.multiple_of(seq * rows + (0 if short else lay.split), 16)
            for part in range(BLOCK // rows):
                home = block * (BLOCK // rows) + part
                piece = source.at[pl.ds(pl.multiple_of(base + part * rows, 16), rows)]
                place = target.at[pl.ds(first, rows), pl.ds(column, WIDE)]

                @pl.when(home != me)
                def _():
                    remote(piece, place, send_sem, recv_sem, home).start()

                @pl.when(home == me)
                def _():
                    near = pltpu.make_async_copy(piece, place, local_sem)
                    near.start()
                    near.wait()


def wait_home(lay, is_short, scratch, sem, tensors, sent):
    for short in (True, False):
        own = 3 * lay.short if short else lay.long
        if sent:
            rows = (3 * LEN_A if short else LEN_B) - own
        else:
            rows = PAIRS * lay.sequences * (lay.short + lay.long) - own

        @pl.when(is_short == short)
        def _():
            for _ in range(tensors):
                piece = scratch.at[pl.ds(0, rows)]
                pltpu.make_async_copy(piece, piece, sem).wait()


class Planes:
    def __init__(self, n_dp):
        self.n = n_dp
        self.me = lax.axis_index("dp")
        self.outer = jnp.logical_or(self.me == 0, self.me == n_dp - 1)
        self.inner = jnp.logical_not(self.outer)
        self.inward = jnp.where(self.me == 0, 1, n_dp - 2)
        self.hosts = jnp.logical_or(self.me == 1, self.me == n_dp - 2)
        self.guest = jnp.where(self.me == 1, 0, n_dp - 1)

    def peers(self, n_sp):
        me = lax.axis_index("sp")
        found = plane_peers(n_sp)
        for sp in range(n_sp):
            found.append((self.outer, {"sp": sp, "dp": self.inward}))
            found.append((self.hosts, {"sp": sp, "dp": self.guest}))
        far = jnp.logical_and(self.inner, self.me + 1 < self.n - 1)
        found.append((far, {"sp": me, "dp": self.me + 1}))
        far = jnp.logical_and(self.inner, self.me - 1 > 0)
        found.append((far, {"sp": me, "dp": self.me - 1}))
        return found

    def takes(self, trained, up):
        other = self.me + 1 if up else self.me - 1
        low, high = (1, self.n - 2) if trained else (0, self.n - 1)
        return jnp.logical_and(other >= low, other <= high)


class Weights:
    def __init__(self, planes, own, every, send, recv, local):
        self.planes, self.own, self.every = planes, own, every
        self.send, self.recv, self.local = send, recv, local

    def copy(self, array, index, up, source):
        other = self.planes.me + 1 if up else self.planes.me - 1
        return remote(
            source, self.every[array].at[index], self.send.at[int(up), array, index], self.recv.at[array, index],
            {"dp": other},
        )

    def begin(self):
        me = self.planes.me
        for array in range(4):
            for up in (True, False):

                @pl.when(self.planes.takes(array < 2, up))
                def _():
                    self.copy(array, me, up, self.own[array]).start()

            pltpu.make_async_copy(self.own[array], self.every[array].at[me], self.local.at[array]).start()

    def own_wait(self):
        for array in range(4):
            pltpu.make_async_copy(self.own[array], self.every[array].at[self.planes.me], self.local.at[array]).wait()

    def pairs(self, array, distance):
        me, n = self.planes.me, self.planes.n
        used = self.planes.inner if array < 2 else True
        for up in (True, False):
            index = me - distance if up else me + distance
            comes = jnp.logical_and(used, jnp.logical_and(index >= 0, index < n))
            yield comes, jnp.logical_and(comes, self.planes.takes(array < 2, up)), jnp.clip(index, 0, n - 1), up

    def pass_on(self, arrays, distance):
        for array in arrays:
            for comes, goes, index, up in self.pairs(array, distance):

                @pl.when(comes)
                def _():
                    place = self.every[array].at[index]
                    pltpu.make_async_copy(place, place, self.recv.at[array, index]).wait()

                @pl.when(goes)
                def _():
                    self.copy(array, index, up, self.every[array].at[index]).start()

    def finish(self):
        for array in range(4):
            for distance in range(self.planes.n):
                for _, goes, index, up in self.pairs(array, distance):
                    goes = goes if distance else self.planes.takes(array < 2, up)

                    @pl.when(goes)
                    def _():
                        self.copy(array, index, up, self.every[array].at[index]).wait_send()


ROWS = 256


def gelu_parts(value):
    root = 0.7978845608028654
    square = value * value
    bent = jnp.tanh(root * value * (1.0 + 0.044715 * square))
    half = 0.5 + 0.5 * bent
    slope = half + 0.5 * value * (1.0 - bent * bent) * (root + 3.0 * 0.044715 * root * square)
    return value * half, slope


def slot_rows(lay, capacity, routes_t):
    n = lay.n
    experts, count = 2 * n, routes_t.shape[1]
    index = lax.broadcasted_iota(jnp.int32, (experts, count), 0)
    matches = [(index == routes_t[c : c + 1]).astype(F32) for c in range(2)]
    earlier = (
        lax.broadcasted_iota(jnp.int32, (count, count), 0) < lax.broadcasted_iota(jnp.int32, (count, count), 1)
    ).astype(F32)
    rank = dot((matches[0] + matches[1]).astype(BF16), earlier.astype(BF16))
    place = rank + (((index % n) * 2 + index // n) * capacity).astype(F32)
    return [jnp.sum(m * place, axis=0, keepdims=True).astype(jnp.int32) for m in matches]


def slot_columns(lay, capacity, routes):
    n = lay.n
    count = routes.shape[0]
    index = lax.broadcasted_iota(jnp.int32, (count, 128), 1)
    matches = [(index == routes[:, c : c + 1]).astype(F32) for c in range(2)]
    earlier = (
        lax.broadcasted_iota(jnp.int32, (count, count), 0) > lax.broadcasted_iota(jnp.int32, (count, count), 1)
    ).astype(F32)
    rank = dot(earlier.astype(BF16), (matches[0] + matches[1]).astype(BF16))
    place = rank + (((index % n) * 2 + index // n) * capacity).astype(F32)
    return [jnp.sum(m * place, axis=1, keepdims=True).astype(jnp.int32) for m in matches], matches


def hot(condition):
    return condition.astype(F32).astype(BF16)


def layer_kernel(
    lay, capacity, n_dp,
    tokens, gain_one, shift_one, w_qkv, w_out, gain_two, shift_two, w_router, routes, routes_t, cotangent, own_a, own_b, own_c, own_d,
    first_norm, unit, attended, log_total, home, middle, second_norm, gates_out, got, got_grad, first_grad, second_grad,
    all_a, all_b, all_c, all_d,
    staged, staged_out, packed, packed_grad, rows_in, rows_grad, weight_a, weight_b, out_sum, in_sum, grad_a, grad_b,
    send, recv, out_send, home_recv, local, stream_send, stream_recv, stream_local, load,
    row_send, row_recv, row_local, back_send, back_recv, back_local,
):
    n = lay.n
    me = lax.axis_index("sp")
    planes = Planes(n_dp)
    is_short, seq, first_pair = lay.role(me)
    meet(planes.peers(n))
    stream = Weights(
        planes, (own_a, own_b, own_c, own_d), (all_a, all_b, all_c, all_d), stream_send, stream_recv, stream_local
    )
    stream.begin()

    hat, _ = normed(tokens[...].astype(F32))
    first_norm[...] = (hat * gain_one[...] + shift_one[...]).astype(BF16)
    started = []
    for chunk in range(9):
        kind, third = divmod(chunk, 3)
        made = dot(first_norm[...], w_qkv[:, chunk * 2 * WIDE : (chunk + 1) * 2 * WIDE]).astype(BF16)
        staged[chunk] = made * BF16(HEAD_DIM**-0.5) if kind == 0 else made
        count = len(lay.owners())
        started += to_owners(
            lay,
            me,
            lambda pair: (pair % 2) * WIDE,
            lambda number: chunk * count + number,
            staged.at[chunk],
            lambda start, rows: unit.at[kind, pl.ds(pl.multiple_of(start, 16), rows)],
            send,
            recv.at[kind],
            local,
            (2 * third, 2 * third + 1),
        )
    for kind in range(3):
        wait_unit(lay, is_short, unit.at[kind], recv.at[kind])
    keep = lanes_first()
    lower = causal(BLOCK)

    def task(index, carry):
        start, block = lay.task(is_short, index)
        base = pl.multiple_of(start + block * BLOCK, BLOCK)
        queries = halves(unit[0, pl.ds(base, BLOCK)])

        def visit(place, state, diagonal):
            keys = unit[1, pl.ds(place, BLOCK)]
            values = unit[2, pl.ds(place, BLOCK)]
            result = []
            for (peak, total, summed), query in zip(state, queries):
                scores = dot_t(query, keys)
                if diagonal:
                    scores = jnp.where(lower, scores, NEGATIVE)
                new_peak = jnp.maximum(peak, jnp.max(scores, axis=1, keepdims=True))
                factor = jnp.exp(peak - new_peak)
                weight = jnp.exp(scores - new_peak)
                total = total * factor + jnp.sum(weight, axis=1, keepdims=True)
                summed = summed * factor + dot(weight.astype(BF16), values)
                result.append((new_peak, total, summed))
            return tuple(result)

        empty = (jnp.full((BLOCK, 1), NEGATIVE, F32), jnp.zeros((BLOCK, 1), F32), jnp.zeros((BLOCK, WIDE), F32))
        state = lax.fori_loop(
            0, block, lambda j, state: visit(pl.multiple_of(start + j * BLOCK, BLOCK), state, False), (empty, empty)
        )
        (peak_a, total_a, summed_a), (peak_b, total_b, summed_b) = visit(base, state, True)
        result = jnp.where(keep, summed_a / total_a, summed_b / total_b)
        attended[pl.ds(base, BLOCK)] = result
        staged_out[pl.ds(base, BLOCK)] = result.astype(BF16)
        log_total[pl.ds(base, BLOCK)] = jnp.where(keep, peak_a + jnp.log(total_a), peak_b + jnp.log(total_b))
        send_home(
            lay, me, is_short, seq, first_pair, base, block, start, staged_out, home, 0, out_send, home_recv, local
        )
        return carry

    lax.fori_loop(0, lay.tasks(is_short), task, 0)
    finish_sends(me, started)
    wait_home(lay, is_short, staged_out, out_send, 1, True)
    wait_home(lay, is_short, staged_out, home_recv, 1, False)

    span = n * capacity
    width, hidden = grad_a.shape
    x1 = tokens[...].astype(F32) + dot(home[...], w_out[...])
    middle[...] = x1
    hat, _ = normed(x1)
    second = (hat * gain_two[...] + shift_two[...]).astype(BF16)
    second_norm[...] = second
    place = slot_rows(lay, capacity, routes_t[...])
    count = tokens.shape[0]

    def dispatch_copies(source, target, which, kind):
        plane = jnp.where(planes.outer, planes.inward, planes.me) if kind == 0 else planes.me
        area = jnp.where(planes.outer, 1, 0) if kind == 0 else 2
        base = pl.multiple_of(area * span + me * capacity, 16)
        into = target.at[pl.ds(base, capacity)]
        for step in range(n):
            to = lax.rem(me + step, n)
            piece = source.at[pl.ds(pl.multiple_of((to * 2 + kind) * capacity, 16), capacity)]
            far = remote(
                piece, into, row_send.at[which, kind, step], row_recv.at[which, area, me], {"sp": to, "dp": plane}
            )
            if step:
                yield True, far
                continue
            if kind == 0:
                yield planes.outer, far
            stays = planes.inner if kind == 0 else True
            yield stays, pltpu.make_async_copy(piece, into, row_local.at[which, kind])

    def each(copies, act):
        for condition, copy in copies:
            if condition is True:
                act(copy)
            else:

                @pl.when(condition)
                def _():
                    act(copy)

    def dispatch(source, target, which):
        for kind in range(2):
            each(dispatch_copies(source, target, which, kind), lambda copy: copy.start())

    for start in range(0, 2 * span, ROWS):
        slots = start + lax.broadcasted_iota(jnp.int32, (ROWS, count), 0)
        packed[start : start + ROWS] = dot(hot(jnp.logical_or(slots == place[0], slots == place[1])), second).astype(BF16)
    dispatch(packed, rows_in, 0)
    logits = dot(second, w_router[...])
    index = lax.broadcasted_iota(jnp.int32, logits.shape, 1)
    chosen = [jnp.sum(jnp.where(index == routes[:, c : c + 1], logits, 0.0), axis=1, keepdims=True) for c in range(2)]
    top = jnp.maximum(chosen[0], chosen[1])
    exped = [jnp.exp(value - top) for value in chosen]
    gates = [value / (exped[0] + exped[1]) for value in exped]
    upstream = cotangent[...].astype(F32)
    lane = lax.broadcasted_iota(jnp.int32, gates_out.shape, 1)
    gates_out[...] = jnp.where(lane == 0, gates[0], gates[1])
    route_grads = [(gate * upstream).astype(BF16) for gate in gates]
    for start in range(0, 2 * span, ROWS):
        slots = start + lax.broadcasted_iota(jnp.int32, (ROWS, count), 0)
        packed_grad[start : start + ROWS] = sum(dot(hot(slots == place[c]), route_grads[c]) for c in range(2)).astype(BF16)
    dispatch(packed_grad, rows_grad, 1)
    stream.own_wait()
    stream.pass_on(range(4), 1)

    def arrived(which, area, host):
        buffer = (rows_in, rows_grad)[which]
        for src in range(n):
            piece = buffer.at[pl.ds(area * span + src * capacity, capacity)]
            wait = pltpu.make_async_copy(piece, piece, row_recv.at[which, area, src]).wait
            if host:
                wait()
            else:
                pl.when(src != me)(wait)

    for which, (source, target) in enumerate(((packed, rows_in), (packed_grad, rows_grad))):
        for kind in range(2):
            each(
                dispatch_copies(source, target, which, kind),
                lambda copy: copy.wait_send() if hasattr(copy, "wait_send") and copy.is_remote else copy.wait(),
            )

    def work(trained, first_row, rows):
        def clear(index, carry):
            part = pl.ds(pl.multiple_of(index * ROWS, ROWS), ROWS)
            out_sum[part] = jnp.zeros((ROWS, out_sum.shape[1]), F32)
            in_sum[part] = jnp.zeros((ROWS, in_sum.shape[1]), F32)
            return carry

        lax.fori_loop(0, rows // ROWS, clear, 0)
        arrays = (0, 1) if trained else (2, 3)
        every = (all_a, all_b) if trained else (all_c, all_d)

        def one(step, carry):
            distance, side = step // 2, lax.rem(step, 2)
            index = jnp.where(side == 0, planes.me - distance, planes.me + distance)
            real = jnp.logical_and(jnp.logical_and(index >= 0, index < n_dp), jnp.logical_or(side == 0, distance > 0))

            @pl.when(jnp.logical_and(side == 0, distance >= 2))
            def _():
                stream.pass_on(arrays, distance)

            @pl.when(real)
            def _():
                loads = [
                    pltpu.make_async_copy(every[i].at[index], (weight_a, weight_b)[i], load.at[i]) for i in range(2)
                ]
                for copy in loads:
                    copy.start()
                for copy in loads:
                    copy.wait()

                def chunk(number, carry):
                    part = pl.ds(pl.multiple_of(number * ROWS, ROWS), ROWS)
                    here = pl.ds(pl.multiple_of(first_row + number * ROWS, ROWS), ROWS)
                    active, slope = gelu_parts(dot(rows_in[here], weight_a[...]))
                    active = active.astype(BF16)
                    back = (dot_t(rows_grad[here], weight_b[...]) * slope).astype(BF16)
                    if trained:
                        packed[part, :hidden] = active
                        packed_grad[part, :hidden] = back
                    out_sum[part] += dot(active, weight_b[...])
                    in_sum[part] += dot_t(back, weight_a[...])
                    return carry

                lax.fori_loop(0, rows // ROWS, chunk, 0)
                if trained:
                    stores = [
                        pltpu.make_async_copy(stage, whole.at[index], load.at[2 + i])
                        for i, (stage, whole) in enumerate(((grad_a, first_grad), (grad_b, second_grad)))
                    ]
                    for total in (span, 2 * span):

                        @pl.when(planes.hosts == (total > span))
                        def _():
                            every_row = pl.ds(0, total)
                            for col in range(0, width, WIDE):
                                cut = pl.ds(col, WIDE)
                                grad_a[cut] = t_dot(rows_in[every_row, cut], packed_grad[every_row, :hidden]).astype(BF16)
                            for col in range(0, hidden, WIDE):
                                cut = pl.ds(col, WIDE)
                                grad_b[cut] = t_dot(packed[every_row, cut], rows_grad[every_row]).astype(BF16)

                    for copy in stores:
                        copy.start()
                    for copy in stores:
                        copy.wait()

            return carry

        lax.fori_loop(0, 2 * n_dp, one, 0)

        def turn(number, carry):
            part = pl.ds(pl.multiple_of(number * ROWS, ROWS), ROWS)
            here = pl.ds(pl.multiple_of(first_row + number * ROWS, ROWS), ROWS)
            rows_in[here] = out_sum[part].astype(BF16)
            rows_grad[here] = in_sum[part].astype(BF16)
            return carry

        lax.fori_loop(0, rows // ROWS, turn, 0)

    def back_copies(kind, guest):
        area = 2 if kind else int(guest)
        plane = planes.guest if guest else planes.me
        for which, (source, target) in enumerate(((rows_in, got), (rows_grad, got_grad))):
            into = target.at[pl.ds(pl.multiple_of((me * 2 + kind) * capacity, 16), capacity)]
            for step in range(n):
                to = lax.rem(me + step, n)
                piece = source.at[pl.ds(pl.multiple_of(area * span + to * capacity, 16), capacity)]
                if step or guest:
                    yield True, remote(
                        piece, into, back_send.at[which, area, step], back_recv.at[which, kind, me], {"sp": to, "dp": plane}
                    )
                else:
                    yield True, pltpu.make_async_copy(piece, into, back_local.at[which, kind])

    @pl.when(planes.inner)
    def _():
        arrived(0, 0, False)
        arrived(1, 0, False)

        @pl.when(planes.hosts)
        def _():
            arrived(0, 1, True)
            arrived(1, 1, True)

        work(True, 0, jnp.where(planes.hosts, 2 * span, span))
        each(back_copies(0, False), lambda copy: copy.start())

        @pl.when(planes.hosts)
        def _():
            each(back_copies(0, True), lambda copy: copy.start())

    arrived(0, 2, False)
    arrived(1, 2, False)
    work(False, 2 * span, span)
    each(back_copies(1, False), lambda copy: copy.start())
    ended = lambda copy: copy.wait_send() if copy.is_remote else copy.wait()
    each(back_copies(1, False), ended)

    @pl.when(planes.inner)
    def _():
        each(back_copies(0, False), ended)

        @pl.when(planes.hosts)
        def _():
            each(back_copies(0, True), ended)

    for kind in range(2):
        for which, buffer in enumerate((got, got_grad)):
            for src in range(n):
                piece = buffer.at[pl.ds((src * 2 + kind) * capacity, capacity)]
                comes = jnp.logical_or(src != me, planes.outer) if kind == 0 else src != me
                pl.when(comes)(pltpu.make_async_copy(piece, piece, back_recv.at[which, kind, src]).wait)
    stream.finish()


ANY = pl.BlockSpec(memory_space=pl.ANY)


def layer(lay, capacity, n_dp, tokens, gain_one, shift_one, w_qkv, w_out, gain_two, shift_two, w_router, routes, cotangent, weights):
    count, width = tokens.shape
    n = lay.n
    owners = len(lay.owners())
    span = n * capacity
    shape = jax.ShapeDtypeStruct
    hidden = weights[0].shape[1]
    every = [shape((n_dp, *weight.shape), BF16) for weight in weights]
    return pl.pallas_call(
        functools.partial(layer_kernel, lay, capacity, n_dp),
        out_shape=(
            shape((count, width), BF16),
            shape((3, UNIT, WIDE), BF16),
            shape((UNIT, WIDE), F32),
            shape((UNIT, WIDE), F32),
            shape((count, width), BF16),
            shape((count, width), F32),
            shape((count, width), BF16),
            shape((count, 128), F32),
            shape((2 * span, width), BF16),
            shape((2 * span, width), BF16),
            every[0],
            every[1],
            *every,
        ),
        in_specs=[VMEM] * 11 + [ANY] * 4,
        out_specs=[VMEM] * 8 + [ANY] * 8,
        scratch_shapes=[
            pltpu.VMEM((9, count, 2 * WIDE), BF16),
            pltpu.VMEM((UNIT, WIDE), BF16),
            pltpu.VMEM((2 * span, width), BF16),
            pltpu.VMEM((2 * span, width), BF16),
            pltpu.VMEM((3 * span, width), BF16),
            pltpu.VMEM((3 * span, width), BF16),
            pltpu.VMEM((width, hidden), BF16),
            pltpu.VMEM((hidden, width), BF16),
            pltpu.VMEM((2 * span, width), F32),
            pltpu.VMEM((2 * span, width), F32),
            pltpu.VMEM((width, hidden), BF16),
            pltpu.VMEM((hidden, width), BF16),
            DMA((9 * owners,)),
            DMA((3,)),
            DMA,
            DMA,
            DMA,
            DMA((2, 4, n_dp)),
            DMA((4, n_dp)),
            DMA((4,)),
            DMA((4,)),
            DMA((2, 2, n)),
            DMA((2, 3, n)),
            DMA((2, 2)),
            DMA((2, 3, n)),
            DMA((2, 2, n)),
            DMA((2, 2)),
        ],
        compiler_params=pltpu.CompilerParams(collective_id=0, has_side_effects=True, vmem_limit_bytes=60 * 2**20),
        cost_estimate=pl.CostEstimate(flops=50 * 10**9, bytes_accessed=100 * 2**20, transcendentals=10**7),
        name="layer",
    )(
        tokens, gain_one, shift_one, w_qkv, w_out, gain_two, shift_two, w_router, routes, routes.T, cotangent, *weights
    )


def back_kernel(
    lay, capacity,
    got, got_grad, middle, second_norm, gates, home_out, w_out, gain_two, w_router, routes, cotangent,
    unit, attended, log_total, first_norm, tokens, gain_one, w_qkv,
    block_out, tokens_grad, grads,
    grad_attended, grad_out, deltas, query_sum, staged, home, send, recv, out_send, home_recv, local,
):
    me = lax.axis_index("sp")
    is_short, seq, first_pair = lay.role(me)
    meet(plane_peers(lay.n))
    place, matches = slot_columns(lay, capacity, routes[...])
    slots = lax.broadcasted_iota(jnp.int32, (tokens.shape[0], got.shape[0]), 1)
    chosen = [hot(slots == place[c]) for c in range(2)]
    upstream = cotangent[...].astype(F32)
    gate = [gates[:, c : c + 1] for c in range(2)]
    total = middle[...]
    grad_gate = []
    for c in range(2):
        produced = dot(chosen[c], got[...])
        total = total + gate[c] * produced
        grad_gate.append(jnp.sum(upstream * produced, axis=1, keepdims=True))
    block_out[...] = total.astype(BF16)
    mean_grad = gate[0] * grad_gate[0] + gate[1] * grad_gate[1]
    grad_logits = sum(matches[c] * (gate[c] * (grad_gate[c] - mean_grad)) for c in range(2))
    high = grad_logits.astype(BF16)
    low = (grad_logits - high.astype(F32)).astype(BF16)
    router_grad = t_dot(second_norm[...], high) + t_dot(second_norm[...], low)
    grad_second = dot_t(high, w_router[...]) + dot_t(low, w_router[...])
    grad_second = grad_second + dot(chosen[0] + chosen[1], got_grad[...])
    hat, scale = normed(middle[...])
    gain_two_grad = jnp.sum(grad_second * hat, axis=0, keepdims=True)
    shift_two_grad = jnp.sum(grad_second, axis=0, keepdims=True)
    grad = upstream + norm_back(grad_second, gain_two[...], hat, scale)
    tokens_grad[...] = grad
    branch = grad.astype(BF16)
    grad_attended[...] = dot_t(branch, w_out[...]).astype(BF16)
    out_proj = t_dot(home_out[...], branch)
    width = w_out.shape[0]
    grads[:width, 3 * width : 4 * width] = out_proj.astype(BF16)
    grads[:width, 4 * width :] = router_grad.astype(BF16)
    started = to_owners(
        lay,
        me,
        lambda pair: pair * WIDE,
        lambda number: number,
        grad_attended,
        lambda start, rows: grad_out.at[pl.ds(pl.multiple_of(start, 16), rows)],
        send,
        recv,
        local,
        range(PAIRS),
    )
    query_sum[...] = jnp.zeros_like(query_sum)
    keep = lanes_first()
    lower = causal(BLOCK)
    wait_unit(lay, is_short, grad_out, recv)

    def make_delta(index, carry):
        part = pl.ds(pl.multiple_of(index * BLOCK, BLOCK), BLOCK)
        first, second = halves(grad_out[part].astype(F32) * attended[part])
        deltas[part] = jnp.where(
            keep, jnp.sum(first, axis=1, keepdims=True), jnp.sum(second, axis=1, keepdims=True)
        )
        return carry

    lax.fori_loop(0, lay.tasks(is_short), make_delta, 0)
    per = jnp.where(is_short, LEN_A // BLOCK, LEN_B // BLOCK)

    def task(index, carry):
        start, block = lay.task(is_short, index)
        base = pl.multiple_of(start + block * BLOCK, BLOCK)
        keys = unit[1, pl.ds(base, BLOCK)]
        values = unit[2, pl.ds(base, BLOCK)]
        key_both = jnp.concatenate(halves(keys), axis=0)

        def visit(place, state, diagonal):
            part = pl.ds(place, BLOCK)
            grad_key, grad_value = state
            queries = halves(unit[0, part])
            outs = halves(grad_out[part])
            weights, grads = [], []
            for which, (query, out) in enumerate(zip(queries, outs)):
                column = which * HEAD_DIM
                scores = dot_t(query, keys)
                if diagonal:
                    scores = jnp.where(lower, scores, NEGATIVE)
                weight = jnp.exp(scores - log_total[part, column : column + 1])
                grad = weight * (dot_t(out, values) - deltas[part, column : column + 1])
                weights.append(weight.astype(BF16))
                grads.append(grad.astype(BF16))
            grad_value = grad_value + t_dot(jnp.concatenate(weights, axis=0), jnp.concatenate(outs, axis=0))
            grad_key = grad_key + t_dot(jnp.concatenate(grads, axis=0), jnp.concatenate(queries, axis=0))
            query_sum[part] += dot(jnp.concatenate(grads, axis=1), key_both)
            return grad_key, grad_value

        zero = jnp.zeros((BLOCK, WIDE), F32)
        state = visit(base, (zero, zero), True)
        grad_key, grad_value = lax.fori_loop(
            block + 1, per, lambda i, state: visit(pl.multiple_of(start + i * BLOCK, BLOCK), state, False), state
        )
        part = pl.ds(base, BLOCK)
        staged[0, part] = (query_sum[part] * HEAD_DIM**-0.5).astype(BF16)
        staged[1, part] = grad_key.astype(BF16)
        staged[2, part] = grad_value.astype(BF16)
        for kind in range(3):
            send_home(
                lay, me, is_short, seq, first_pair, base, block, start, staged.at[kind], home, kind * PAIRS * WIDE,
                out_send.at[kind], home_recv.at[kind], local,
            )
        return carry

    lax.fori_loop(0, lay.tasks(is_short), task, 0)
    for kind in range(3):
        wait_home(lay, is_short, staged.at[kind], home_recv.at[kind], 1, False)
    grad_first = dot_t(home[...], w_qkv[...])
    hat, scale = normed(tokens[...].astype(F32))
    gain_one_grad = jnp.sum(grad_first * hat, axis=0, keepdims=True)
    shift_one_grad = jnp.sum(grad_first, axis=0, keepdims=True)
    tokens_grad[...] += norm_back(grad_first, gain_one[...], hat, scale)
    width = grads.shape[0] - 16
    for chunk in range(0, 3 * PAIRS * WIDE, 2 * WIDE):
        grads[:width, chunk : chunk + 2 * WIDE] = t_dot(first_norm[...], home[:, chunk : chunk + 2 * WIDE]).astype(BF16)
    grads[width:, :] = jnp.zeros((16, grads.shape[1]), BF16)
    for number, vector in enumerate((gain_one_grad, shift_one_grad, gain_two_grad, shift_two_grad)):
        grads[width : width + 1, number * width : (number + 1) * width] = vector.astype(BF16)
    finish_sends(me, started)
    for kind in range(3):
        wait_home(lay, is_short, staged.at[kind], out_send.at[kind], 1, True)


def backward(lay, capacity, values):
    count, width = values[2].shape
    owners = len(lay.owners())
    shape = jax.ShapeDtypeStruct
    return pl.pallas_call(
        functools.partial(back_kernel, lay, capacity),
        out_shape=(shape((count, width), BF16), shape((count, width), F32), shape((width + 16, 4 * width + 128), BF16)),
        in_specs=[VMEM] * 18,
        out_specs=[VMEM] * 3,
        scratch_shapes=[
            pltpu.VMEM((count, width), BF16),
            pltpu.VMEM((UNIT, WIDE), BF16),
            pltpu.VMEM((UNIT, WIDE), F32),
            pltpu.VMEM((UNIT, WIDE), F32),
            pltpu.VMEM((3, UNIT, WIDE), BF16),
            pltpu.VMEM((count, 3 * width), BF16),
            DMA((owners,)),
            DMA,
            DMA((3,)),
            DMA((3,)),
            DMA,
        ],
        compiler_params=pltpu.CompilerParams(collective_id=1, has_side_effects=True, vmem_limit_bytes=60 * 2**20),
        cost_estimate=pl.CostEstimate(flops=16 * 10**9, bytes_accessed=60 * 2**20, transcendentals=5 * 10**6),
        name="backward",
    )(*values)


def reduce_kernel(
    n, first, second, first_out, second_out, below_a, below_b, above_a, above_b,
    mine_a, mine_b, theirs_a, theirs_b, sums_a, sums_b, send, recv, load,
):
    me = lax.axis_index("dp")
    inner = jnp.logical_and(me >= 1, me <= n - 2)
    meet([(me + 1 < n, {"dp": me + 1}), (me > 0, {"dp": me - 1})])
    own, mine, theirs = (first, second), (mine_a, mine_b), (theirs_a, theirs_b)
    from_below, from_above, sums = (below_a, below_b), (above_a, above_b), (sums_a, sums_b)

    def copy(array, index, up, source):
        target = (from_below if up else from_above)[array].at[index]
        return remote(
            source, target, send.at[int(up), array, index], recv.at[int(up), array, index], {"dp": me + 1 if up else me - 1}
        )

    def fetch(source, buffer, number):
        moved = pltpu.make_async_copy(source, buffer, load.at[number])
        moved.start()
        return moved

    def order(up):
        return range(n - 1, -1, -1) if up else range(n)

    def wanted(index, up):
        return jnp.logical_and(inner, index > me if up else index < me)

    for index_up, index_down in zip(order(True), order(False)):
        for array in range(2):
            for up, index in ((True, index_up), (False, index_down)):
                begins = me == 1 if up else me == n - 2

                @pl.when(jnp.logical_and(wanted(index, up), begins))
                def _():
                    copy(array, index, up, own[array].at[index]).start()

    def came(array, index, up):
        buffer = (from_below if up else from_above)[array].at[index]
        pltpu.make_async_copy(buffer, buffer, recv.at[int(up), array, index]).wait()
        return buffer

    for index_up, index_down in zip(order(True), order(False)):
        for array in range(2):
            for up, index in ((True, index_up), (False, index_down)):
                begins = me == 1 if up else me == n - 2

                @pl.when(jnp.logical_and(wanted(index, up), jnp.logical_not(begins)))
                def _():
                    here = fetch(own[array].at[index], mine[array], 0)
                    there = fetch(came(array, index, up), theirs[array], 1)
                    here.wait()
                    there.wait()
                    sums[array][int(up), index] = (mine[array][...].astype(F32) + theirs[array][...].astype(F32)).astype(BF16)
                    copy(array, index, up, sums[array].at[int(up), index]).start()

    for array, out in enumerate((first_out, second_out)):
        out[...] = jnp.zeros_like(out)

        @pl.when(inner)
        def _():
            fetch(own[array].at[me], mine[array], 0).wait()
            out[...] += mine[array][...].astype(F32)

        for up in (True, False):

            @pl.when(me >= 2 if up else me <= n - 3)
            def _():
                fetch(came(array, me, up), theirs[array], 1).wait()
                out[...] += theirs[array][...].astype(F32)

    for array in range(2):
        for up in (True, False):
            for index in range(n):

                @pl.when(wanted(index, up))
                def _():
                    copy(array, index, up, sums[array].at[int(up), index]).wait_send()


def reduce_grads(n, first, second):
    shape = jax.ShapeDtypeStruct
    width, hidden = first.shape[1:]
    found = pl.pallas_call(
        functools.partial(reduce_kernel, n),
        out_shape=(shape((width, hidden), F32), shape((hidden, width), F32), *(shape(g.shape, BF16) for g in (first, second, first, second))),
        in_specs=[ANY] * 2,
        out_specs=[VMEM] * 2 + [ANY] * 4,
        scratch_shapes=[
            pltpu.VMEM((width, hidden), BF16),
            pltpu.VMEM((hidden, width), BF16),
            pltpu.VMEM((width, hidden), BF16),
            pltpu.VMEM((hidden, width), BF16),
            pltpu.VMEM((2, *first.shape), BF16),
            pltpu.VMEM((2, *second.shape), BF16),
            DMA((2, 2, n)),
            DMA((2, 2, n)),
            DMA((2,)),
        ],
        compiler_params=pltpu.CompilerParams(collective_id=2, has_side_effects=True, vmem_limit_bytes=60 * 2**20),
        cost_estimate=pl.CostEstimate(flops=10**7, bytes_accessed=200 * 2**20, transcendentals=0),
        name="reduce_grads",
    )(first, second)
    return found[:2]


def shards(
    tokens, ln1_gain, ln1_shift, w_qkv, w_out, ln2_gain, ln2_shift, w_router,
    train_w1, train_w2, frozen_w1, frozen_w2, routes, cotangent,
):
    lay = Layout(lax.axis_size("sp"))
    n_dp = lax.axis_size("dp")
    tokens, routes, cotangent = tokens[0], routes[0], cotangent[0]
    count, width = tokens.shape
    capacity = 2 * count // lay.n
    experts = w_router.shape[1]
    row = lambda vector: vector.reshape(1, -1)
    router_wide = jnp.pad(w_router, ((0, 0), (0, 128 - experts)))
    weights = [weight[0] for weight in (train_w1, train_w2, frozen_w1, frozen_w2)]
    first_norm, unit, attended, log_total, home, middle, second, gates, got, got_grad, first_grad, second_grad, *_ = layer(
        lay, capacity, n_dp, tokens, row(ln1_gain), row(ln1_shift), w_qkv, w_out, row(ln2_gain), row(ln2_shift),
        router_wide, routes, cotangent, weights,
    )
    block_out, tokens_grad, grads = backward(
        lay, capacity,
        (
            got, got_grad, middle, second, gates, home, w_out, row(ln2_gain), router_wide, routes, cotangent,
            unit, attended, log_total, first_norm, tokens, row(ln1_gain), w_qkv,
        ),
    )
    first_grad, second_grad = reduce_grads(n_dp, first_grad, second_grad)
    total = lax.psum(grads, ("sp", "dp")).astype(F32)
    vectors = total[width, : 4 * width].reshape(4, width)
    return (
        block_out[None],
        tokens_grad[None],
        vectors[0],
        vectors[1],
        total[:width, : 3 * width],
        total[:width, 3 * width : 4 * width],
        vectors[2],
        vectors[3],
        total[:width, 4 * width : 4 * width + experts],
        first_grad[None],
        second_grad[None],
    )


def solution(mesh):
    in_specs = (
        P("dp", "sp", None), P(), P(), P(), P(), P(), P(), P(),
        P("sp", None, "dp"), P("sp", "dp", None), P("sp", None, "dp"), P("sp", "dp", None),
        P("dp", "sp", None), P("dp", "sp", None),
    )
    out_specs = (
        P("dp", "sp", None), P("dp", "sp", None), P(), P(), P(), P(), P(), P(), P(),
        P("sp", None, "dp"), P("sp", "dp", None),
    )
    return jax.shard_map(shards, mesh=mesh, in_specs=in_specs, out_specs=out_specs, check_vma=False)
```

```python
import functools
import math

import jax
import jax.numpy as jnp
from jax import lax
from jax.experimental import pallas as pl
from jax.experimental.pallas import tpu as pltpu
from jax.sharding import PartitionSpec as P

HEADS = 12
HEAD_DIM = 64
LEN_A = 1024
LEN_B = 2048
PAIRS = HEADS // 2
WIDE = 2 * HEAD_DIM
UNIT = 3 * LEN_A
BLOCK = 256
EPSILON = 1e-05
NEGATIVE = -1e30
MESH = pl.DeviceIdType.MESH
DMA = pltpu.SemaphoreType.DMA
F32 = jnp.float32
BF16 = jnp.bfloat16
VMEM = pl.BlockSpec(memory_space=pltpu.VMEM)


def dot(a, b):
    return jnp.dot(a, b, preferred_element_type=F32)


def dot_t(a, b):
    return lax.dot_general(a, b, (((1,), (1,)), ((), ())), preferred_element_type=F32)


def t_dot(a, b):
    return lax.dot_general(a, b, (((0,), (0,)), ((), ())), preferred_element_type=F32)


def normed(value):
    centre = jnp.mean(value, axis=-1, keepdims=True)
    centred = value - centre
    spread = jnp.mean(centred * centred, axis=-1, keepdims=True)
    scale = lax.rsqrt(spread + EPSILON)
    return centred * scale, scale


def norm_back(grad, gain, hat, scale):
    scaled = grad * gain
    first = jnp.mean(scaled, axis=-1, keepdims=True)
    second = jnp.mean(scaled * hat, axis=-1, keepdims=True)
    return (scaled - first - hat * second) * scale


class Layout:
    def __init__(self, n_sp):
        self.n = n_sp
        self.sequences = n_sp // 8
        self.short = LEN_A // n_sp
        self.long = LEN_B // n_sp
        self.split = self.sequences * self.short

    def owners(self):
        found = []
        for seq in range(self.sequences):
            for pair in range(PAIRS):
                number = seq * PAIRS + pair
                found.append((number + number // 3 + 1, True, self.split + seq * self.long, self.long, pair, 0))
                found.append((4 * (seq * 2 + pair // 3), False, seq * self.short, self.short, pair, (pair % 3) * LEN_A))
        return found

    def role(self, me):
        is_short = lax.rem(me, 4) == 0
        number = me - me // 4 - 1
        group = me // 4
        seq = jnp.where(is_short, group // 2, number // PAIRS)
        pair = jnp.where(is_short, 3 * lax.rem(group, 2), lax.rem(number, PAIRS))
        return is_short, seq, pair

    def task(self, is_short, index):
        per = LEN_A // BLOCK
        start = jnp.where(is_short, (index // per) * LEN_A, 0)
        block = jnp.where(is_short, lax.rem(index, per), index)
        return pl.multiple_of(start, BLOCK), block

    def tasks(self, is_short):
        return jnp.where(is_short, 3 * LEN_A // BLOCK, LEN_B // BLOCK)


def meet(peers):
    barrier = pltpu.get_barrier_semaphore()
    for wanted, device in peers:

        @pl.when(wanted)
        def _():
            pl.semaphore_signal(barrier, inc=1, device_id=device, device_id_type=MESH)

    pl.semaphore_wait(barrier, sum(jnp.asarray(wanted, jnp.int32) for wanted, _ in peers))


def plane_peers(n):
    me = lax.axis_index("sp")
    return [(True, {"sp": lax.rem(me + step, n)}) for step in range(1, n)]


def remote(source, target, send_sem, recv_sem, device):
    device = device if isinstance(device, dict) else {"sp": device}
    return pltpu.make_async_remote_copy(
        src_ref=source, dst_ref=target, send_sem=send_sem, recv_sem=recv_sem, device_id=device, device_id_type=MESH
    )


def lanes_first():
    return lax.broadcasted_iota(jnp.int32, (1, WIDE), 1) < HEAD_DIM


def halves(value):
    keep = lanes_first()
    zero = jnp.zeros_like(value)
    return jnp.where(keep, value, zero), jnp.where(keep, zero, value)


def causal(rows):
    return lax.broadcasted_iota(jnp.int32, (rows, rows), 0) >= lax.broadcasted_iota(jnp.int32, (rows, rows), 1)


def to_owners(lay, me, cols, slot, source, target, send_sems, recv_sem, local_sem, wanted):
    started = []
    for number, (owner, is_long, start, rows, pair, unit) in enumerate(lay.owners()):
        if pair not in wanted:
            continue
        piece = source.at[pl.ds(start, rows), pl.ds(cols(pair), WIDE)]
        place = target(unit + me * rows, rows)
        far = remote(piece, place, send_sems.at[slot(number)], recv_sem, owner)
        near = pltpu.make_async_copy(piece, place, local_sem)

        @pl.when(me != owner)
        def _():
            far.start()

        @pl.when(me == owner)
        def _():
            near.start()
            near.wait()

        started.append((owner, far))
    return started


def finish_sends(me, started):
    for owner, copy in started:

        @pl.when(me != owner)
        def _():
            copy.wait_send()


def wait_unit(lay, is_short, buffer, sem):
    for short, rows in ((True, 3 * (lay.n - 1) * lay.short), (False, (lay.n - 1) * lay.long)):

        @pl.when(is_short == short)
        def _():
            piece = buffer.at[pl.ds(0, rows)]
            pltpu.make_async_copy(piece, piece, sem).wait()


def send_home(lay, me, is_short, seq, first_pair, base, block, unit_start, source, target, base_col, send_sem, recv_sem, local_sem):
    for short, rows in ((True, lay.short), (False, lay.long)):

        @pl.when(is_short == short)
        def _():
            pair = first_pair + (unit_start // LEN_A if short else 0)
            column = pl.multiple_of(base_col + pair * WIDE, WIDE)
            first = pl.multiple_of(seq * rows + (0 if short else lay.split), 16)
            for part in range(BLOCK // rows):
                home = block * (BLOCK // rows) + part
                piece = source.at[pl.ds(pl.multiple_of(base + part * rows, 16), rows)]
                place = target.at[pl.ds(first, rows), pl.ds(column, WIDE)]

                @pl.when(home != me)
                def _():
                    remote(piece, place, send_sem, recv_sem, home).start()

                @pl.when(home == me)
                def _():
                    near = pltpu.make_async_copy(piece, place, local_sem)
                    near.start()
                    near.wait()


def wait_home(lay, is_short, scratch, sem, tensors, sent):
    for short in (True, False):
        own = 3 * lay.short if short else lay.long
        if sent:
            rows = (3 * LEN_A if short else LEN_B) - own
        else:
            rows = PAIRS * lay.sequences * (lay.short + lay.long) - own

        @pl.when(is_short == short)
        def _():
            for _ in range(tensors):
                piece = scratch.at[pl.ds(0, rows)]
                pltpu.make_async_copy(piece, piece, sem).wait()


class Planes:
    def __init__(self, n_dp):
        self.n = n_dp
        self.me = lax.axis_index("dp")
        self.outer = jnp.logical_or(self.me == 0, self.me == n_dp - 1)
        self.inner = jnp.logical_not(self.outer)
        self.inward = jnp.where(self.me == 0, 1, n_dp - 2)
        self.hosts = jnp.logical_or(self.me == 1, self.me == n_dp - 2)
        self.guest = jnp.where(self.me == 1, 0, n_dp - 1)

    def peers(self, n_sp):
        me = lax.axis_index("sp")
        found = plane_peers(n_sp)
        for sp in range(n_sp):
            found.append((self.outer, {"sp": sp, "dp": self.inward}))
            found.append((self.hosts, {"sp": sp, "dp": self.guest}))
        far = jnp.logical_and(self.inner, self.me + 1 < self.n - 1)
        found.append((far, {"sp": me, "dp": self.me + 1}))
        far = jnp.logical_and(self.inner, self.me - 1 > 0)
        found.append((far, {"sp": me, "dp": self.me - 1}))
        return found

    def takes(self, trained, up):
        other = self.me + 1 if up else self.me - 1
        low, high = (1, self.n - 2) if trained else (0, self.n - 1)
        return jnp.logical_and(other >= low, other <= high)


class Weights:
    def __init__(self, planes, own, every, send, recv):
        self.planes, self.own, self.every = planes, own, every
        self.send, self.recv = send, recv

    def copy(self, array, index, up, source):
        other = self.planes.me + 1 if up else self.planes.me - 1
        return remote(
            source, self.every[array].at[index], self.send.at[int(up), array, index], self.recv.at[array, index],
            {"dp": other},
        )

    def begin(self, arrays):
        me = self.planes.me
        for array in arrays:
            for up in (True, False):

                @pl.when(self.planes.takes(array < 2, up))
                def _():
                    self.copy(array, me, up, self.own[array]).start()

    def pairs(self, array, distance):
        me, n = self.planes.me, self.planes.n
        used = self.planes.inner if array < 2 else True
        for up in (True, False):
            index = me - distance if up else me + distance
            comes = jnp.logical_and(used, jnp.logical_and(index >= 0, index < n))
            yield comes, jnp.logical_and(comes, self.planes.takes(array < 2, up)), jnp.clip(index, 0, n - 1), up

    def pass_on(self, arrays, distance):
        for array in arrays:
            for comes, goes, index, up in self.pairs(array, distance):

                @pl.when(comes)
                def _():
                    place = self.every[array].at[index]
                    pltpu.make_async_copy(place, place, self.recv.at[array, index]).wait()

                @pl.when(goes)
                def _():
                    self.copy(array, index, up, self.every[array].at[index]).start()

    def finish(self):
        for array in range(4):
            for distance in range(self.planes.n):
                for _, goes, index, up in self.pairs(array, distance):
                    goes = goes if distance else self.planes.takes(array < 2, up)

                    @pl.when(goes)
                    def _():
                        self.copy(array, index, up, self.every[array].at[index]).wait_send()


ROWS = 256
LIMIT = 60 * 2**20


def gelu_parts(value):
    root = 0.7978845608028654
    square = value * value
    bent = jnp.tanh(root * value * (1.0 + 0.044715 * square))
    half = 0.5 + 0.5 * bent
    slope = half + 0.5 * value * (1.0 - bent * bent) * (root + 3.0 * 0.044715 * root * square)
    return value * half, slope


def slot_rows(lay, capacity, routes_t):
    n = lay.n
    experts, count = 2 * n, routes_t.shape[1]
    index = lax.broadcasted_iota(jnp.int32, (experts, count), 0)
    matches = [(index == routes_t[c : c + 1]).astype(F32) for c in range(2)]
    earlier = (
        lax.broadcasted_iota(jnp.int32, (count, count), 0) < lax.broadcasted_iota(jnp.int32, (count, count), 1)
    ).astype(F32)
    rank = dot((matches[0] + matches[1]).astype(BF16), earlier.astype(BF16))
    place = rank + (((index % n) * 2 + index // n) * capacity).astype(F32)
    return [jnp.sum(m * place, axis=0, keepdims=True).astype(jnp.int32) for m in matches]


def slot_columns(lay, capacity, routes):
    n = lay.n
    count = routes.shape[0]
    index = lax.broadcasted_iota(jnp.int32, (count, 128), 1)
    matches = [(index == routes[:, c : c + 1]).astype(F32) for c in range(2)]
    earlier = (
        lax.broadcasted_iota(jnp.int32, (count, count), 0) > lax.broadcasted_iota(jnp.int32, (count, count), 1)
    ).astype(F32)
    rank = dot(earlier.astype(BF16), (matches[0] + matches[1]).astype(BF16))
    place = rank + (((index % n) * 2 + index // n) * capacity).astype(F32)
    return [jnp.sum(m * place, axis=1, keepdims=True).astype(jnp.int32) for m in matches], matches


def hot(condition):
    return condition.astype(F32).astype(BF16)


def layer_kernel(
    lay, capacity, n_dp,
    tokens, vectors, w_qkv, w_out, w_router, routes, routes_t, cotangent, own_a, own_b, own_c, own_d,
    first_norm, unit, attended, log_total, home, middle, second_norm, gates_out, got, got_grad, first_grad, second_grad,
    all_a, all_b, all_c, all_d, hop_a, hop_b,
    staged_out, packed, packed_grad, rows_in, rows_grad, weight_a, weight_b, out_sum, in_sum, out_other, in_other, grad_a, grad_b,
    packed_gates, rows_gates, send, recv, out_send, home_recv, local, stream_send, stream_recv, load,
    row_send, row_recv, row_local, back_send, back_recv, back_local, hop_send, hop_recv,
):
    n = lay.n
    me = lax.axis_index("sp")
    gain_one, shift_one, gain_two, shift_two = (vectors.at[i : i + 1] for i in range(4))
    planes = Planes(n_dp)
    is_short, seq, first_pair = lay.role(me)
    meet(planes.peers(n))
    stream = Weights(
        planes, (own_a, own_b, own_c, own_d), (all_a, all_b, all_c, all_d), stream_send, stream_recv
    )
    stream.begin((2, 3))

    hat, _ = normed(tokens[...].astype(F32))
    first_norm[...] = (hat * gain_one[...] + shift_one[...]).astype(BF16)
    started = []
    for chunk in range(9):
        kind, third = divmod(chunk, 3)
        made = dot(first_norm[...], w_qkv[:, chunk * 2 * WIDE : (chunk + 1) * 2 * WIDE]).astype(BF16)
        made = made * BF16(HEAD_DIM**-0.5) if kind == 0 else made
        area = packed.at[pl.ds(kind * tokens.shape[0], tokens.shape[0]), pl.ds(third * 2 * WIDE, 2 * WIDE)]
        area[...] = made
        count = len(lay.owners())
        started += to_owners(
            lay,
            me,
            lambda pair: (pair % 2) * WIDE,
            lambda number: chunk * count + number,
            area,
            lambda start, rows: unit.at[kind, pl.ds(pl.multiple_of(start, 16), rows)],
            send,
            recv.at[kind],
            local,
            (2 * third, 2 * third + 1),
        )
    span = n * capacity
    width, hidden = grad_a.shape
    count = tokens.shape[0]
    place = slot_rows(lay, capacity, routes_t[...])

    def dispatch_copies(which, kind):
        source, target = ((packed, rows_in), (packed_grad, rows_grad), (packed_gates, rows_gates))[which]
        plane = jnp.where(planes.outer, planes.inward, planes.me) if kind == 0 else planes.me
        area = jnp.where(planes.outer, 1, 0) if kind == 0 else 2

        def block(buffer, number):
            if which == 2:
                return buffer.at[number]
            return buffer.at[pl.ds(pl.multiple_of(number * capacity, 16), capacity)]

        into = block(target, area * n + me)
        for step in range(n):
            to = lax.rem(me + step, n)
            piece = block(source, to * 2 + kind)
            far = remote(
                piece, into, row_send.at[which, kind, step], row_recv.at[which, area, me], {"sp": to, "dp": plane}
            )
            if step:
                yield True, far
                continue
            if kind == 0:
                yield planes.outer, far
            stays = planes.inner if kind == 0 else True
            yield stays, pltpu.make_async_copy(piece, into, row_local.at[which, kind])

    def each(copies, act):
        for condition, copy in copies:
            if condition is True:
                act(copy)
            else:
                pl.when(condition)(functools.partial(act, copy))

    def start(copy):
        copy.start()

    def end(copy):
        if copy.is_remote:
            copy.wait_send()
        else:
            copy.wait()

    def dispatch(which):
        for kind in range(2):
            each(dispatch_copies(which, kind), start)

    for first in range(0, 2 * span, ROWS):
        slots = first + lax.broadcasted_iota(jnp.int32, (ROWS, count), 0)
        chosen = hot(jnp.logical_or(slots == place[0], slots == place[1]))
        packed_grad[first : first + ROWS] = dot(chosen, cotangent[...]).astype(BF16)
    dispatch(1)
    for kind in range(3):
        wait_unit(lay, is_short, unit.at[kind], recv.at[kind])
    keep = lanes_first()
    lower = causal(BLOCK)

    def task(index, carry):
        start, block = lay.task(is_short, index)
        base = pl.multiple_of(start + block * BLOCK, BLOCK)
        queries = halves(unit[0, pl.ds(base, BLOCK)])

        def visit(place, state, diagonal):
            keys = unit[1, pl.ds(place, BLOCK)]
            values = unit[2, pl.ds(place, BLOCK)]
            result = []
            for (peak, total, summed), query in zip(state, queries):
                scores = dot_t(query, keys)
                if diagonal:
                    scores = jnp.where(lower, scores, NEGATIVE)
                new_peak = jnp.maximum(peak, jnp.max(scores, axis=1, keepdims=True))
                factor = jnp.exp(peak - new_peak)
                weight = jnp.exp(scores - new_peak)
                total = total * factor + jnp.sum(weight, axis=1, keepdims=True)
                summed = summed * factor + dot(weight.astype(BF16), values)
                result.append((new_peak, total, summed))
            return tuple(result)

        empty = (jnp.full((BLOCK, 1), NEGATIVE, F32), jnp.zeros((BLOCK, 1), F32), jnp.zeros((BLOCK, WIDE), F32))
        state = lax.fori_loop(
            0, block, lambda j, state: visit(pl.multiple_of(start + j * BLOCK, BLOCK), state, False), (empty, empty)
        )
        (peak_a, total_a, summed_a), (peak_b, total_b, summed_b) = visit(base, state, True)
        result = jnp.where(keep, summed_a / total_a, summed_b / total_b)
        attended[pl.ds(base, BLOCK)] = result
        staged_out[pl.ds(base, BLOCK)] = result.astype(BF16)
        log_total[pl.ds(base, BLOCK)] = jnp.where(keep, peak_a + jnp.log(total_a), peak_b + jnp.log(total_b))
        send_home(
            lay, me, is_short, seq, first_pair, base, block, start, staged_out, home, 0, out_send, home_recv, local
        )
        return carry

    lax.fori_loop(0, lay.tasks(is_short), task, 0)
    finish_sends(me, started)
    wait_home(lay, is_short, staged_out, out_send, 1, True)
    wait_home(lay, is_short, staged_out, home_recv, 1, False)

    stream.begin((0, 1))
    stream.pass_on((2, 3), 1)
    x1 = tokens[...].astype(F32) + dot(home[...], w_out[...])
    middle[...] = x1
    hat, _ = normed(x1)
    second = (hat * gain_two[...] + shift_two[...]).astype(BF16)
    second_norm[...] = second
    for first in range(0, 2 * span, ROWS):
        slots = first + lax.broadcasted_iota(jnp.int32, (ROWS, count), 0)
        chosen = hot(jnp.logical_or(slots == place[0], slots == place[1]))
        packed[first : first + ROWS] = dot(chosen, second).astype(BF16)
    dispatch(0)
    logits = dot(second, w_router[...])
    index = lax.broadcasted_iota(jnp.int32, logits.shape, 1)
    chosen = [jnp.sum(jnp.where(index == routes[:, c : c + 1], logits, 0.0), axis=1, keepdims=True) for c in range(2)]
    top = jnp.maximum(chosen[0], chosen[1])
    exped = [jnp.exp(value - top) for value in chosen]
    gates = [value / (exped[0] + exped[1]) for value in exped]
    lane = lax.broadcasted_iota(jnp.int32, gates_out.shape, 1)
    gates_out[...] = jnp.where(lane == 0, gates[0], gates[1])
    column, _ = slot_columns(lay, capacity, routes[...])
    for number in range(2 * n):
        held = [
            jnp.where(jnp.logical_and(lane < capacity, lane + number * capacity == column[c]), gates[c], 0.0)
            for c in range(2)
        ]
        packed_gates[number] = jnp.broadcast_to(jnp.sum(held[0] + held[1], axis=0, keepdims=True), (8, 128))
    dispatch(2)

    def arrived(which, area):
        buffer = (rows_in, rows_grad, rows_gates)[which]
        for src in range(n):
            piece = buffer.at[area * n + src] if which == 2 else buffer.at[pl.ds((area * n + src) * capacity, capacity)]
            wait = pltpu.make_async_copy(piece, piece, row_recv.at[which, area, src]).wait
            if area == 1:
                wait()
            else:
                pl.when(src != me)(wait)

    for which in (1, 0, 2):
        for kind in range(2):
            each(dispatch_copies(which, kind), end)

    def take(area):
        for which in (1, 0, 2):
            arrived(which, area)
        one = lax.broadcasted_iota(jnp.int32, (capacity, 128), 0) == lax.broadcasted_iota(jnp.int32, (capacity, 128), 1)

        def gated(src, carry):
            gate = jnp.sum(jnp.where(one, rows_gates[area * n + src, 0:1], 0.0), axis=1, keepdims=True)
            part = pl.ds(pl.multiple_of((area * n + src) * capacity, 16), capacity)
            rows_grad[part] = (gate * rows_grad[part].astype(F32)).astype(BF16)
            return carry

        lax.fori_loop(0, n, gated, 0)

    def clear(sums, rows):
        def one(index, carry):
            part = pl.ds(pl.multiple_of(index * ROWS, ROWS), ROWS)
            for total in sums:
                total[part] = jnp.zeros((ROWS, width), F32)
            return carry

        lax.fori_loop(0, rows // ROWS, one, 0)

    def work(trained, sums, first_row, rows, nearest, farthest):
        arrays = (0, 1) if trained else (2, 3)
        every = (all_a, all_b) if trained else (all_c, all_d)
        own = (own_a, own_b) if trained else (own_c, own_d)

        def one(step, carry):
            distance, side = step // 2, lax.rem(step, 2)
            index = jnp.where(side == 0, planes.me - distance, planes.me + distance)
            real = jnp.logical_and(jnp.logical_and(index >= 0, index < n_dp), jnp.logical_or(side == 0, distance > 0))

            @pl.when(jnp.logical_and(side == 0, distance >= (2 if trained else 3)))
            def _():
                stream.pass_on(arrays, distance)

            @pl.when(real)
            def _():
                near = [pltpu.make_async_copy(own[i], (weight_a, weight_b)[i], load.at[i]) for i in range(2)]
                far = [pltpu.make_async_copy(every[i].at[index], (weight_a, weight_b)[i], load.at[i]) for i in range(2)]

                @pl.when(distance == 0)
                def _():
                    for copy in near:
                        copy.start()

                @pl.when(distance > 0)
                def _():
                    for copy in far:
                        copy.start()

                for copy in near:
                    copy.wait()

                def chunk(number, carry):
                    part = pl.ds(pl.multiple_of(number * ROWS, ROWS), ROWS)
                    here = pl.ds(pl.multiple_of(first_row + number * ROWS, ROWS), ROWS)
                    active, slope = gelu_parts(dot(rows_in[here], weight_a[...]))
                    active = active.astype(BF16)
                    back = (dot_t(rows_grad[here], weight_b[...]) * slope).astype(BF16)
                    if trained:
                        packed[part, :hidden] = active
                        packed_grad[part, :hidden] = back
                    sums[0][part] += dot(active, weight_b[...])
                    sums[1][part] += dot_t(back, weight_a[...])
                    return carry

                lax.fori_loop(0, rows // ROWS, chunk, 0)
                if trained:
                    stores = [
                        pltpu.make_async_copy(stage, whole.at[index], load.at[2 + i])
                        for i, (stage, whole) in enumerate(((grad_a, first_grad), (grad_b, second_grad)))
                    ]
                    for total in (span, 2 * span):

                        @pl.when(planes.hosts == (total > span))
                        def _():
                            every_row = pl.ds(0, total)
                            for col in range(0, width, WIDE):
                                cut = pl.ds(col, WIDE)
                                grad_a[cut] = t_dot(rows_in[every_row, cut], packed_grad[every_row, :hidden]).astype(BF16)
                            for col in range(0, hidden, WIDE):
                                cut = pl.ds(col, WIDE)
                                grad_b[cut] = t_dot(packed[every_row, cut], rows_grad[every_row]).astype(BF16)

                    for copy in stores:
                        copy.start()
                    for copy in stores:
                        copy.wait()

            return carry

        lax.fori_loop(2 * nearest, 2 * farthest + 2, one, 0)

    def turn(sums, first_row, base, rows):
        def one(number, carry):
            part = pl.ds(pl.multiple_of(base + number * ROWS, ROWS), ROWS)
            here = pl.ds(pl.multiple_of(first_row + number * ROWS, ROWS), ROWS)
            rows_in[here] = sums[0][part].astype(BF16)
            rows_grad[here] = sums[1][part].astype(BF16)
            return carry

        lax.fori_loop(0, rows // ROWS, one, 0)

    def back_copies(kind, guest):
        area = 2 if kind else int(guest)
        plane = planes.guest if guest else planes.me
        for which, (source, target) in enumerate(((rows_in, got), (rows_grad, got_grad))):
            into = target.at[pl.ds(pl.multiple_of((me * 2 + kind) * capacity, 16), capacity)]
            for step in range(n):
                to = lax.rem(me + step, n)
                piece = source.at[pl.ds(pl.multiple_of((area * n + to) * capacity, 16), capacity)]
                if step or guest:
                    yield True, remote(
                        piece, into, back_send.at[which, area, step], back_recv.at[which, kind, me], {"sp": to, "dp": plane}
                    )
                else:
                    yield True, pltpu.make_async_copy(piece, into, back_local.at[which, kind])

    def hops(act):
        for up in (True, False):
            for array, (whole, hop) in enumerate(((first_grad, hop_a), (second_grad, hop_b))):

                @pl.when(planes.me == (1 if up else n_dp - 2))
                def _():
                    act(
                        remote(
                            whole.at[n_dp - 1 if up else 0], hop.at[int(up)], hop_send.at[int(up), array],
                            hop_recv.at[int(up), array], {"dp": planes.me + (1 if up else -1)},
                        )
                    )

    train_sums, frozen_sums = (out_sum, in_sum), (out_other, in_other)
    train_rows = jnp.where(planes.hosts, 2 * span, span)
    clear(frozen_sums, span)

    @pl.when(planes.inner)
    def _():
        clear(train_sums, train_rows)
        take(0)

        @pl.when(planes.hosts)
        def _():
            take(1)

        work(True, train_sums, 0, train_rows, 0, 0)
        stream.pass_on((0, 1), 1)
        work(True, train_sums, 0, train_rows, 1, 1)

    take(2)
    work(False, frozen_sums, 2 * span, span, 0, 1)
    stream.pass_on((2, 3), 2)
    work(False, frozen_sums, 2 * span, span, 2, n_dp - 1)
    turn(frozen_sums, 2 * span, 0, span)
    each(back_copies(1, False), start)

    @pl.when(planes.inner)
    def _():
        work(True, train_sums, 0, train_rows, 2, n_dp - 1)

        @pl.when(planes.hosts)
        def _():
            turn(train_sums, span, span, span)
            each(back_copies(0, True), start)

        turn(train_sums, 0, 0, span)
        each(back_copies(0, False), start)
        hops(start)

    each(back_copies(1, False), end)

    @pl.when(planes.inner)
    def _():
        each(back_copies(0, False), end)

        @pl.when(planes.hosts)
        def _():
            each(back_copies(0, True), end)

    for kind in range(2):
        for which, buffer in enumerate((got, got_grad)):
            for src in range(n):
                piece = buffer.at[pl.ds((src * 2 + kind) * capacity, capacity)]
                comes = jnp.logical_or(src != me, planes.outer) if kind == 0 else src != me
                pl.when(comes)(pltpu.make_async_copy(piece, piece, back_recv.at[which, kind, src]).wait)
    stream.finish()
    hops(end)
    for up in (True, False):
        for array, hop in enumerate((hop_a, hop_b)):

            @pl.when(planes.me == (2 if up else n_dp - 3))
            def _():
                pltpu.make_async_copy(hop.at[int(up)], hop.at[int(up)], hop_recv.at[int(up), array]).wait()


ANY = pl.BlockSpec(memory_space=pl.ANY)


def layer(lay, capacity, n_dp, tokens, vectors, w_qkv, w_out, w_router, routes, cotangent, weights):
    count, width = tokens.shape
    n = lay.n
    owners = len(lay.owners())
    span = n * capacity
    shape = jax.ShapeDtypeStruct
    hidden = weights[0].shape[1]
    every = [shape((n_dp, *weight.shape), BF16) for weight in weights]
    return pl.pallas_call(
        functools.partial(layer_kernel, lay, capacity, n_dp),
        out_shape=(
            shape((count, width), BF16),
            shape((3, UNIT, WIDE), BF16),
            shape((UNIT, WIDE), F32),
            shape((UNIT, WIDE), F32),
            shape((count, width), BF16),
            shape((count, width), F32),
            shape((count, width), BF16),
            shape((count, 128), F32),
            shape((2 * span, width), BF16),
            shape((2 * span, width), BF16),
            every[0],
            every[1],
            *every,
            shape((2, *weights[0].shape), BF16),
            shape((2, *weights[1].shape), BF16),
        ),
        in_specs=[VMEM] * 8 + [ANY] * 4,
        out_specs=[VMEM] * 8 + [ANY] * 10,
        scratch_shapes=[
            pltpu.VMEM((UNIT, WIDE), BF16),
            pltpu.VMEM((2 * span, width), BF16),
            pltpu.VMEM((2 * span, width), BF16),
            pltpu.VMEM((3 * span, width), BF16),
            pltpu.VMEM((3 * span, width), BF16),
            pltpu.VMEM((width, hidden), BF16),
            pltpu.VMEM((hidden, width), BF16),
            pltpu.VMEM((2 * span, width), F32),
            pltpu.VMEM((2 * span, width), F32),
            pltpu.VMEM((span, width), F32),
            pltpu.VMEM((span, width), F32),
            pltpu.VMEM((width, hidden), BF16),
            pltpu.VMEM((hidden, width), BF16),
            pltpu.VMEM((2 * n, 8, 128), F32),
            pltpu.VMEM((3 * n, 8, 128), F32),
            DMA((9 * owners,)),
            DMA((3,)),
            DMA,
            DMA,
            DMA,
            DMA((2, 4, n_dp)),
            DMA((4, n_dp)),
            DMA((4,)),
            DMA((3, 2, n)),
            DMA((3, 3, n)),
            DMA((3, 2)),
            DMA((2, 3, n)),
            DMA((2, 2, n)),
            DMA((2, 2)),
            DMA((2, 2)),
            DMA((2, 2)),
        ],
        compiler_params=pltpu.CompilerParams(collective_id=0, has_side_effects=True, vmem_limit_bytes=LIMIT),
        cost_estimate=pl.CostEstimate(flops=50 * 10**9, bytes_accessed=100 * 2**20, transcendentals=10**7),
        name="layer",
    )(
        tokens, vectors, w_qkv, w_out, w_router, routes, routes.T, cotangent, *weights
    )


class Sum:
    def __init__(self, n_sp, n_dp, pieces, quantum, needed):
        self.n_sp, self.n_dp = n_sp, n_dp
        self.bits = n_sp.bit_length() - 1
        unit = math.lcm(16 * n_sp * n_dp, quantum)
        units = -(-needed // unit)
        pieces = min(pieces, units)
        sizes = [units // pieces + (p < units % pieces) for p in range(pieces)]
        self.pieces = [(unit * sum(sizes[:p]), unit * size) for p, size in enumerate(sizes)]
        self.rows = unit * units
        self.steps = 2 * self.bits + 2

    def order(self, piece):
        later = list(range(1, self.bits))
        return [0] + (later[::-1] if piece % 2 else later)

    def landing(self):
        places, start = [], 0
        for _, rows in self.pieces:
            places.append([])
            for step in range(self.bits + 1):
                rows = rows // 2 if step < self.bits else rows
                places[-1].append((start, rows))
                start += rows
        return places, start

    def bind(self, mine, landed, whole, send, recv):
        self.mine, self.landed, self.whole, self.send, self.recv = mine, landed, whole, send, recv
        self.me, self.plane = lax.axis_index("sp"), lax.axis_index("dp")
        self.places, _ = self.landing()
        self.starts = [[start] for start, _ in self.pieces]
        for piece, (_, rows) in enumerate(self.pieces):
            for bit in self.order(piece):
                rows //= 2
                value = (self.me // (1 << bit)) % 2
                self.starts[piece].append(self.starts[piece][-1] + value * rows)

    def partner(self, bit):
        value = (self.me // (1 << bit)) % 2
        return self.me + (1 - 2 * value) * (1 << bit)

    def peers(self):
        found = [(True, {"sp": self.partner(bit)}) for bit in range(self.bits)]
        return found + [(True, {"dp": lax.rem(self.plane + step, self.n_dp)}) for step in range(1, self.n_dp)]

    def cut(self, start, rows):
        return pl.ds(pl.multiple_of(start, 16), rows)

    def copies(self, piece, step):
        bits = self.bits
        rows = self.pieces[piece][1]
        if step < bits or step > bits + 1:
            level = step if step < bits else 2 * bits + 1 - step
            bit = self.order(piece)[level]
            half = rows >> (level + 1)
            held, kept = self.starts[piece][level], self.starts[piece][level + 1]
            if step < bits:
                start, _ = self.places[piece][step]
                source = self.mine.at[self.cut(2 * held + half - kept, half)]
                target = self.landed.at[pl.ds(start, half)]
            else:
                source = target = self.whole.at[self.cut(kept, half)]
            yield remote(source, target, self.send.at[piece, step, 0], self.recv.at[piece, step, 0], self.partner(bit))
            return
        block = (rows >> bits) // self.n_dp
        base = self.starts[piece][bits]
        start, _ = self.places[piece][bits]
        for far in range(1, self.n_dp):
            other = lax.rem(self.plane + far, self.n_dp)
            if step == bits:
                source = self.mine.at[self.cut(base + other * block, block)]
                target = self.landed.at[self.cut(start + self.plane * block, block)]
            else:
                source = target = self.whole.at[self.cut(base + self.plane * block, block)]
            yield remote(source, target, self.send.at[piece, step, far], self.recv.at[piece, step, far], {"dp": other})

    def start(self, piece, step):
        for copy in self.copies(piece, step):
            copy.start()

    def add(self, piece, step):
        for copy in self.copies(piece, step):
            copy.wait()
        bits, rows = self.bits, self.pieces[piece][1]
        if step > bits:
            return
        start, _ = self.places[piece][step]
        if step < bits:
            size, kept = rows >> (step + 1), self.starts[piece][step + 1]
            for first, count in blocks(size):

                def one(number, carry):
                    part = self.cut(kept + first + number * count[0], count[0])
                    here = self.cut(start + first + number * count[0], count[0])
                    self.mine[part] = (self.mine[part].astype(F32) + self.landed[here].astype(F32)).astype(BF16)
                    return carry

                lax.fori_loop(0, count[1], one, 0)
            return
        block = (rows >> bits) // self.n_dp
        own = self.cut(self.starts[piece][bits] + self.plane * block, block)
        total = self.mine[own].astype(F32)
        for far in range(1, self.n_dp):
            other = lax.rem(self.plane + far, self.n_dp)
            total = total + self.landed[self.cut(start + other * block, block)].astype(F32)
        self.whole[own] = total.astype(BF16)


def blocks(rows, size=512):
    found = []
    if rows >= size:
        found.append((0, (size, rows // size)))
    if rows % size:
        found.append((rows - rows % size, (rows % size, 1)))
    return found


def run_sum(total, ready=lambda piece: None, done=lambda piece: None):
    count = len(total.pieces)
    for tick in range(total.steps + count):
        for piece in range(count):
            step = tick - piece
            if step > 0 and step <= total.steps:
                total.add(piece, step - 1)
                if step == total.steps:
                    done(piece)
            if step == 0:
                ready(piece)
            if 0 <= step < total.steps:
                total.start(piece, step)


class Gather:
    def __init__(self, n, own, hop, below, above, theirs, sums, stage, send, recv, load):
        self.n, self.own, self.hop, self.below, self.above, self.stage = n, own, hop, below, above, stage
        self.theirs, self.sums, self.send, self.recv, self.load = theirs, sums, send, recv, load
        self.me = lax.axis_index("dp")
        self.inner = jnp.logical_and(self.me >= 1, self.me <= n - 2)

    def copy(self, array, index, up, source):
        target = (self.below if up else self.above)[array].at[index]
        other = self.me + 1 if up else self.me - 1
        return remote(
            source, target, self.send.at[int(up), array, index], self.recv.at[int(up), array, index], {"dp": other}
        )

    def fetch(self, source, buffer, number):
        moved = pltpu.make_async_copy(source, buffer, self.load.at[number])
        moved.start()
        return moved

    def wanted(self, index, up):
        return jnp.logical_and(self.inner, index > self.me if up else index < self.me)

    def begins(self, up):
        return self.me == 1 if up else self.me == self.n - 2

    def hopped(self, index, up):
        if index not in (0, self.n - 1):
            return False
        return self.me == 2 if up else self.me == self.n - 3

    def begin(self, array, index, up):
        @pl.when(jnp.logical_and(self.wanted(index, up), self.begins(up)))
        def _():
            self.copy(array, index, up, self.own[array].at[index]).start()

    def came(self, array, index, up):
        buffer = (self.below if up else self.above)[array].at[index]
        pltpu.make_async_copy(buffer, buffer, self.recv.at[int(up), array, index]).wait()
        return buffer

    def pass_on(self, array, index, up):
        @pl.when(jnp.logical_and(self.wanted(index, up), jnp.logical_not(self.begins(up))))
        def _():
            total, theirs = self.sums[array].at[int(up)], self.theirs[array]
            here = self.fetch(self.own[array].at[index], total, 0)
            hopped = self.hopped(index, up)

            @pl.when(hopped)
            def _():
                self.fetch(self.hop[array].at[int(up)], theirs, 1).wait()

            @pl.when(jnp.logical_not(hopped))
            def _():
                self.fetch(self.came(array, index, up), theirs, 1).wait()

            here.wait()
            total[...] = (total[...].astype(F32) + theirs[...].astype(F32)).astype(BF16)
            self.copy(array, index, up, total).start()

    def finish(self, array, index, up):
        waits = self.wanted(index, up)
        if index in (0, self.n - 1):
            waits = jnp.logical_and(waits, jnp.logical_not(self.begins(up)))

        @pl.when(waits)
        def _():
            self.copy(array, index, up, self.sums[array].at[int(up)]).wait_send()

    def total(self, array, out):
        theirs = self.theirs[array]

        @pl.when(self.inner)
        def _():
            self.fetch(self.own[array].at[self.me], theirs, 0).wait()

        @pl.when(jnp.logical_not(self.inner))
        def _():
            theirs[...] = jnp.zeros_like(theirs)

        sides = ((True, self.me >= 2), (False, self.me <= self.n - 3))
        for up, comes in sides:

            @pl.when(comes)
            def _():
                self.fetch(self.came(array, self.me, up), self.sums[array].at[int(up)], 1).wait()

        size = out.shape[0] // 6
        lanes = pl.ds(0, out.shape[1])
        stores = []
        for number in range(6):
            part = pl.ds(number * size, size)
            stage = self.stage.at[number % 2, pl.ds(0, size), lanes]
            if number >= 2:
                stores[number - 2].wait()
            stage[...] = theirs[part].astype(F32)
            for up, comes in sides:

                @pl.when(comes)
                def _():
                    stage[...] += self.sums[array][int(up), part].astype(F32)

            stores.append(pltpu.make_async_copy(stage, out.at[part], self.load.at[3 + number % 2]))
            stores[number].start()
        for store in stores[-2:]:
            store.wait()


def gather_scratch(n, first, second):
    shapes = [first.shape[1:], second.shape[1:]]
    return [
        *(pltpu.VMEM(shape, BF16) for shape in shapes),
        *(pltpu.VMEM((2, *shape), BF16) for shape in shapes),
        pltpu.VMEM((2, 128, max(map(max, shapes))), F32),
        DMA((2, 2, n)),
        DMA((2, 2, n)),
        DMA((5,)),
    ]


def back_kernel(
    lay, capacity, replicated,
    got, got_grad, middle, second_norm, gates, home_out, w_out, vectors, w_router, routes, cotangent,
    unit, attended, log_total, first_norm, tokens, w_qkv, first_own, second_own, hop_a, hop_b,
    block_out, tokens_grad, summed, first_total, second_total, below_a, below_b, above_a, above_b,
    grad_attended, grad_out, deltas, query_sum, staged, home, send, recv, out_send, home_recv, local,
    theirs_a, theirs_b, sums_a, sums_b, stage, pass_send, pass_recv, load,
    grads, landed, sum_send, sum_recv,
):
    n_dp = first_own.shape[0]
    gather = Gather(
        n_dp, (first_own, second_own), (hop_a, hop_b), (below_a, below_b), (above_a, above_b), (theirs_a, theirs_b),
        (sums_a, sums_b), stage, pass_send, pass_recv, load,
    )
    gain_one, gain_two = vectors.at[0:1], vectors.at[2:3]
    replicated.bind(grads, landed, summed, sum_send, sum_recv)
    me = lax.axis_index("sp")
    is_short, seq, first_pair = lay.role(me)
    everywhere = [(True, {"dp": lax.rem(gather.me + step, n_dp)}) for step in range(1, n_dp)]
    meet(plane_peers(lay.n) + everywhere)
    kept = pltpu.make_async_copy(attended, deltas, load.at[2])
    kept.start()
    inside = [(up, index) for index in range(1, n_dp - 1) for up in (True, False)]
    ends = [(True, n_dp - 1), (False, 0)]
    for array in range(2):
        for up, index in inside:
            gather.begin(array, index, up)
    place, matches = slot_columns(lay, capacity, routes[...])
    slots = lax.broadcasted_iota(jnp.int32, (tokens.shape[0], got.shape[0]), 1)
    chosen = [hot(slots == place[c]) for c in range(2)]
    upstream = cotangent[...].astype(F32)
    gate = [gates[:, c : c + 1] for c in range(2)]
    total = middle[...]
    grad_gate = []
    for c in range(2):
        produced = dot(chosen[c], got[...])
        total = total + gate[c] * produced
        grad_gate.append(jnp.sum(upstream * produced, axis=1, keepdims=True))
    block_out[...] = total.astype(BF16)
    mean_grad = gate[0] * grad_gate[0] + gate[1] * grad_gate[1]
    grad_logits = sum(matches[c] * (gate[c] * (grad_gate[c] - mean_grad)) for c in range(2))
    high = grad_logits.astype(BF16)
    low = (grad_logits - high.astype(F32)).astype(BF16)
    router_grad = t_dot(second_norm[...], high) + t_dot(second_norm[...], low)
    grad_second = dot_t(high, w_router[...]) + dot_t(low, w_router[...])
    grad_second = grad_second + dot(chosen[0] + chosen[1], got_grad[...])
    hat, scale = normed(middle[...])
    gain_two_grad = jnp.sum(grad_second * hat, axis=0, keepdims=True)
    shift_two_grad = jnp.sum(grad_second, axis=0, keepdims=True)
    grad = upstream + norm_back(grad_second, gain_two[...], hat, scale)
    tokens_grad[...] = grad
    branch = grad.astype(BF16)
    grad_attended[...] = dot_t(branch, w_out[...]).astype(BF16)
    out_proj = t_dot(home_out[...], branch)
    width = w_out.shape[0]

    def put(column, value):
        for lane in range(0, value.shape[1], WIDE):
            grads[pl.ds((column + lane) // WIDE * width, width)] = value[:, lane : lane + WIDE].astype(BF16)

    put(0, out_proj)
    started = to_owners(
        lay,
        me,
        lambda pair: pair * WIDE,
        lambda number: number,
        grad_attended,
        lambda start, rows: grad_out.at[pl.ds(pl.multiple_of(start, 16), rows)],
        send,
        recv,
        local,
        range(PAIRS),
    )
    for array in range(2):
        for up, index in ends:
            gather.pass_on(array, index, up)
    query_sum[...] = jnp.zeros_like(query_sum)
    keep = lanes_first()
    lower = causal(BLOCK)
    wait_unit(lay, is_short, grad_out, recv)
    kept.wait()

    def make_delta(index, carry):
        part = pl.ds(pl.multiple_of(index * BLOCK, BLOCK), BLOCK)
        first, second = halves(grad_out[part].astype(F32) * deltas[part])
        deltas[part] = jnp.where(
            keep, jnp.sum(first, axis=1, keepdims=True), jnp.sum(second, axis=1, keepdims=True)
        )
        return carry

    lax.fori_loop(0, lay.tasks(is_short), make_delta, 0)
    per = jnp.where(is_short, LEN_A // BLOCK, LEN_B // BLOCK)

    def task(index, carry):
        start, block = lay.task(is_short, index)
        base = pl.multiple_of(start + block * BLOCK, BLOCK)
        keys = unit[1, pl.ds(base, BLOCK)]
        values = unit[2, pl.ds(base, BLOCK)]
        key_both = jnp.concatenate(halves(keys), axis=0)

        def visit(place, state, diagonal):
            part = pl.ds(place, BLOCK)
            grad_key, grad_value = state
            queries = halves(unit[0, part])
            outs = halves(grad_out[part])
            weights, grads = [], []
            for which, (query, out) in enumerate(zip(queries, outs)):
                column = which * HEAD_DIM
                scores = dot_t(query, keys)
                if diagonal:
                    scores = jnp.where(lower, scores, NEGATIVE)
                weight = jnp.exp(scores - log_total[part, column : column + 1])
                grad = weight * (dot_t(out, values) - deltas[part, column : column + 1])
                weights.append(weight.astype(BF16))
                grads.append(grad.astype(BF16))
            grad_value = grad_value + t_dot(jnp.concatenate(weights, axis=0), jnp.concatenate(outs, axis=0))
            grad_key = grad_key + t_dot(jnp.concatenate(grads, axis=0), jnp.concatenate(queries, axis=0))
            query_sum[part] += dot(jnp.concatenate(grads, axis=1), key_both)
            return grad_key, grad_value

        zero = jnp.zeros((BLOCK, WIDE), F32)
        state = visit(base, (zero, zero), True)
        grad_key, grad_value = lax.fori_loop(
            block + 1, per, lambda i, state: visit(pl.multiple_of(start + i * BLOCK, BLOCK), state, False), state
        )
        part = pl.ds(base, BLOCK)
        staged[0, part] = (query_sum[part] * HEAD_DIM**-0.5).astype(BF16)
        staged[1, part] = grad_key.astype(BF16)
        staged[2, part] = grad_value.astype(BF16)
        for kind in range(3):
            send_home(
                lay, me, is_short, seq, first_pair, base, block, start, staged.at[kind], home, kind * PAIRS * WIDE,
                out_send.at[kind], home_recv.at[kind], local,
            )
        return carry

    lax.fori_loop(0, lay.tasks(is_short), task, 0)
    for kind in range(3):
        wait_home(lay, is_short, staged.at[kind], home_recv.at[kind], 1, False)
    grad_first = dot_t(home[...], w_qkv[...])
    hat, scale = normed(tokens[...].astype(F32))
    gain_one_grad = jnp.sum(grad_first * hat, axis=0, keepdims=True)
    shift_one_grad = jnp.sum(grad_first, axis=0, keepdims=True)
    tokens_grad[...] += norm_back(grad_first, gain_one[...], hat, scale)
    parts = (gain_one_grad, shift_one_grad, gain_two_grad, shift_two_grad)
    row = lax.broadcasted_iota(jnp.int32, (8, width), 0)
    stack = sum(jnp.where(row == i, part, 0.0) for i, part in enumerate(parts)).astype(BF16)
    lane = lax.broadcasted_iota(jnp.int32, (8, WIDE), 1)
    spot = hot(lane == HEAD_DIM + lax.broadcasted_iota(jnp.int32, (8, WIDE), 0))
    grads[pl.ds(width // WIDE * width, width)] = (router_grad + t_dot(stack, spot)).astype(BF16)
    first = 8
    last = first + 3 * PAIRS
    for spare in [7, *range(last, replicated.rows // width)]:
        grads[pl.ds(spare * width, width)] = jnp.zeros((width, WIDE), BF16)

    def ready(piece):
        start, rows = replicated.pieces[piece]
        for column in range(start // width, (start + rows) // width, 2):
            if first <= column < last:
                lanes = pl.ds((column - first) * WIDE, 2 * WIDE)
                put(column * WIDE, t_dot(first_norm[...], home[:, lanes]))

    run_sum(replicated, ready)
    for array, out in enumerate((first_total, second_total)):
        for up, index in inside:
            gather.pass_on(array, index, up)
        for up, index in inside + ends:
            gather.finish(array, index, up)
        gather.total(array, out)
    finish_sends(me, started)
    for kind in range(3):
        wait_home(lay, is_short, staged.at[kind], out_send.at[kind], 1, True)


def backward(lay, capacity, values):
    count, width = values[2].shape
    owners = len(lay.owners())
    shape = jax.ShapeDtypeStruct
    slices = values[-4:-2]
    replicated = Sum(lay.n, slices[0].shape[0], 6, 2 * width, 26 * width)
    return pl.pallas_call(
        functools.partial(back_kernel, lay, capacity, replicated),
        out_shape=(
            shape((count, width), BF16), shape((count, width), F32), shape((replicated.rows, WIDE), BF16),
            *(shape(g.shape[1:], F32) for g in slices), *(shape(g.shape, BF16) for g in slices * 2),
        ),
        in_specs=[VMEM] * 12 + [ANY] + [VMEM] * 4 + [ANY] * 4,
        out_specs=[VMEM] * 3 + [ANY] * 6,
        scratch_shapes=[
            pltpu.VMEM((count, width), BF16),
            pltpu.VMEM((UNIT, WIDE), BF16),
            pltpu.VMEM((UNIT, WIDE), F32),
            pltpu.VMEM((UNIT, WIDE), F32),
            pltpu.VMEM((3, UNIT, WIDE), BF16),
            pltpu.VMEM((count, 3 * width), BF16),
            DMA((owners,)),
            DMA,
            DMA((3,)),
            DMA((3,)),
            DMA,
            *gather_scratch(slices[0].shape[0], *slices),
            pltpu.VMEM((replicated.rows, WIDE), BF16),
            pltpu.VMEM((replicated.landing()[1], WIDE), BF16),
            DMA((len(replicated.pieces), replicated.steps, slices[0].shape[0])),
            DMA((len(replicated.pieces), replicated.steps, slices[0].shape[0])),
        ],
        compiler_params=pltpu.CompilerParams(collective_id=1, has_side_effects=True, vmem_limit_bytes=LIMIT),
        cost_estimate=pl.CostEstimate(flops=16 * 10**9, bytes_accessed=60 * 2**20, transcendentals=5 * 10**6),
        name="backward",
    )(*values)


def shards(
    tokens, ln1_gain, ln1_shift, w_qkv, w_out, ln2_gain, ln2_shift, w_router,
    train_w1, train_w2, frozen_w1, frozen_w2, routes, cotangent,
):
    lay = Layout(lax.axis_size("sp"))
    n_dp = lax.axis_size("dp")
    tokens, routes, cotangent = tokens[0], routes[0], cotangent[0]
    count, width = tokens.shape
    capacity = 2 * count // lay.n
    experts = w_router.shape[1]
    router_wide = jnp.pad(w_router, ((0, 0), (0, 128 - experts)))
    vectors = jnp.stack([ln1_gain, ln1_shift, ln2_gain, ln2_shift])
    weights = [weight[0] for weight in (train_w1, train_w2, frozen_w1, frozen_w2)]
    (
        first_norm, unit, attended, log_total, home, middle, second, gates, got, got_grad, first_grad, second_grad,
        _, _, _, _, hop_a, hop_b,
    ) = layer(lay, capacity, n_dp, tokens, vectors, w_qkv, w_out, router_wide, routes, cotangent, weights)
    block_out, tokens_grad, summed, first_total, second_total, *_ = backward(
        lay, capacity,
        (
            got, got_grad, middle, second, gates, home, w_out, vectors, router_wide, routes, cotangent,
            unit, attended, log_total, first_norm, tokens, w_qkv, first_grad, second_grad, hop_a, hop_b,
        ),
    )

    def columns(first, count):
        part = summed[first * width : (first + count) * width].reshape(count, width, WIDE)
        return jnp.transpose(part, (1, 0, 2)).reshape(width, count * WIDE).astype(F32)

    mixed = columns(width // WIDE, 1)
    return (
        block_out[None],
        tokens_grad[None],
        mixed[:, HEAD_DIM],
        mixed[:, HEAD_DIM + 1],
        columns(8, 3 * PAIRS),
        columns(0, PAIRS),
        mixed[:, HEAD_DIM + 2],
        mixed[:, HEAD_DIM + 3],
        mixed[:, :experts],
        first_total[None],
        second_total[None],
    )


def solution(mesh):
    in_specs = (
        P("dp", "sp", None), P(), P(), P(), P(), P(), P(), P(),
        P("sp", None, "dp"), P("sp", "dp", None), P("sp", None, "dp"), P("sp", "dp", None),
        P("dp", "sp", None), P("dp", "sp", None),
    )
    out_specs = (
        P("dp", "sp", None), P("dp", "sp", None), P(), P(), P(), P(), P(), P(), P(),
        P("sp", None, "dp"), P("sp", "dp", None),
    )
    return jax.shard_map(shards, mesh=mesh, in_specs=in_specs, out_specs=out_specs, check_vma=False)
```

```python
import functools
import math

import jax
import jax.numpy as jnp
from jax import lax
from jax.experimental import pallas as pl
from jax.experimental.pallas import tpu as pltpu
from jax.sharding import PartitionSpec as P

HEADS = 12
HEAD_DIM = 64
LEN_A = 1024
LEN_B = 2048
PAIRS = HEADS // 2
WIDE = 2 * HEAD_DIM
UNIT = 3 * LEN_A
BLOCK = 256
EPSILON = 1e-05
NEGATIVE = -1e30
MESH = pl.DeviceIdType.MESH
DMA = pltpu.SemaphoreType.DMA
F32 = jnp.float32
BF16 = jnp.bfloat16
VMEM = pl.BlockSpec(memory_space=pltpu.VMEM)


def dot(a, b):
    return jnp.dot(a, b, preferred_element_type=F32)


def dot_t(a, b):
    return lax.dot_general(a, b, (((1,), (1,)), ((), ())), preferred_element_type=F32)


def t_dot(a, b):
    return lax.dot_general(a, b, (((0,), (0,)), ((), ())), preferred_element_type=F32)


def normed(value):
    centre = jnp.mean(value, axis=-1, keepdims=True)
    centred = value - centre
    spread = jnp.mean(centred * centred, axis=-1, keepdims=True)
    scale = lax.rsqrt(spread + EPSILON)
    return centred * scale, scale


def norm_back(grad, gain, hat, scale):
    scaled = grad * gain
    first = jnp.mean(scaled, axis=-1, keepdims=True)
    second = jnp.mean(scaled * hat, axis=-1, keepdims=True)
    return (scaled - first - hat * second) * scale


class Layout:
    def __init__(self, n_sp):
        self.n = n_sp
        self.sequences = n_sp // 8
        self.short = LEN_A // n_sp
        self.long = LEN_B // n_sp
        self.split = self.sequences * self.short

    def owners(self):
        found = []
        for seq in range(self.sequences):
            for pair in range(PAIRS):
                number = seq * PAIRS + pair
                found.append((number + number // 3 + 1, True, self.split + seq * self.long, self.long, pair, 0))
                found.append((4 * (seq * 2 + pair // 3), False, seq * self.short, self.short, pair, (pair % 3) * LEN_A))
        return found

    def role(self, me):
        is_short = lax.rem(me, 4) == 0
        number = me - me // 4 - 1
        group = me // 4
        seq = jnp.where(is_short, group // 2, number // PAIRS)
        pair = jnp.where(is_short, 3 * lax.rem(group, 2), lax.rem(number, PAIRS))
        return is_short, seq, pair

    def task(self, is_short, index):
        per = LEN_A // BLOCK
        start = jnp.where(is_short, (index // per) * LEN_A, 0)
        block = jnp.where(is_short, lax.rem(index, per), index)
        return pl.multiple_of(start, BLOCK), block

    def tasks(self, is_short):
        return jnp.where(is_short, 3 * LEN_A // BLOCK, LEN_B // BLOCK)


def meet(peers):
    barrier = pltpu.get_barrier_semaphore()
    for wanted, device in peers:

        @pl.when(wanted)
        def _():
            pl.semaphore_signal(barrier, inc=1, device_id=device, device_id_type=MESH)

    pl.semaphore_wait(barrier, sum(jnp.asarray(wanted, jnp.int32) for wanted, _ in peers))


def plane_peers(n):
    me = lax.axis_index("sp")
    return [(True, {"sp": lax.rem(me + step, n)}) for step in range(1, n)]


def remote(source, target, send_sem, recv_sem, device):
    device = device if isinstance(device, dict) else {"sp": device}
    return pltpu.make_async_remote_copy(
        src_ref=source, dst_ref=target, send_sem=send_sem, recv_sem=recv_sem, device_id=device, device_id_type=MESH
    )


def lanes_first():
    return lax.broadcasted_iota(jnp.int32, (1, WIDE), 1) < HEAD_DIM


def halves(value):
    keep = lanes_first()
    zero = jnp.zeros_like(value)
    return jnp.where(keep, value, zero), jnp.where(keep, zero, value)


def causal(rows):
    return lax.broadcasted_iota(jnp.int32, (rows, rows), 0) >= lax.broadcasted_iota(jnp.int32, (rows, rows), 1)


def to_owners(lay, me, cols, slot, source, target, send_sems, recv_sem, local_sem, wanted):
    started = []
    for number, (owner, is_long, start, rows, pair, unit) in enumerate(lay.owners()):
        if pair not in wanted:
            continue
        piece = source.at[pl.ds(start, rows), pl.ds(cols(pair), WIDE)]
        place = target(unit + me * rows, rows)
        far = remote(piece, place, send_sems.at[slot(number)], recv_sem, owner)
        near = pltpu.make_async_copy(piece, place, local_sem)

        @pl.when(me != owner)
        def _():
            far.start()

        @pl.when(me == owner)
        def _():
            near.start()
            near.wait()

        started.append((owner, far))
    return started


def finish_sends(me, started):
    for owner, copy in started:

        @pl.when(me != owner)
        def _():
            copy.wait_send()


def wait_unit(lay, is_short, buffer, sem):
    for short, rows in ((True, 3 * (lay.n - 1) * lay.short), (False, (lay.n - 1) * lay.long)):

        @pl.when(is_short == short)
        def _():
            piece = buffer.at[pl.ds(0, rows)]
            pltpu.make_async_copy(piece, piece, sem).wait()


def send_home(lay, me, is_short, seq, first_pair, base, block, unit_start, source, target, base_col, send_sem, recv_sem, local_sem):
    for short, rows in ((True, lay.short), (False, lay.long)):

        @pl.when(is_short == short)
        def _():
            pair = first_pair + (unit_start // LEN_A if short else 0)
            column = pl.multiple_of(base_col + pair * WIDE, WIDE)
            first = pl.multiple_of(seq * rows + (0 if short else lay.split), 16)
            for part in range(BLOCK // rows):
                home = block * (BLOCK // rows) + part
                piece = source.at[pl.ds(pl.multiple_of(base + part * rows, 16), rows)]
                place = target.at[pl.ds(first, rows), pl.ds(column, WIDE)]

                @pl.when(home != me)
                def _():
                    remote(piece, place, send_sem, recv_sem, home).start()

                @pl.when(home == me)
                def _():
                    near = pltpu.make_async_copy(piece, place, local_sem)
                    near.start()
                    near.wait()


def wait_home(lay, is_short, scratch, sem, tensors, sent):
    for short in (True, False):
        own = 3 * lay.short if short else lay.long
        if sent:
            rows = (3 * LEN_A if short else LEN_B) - own
        else:
            rows = PAIRS * lay.sequences * (lay.short + lay.long) - own

        @pl.when(is_short == short)
        def _():
            for _ in range(tensors):
                piece = scratch.at[pl.ds(0, rows)]
                pltpu.make_async_copy(piece, piece, sem).wait()


class Planes:
    def __init__(self, n_dp):
        self.n = n_dp
        self.me = lax.axis_index("dp")
        self.outer = jnp.logical_or(self.me == 0, self.me == n_dp - 1)
        self.inner = jnp.logical_not(self.outer)
        self.inward = jnp.where(self.me == 0, 1, n_dp - 2)
        self.hosts = jnp.logical_or(self.me == 1, self.me == n_dp - 2)
        self.guest = jnp.where(self.me == 1, 0, n_dp - 1)

    def peers(self, n_sp):
        me = lax.axis_index("sp")
        found = plane_peers(n_sp)
        for sp in range(n_sp):
            found.append((self.outer, {"sp": sp, "dp": self.inward}))
            found.append((self.hosts, {"sp": sp, "dp": self.guest}))
        far = jnp.logical_and(self.inner, self.me + 1 < self.n - 1)
        found.append((far, {"sp": me, "dp": self.me + 1}))
        far = jnp.logical_and(self.inner, self.me - 1 > 0)
        found.append((far, {"sp": me, "dp": self.me - 1}))
        return found

    def takes(self, trained, up):
        other = self.me + 1 if up else self.me - 1
        low, high = (1, self.n - 2) if trained else (0, self.n - 1)
        return jnp.logical_and(other >= low, other <= high)


class Weights:
    def __init__(self, planes, own, every, send, recv):
        self.planes, self.own, self.every = planes, own, every
        self.send, self.recv = send, recv

    def copy(self, array, index, up, source):
        other = self.planes.me + 1 if up else self.planes.me - 1
        return remote(
            source, self.every[array].at[index], self.send.at[int(up), array, index], self.recv.at[array, index],
            {"dp": other},
        )

    def begin(self, arrays, wanted):
        me = self.planes.me
        for array in arrays:
            for up in (True, False):

                @pl.when(jnp.logical_and(wanted, self.planes.takes(array < 2, up)))
                def _():
                    self.copy(array, me, up, self.own[array]).start()

    def pairs(self, array, distance):
        me, n = self.planes.me, self.planes.n
        used = self.planes.inner if array < 2 else True
        for up in (True, False):
            index = me - distance if up else me + distance
            comes = jnp.logical_and(used, jnp.logical_and(index >= 0, index < n))
            yield comes, jnp.logical_and(comes, self.planes.takes(array < 2, up)), jnp.clip(index, 0, n - 1), up

    def pass_on(self, arrays, distance, of_ends=None):
        for array in arrays:
            for comes, goes, index, up in self.pairs(array, distance):
                if of_ends is not None:
                    end = jnp.logical_or(index == 0, index == self.planes.n - 1)
                    chosen = end if of_ends else jnp.logical_not(end)
                    comes, goes = jnp.logical_and(comes, chosen), jnp.logical_and(goes, chosen)

                @pl.when(comes)
                def _():
                    place = self.every[array].at[index]
                    pltpu.make_async_copy(place, place, self.recv.at[array, index]).wait()

                @pl.when(goes)
                def _():
                    self.copy(array, index, up, self.every[array].at[index]).start()

    def finish(self):
        for array in range(4):
            for distance in range(self.planes.n):
                for _, goes, index, up in self.pairs(array, distance):
                    goes = goes if distance else self.planes.takes(array < 2, up)

                    @pl.when(goes)
                    def _():
                        self.copy(array, index, up, self.every[array].at[index]).wait_send()


ROWS = 256
LIMIT = 60 * 2**20


def gelu_parts(value):
    root = 0.7978845608028654
    square = value * value
    bent = jnp.tanh(root * value * (1.0 + 0.044715 * square))
    half = 0.5 + 0.5 * bent
    slope = half + 0.5 * value * (1.0 - bent * bent) * (root + 3.0 * 0.044715 * root * square)
    return value * half, slope


def slot_rows(lay, capacity, routes_t):
    n = lay.n
    experts, count = 2 * n, routes_t.shape[1]
    index = lax.broadcasted_iota(jnp.int32, (experts, count), 0)
    matches = [(index == routes_t[c : c + 1]).astype(F32) for c in range(2)]
    earlier = (
        lax.broadcasted_iota(jnp.int32, (count, count), 0) < lax.broadcasted_iota(jnp.int32, (count, count), 1)
    ).astype(F32)
    rank = dot((matches[0] + matches[1]).astype(BF16), earlier.astype(BF16))
    place = rank + (((index % n) * 2 + index // n) * capacity).astype(F32)
    return [jnp.sum(m * place, axis=0, keepdims=True).astype(jnp.int32) for m in matches]


def slot_columns(lay, capacity, routes):
    n = lay.n
    count = routes.shape[0]
    index = lax.broadcasted_iota(jnp.int32, (count, 128), 1)
    matches = [(index == routes[:, c : c + 1]).astype(F32) for c in range(2)]
    earlier = (
        lax.broadcasted_iota(jnp.int32, (count, count), 0) > lax.broadcasted_iota(jnp.int32, (count, count), 1)
    ).astype(F32)
    rank = dot(earlier.astype(BF16), (matches[0] + matches[1]).astype(BF16))
    place = rank + (((index % n) * 2 + index // n) * capacity).astype(F32)
    return [jnp.sum(m * place, axis=1, keepdims=True).astype(jnp.int32) for m in matches], matches


def hot(condition):
    return condition.astype(F32).astype(BF16)


def layer_kernel(
    lay, capacity, n_dp,
    tokens, vectors, w_qkv, w_out, w_router, routes, routes_t, cotangent, own_a, own_b, own_c, own_d,
    first_norm, unit, attended, log_total, home, middle, second_norm, gates_out, got, got_grad, first_grad, second_grad,
    all_a, all_b, all_c, all_d, hop_a, hop_b,
    staged_out, packed, packed_grad, rows_in, rows_grad, weight_a, weight_b, out_sum, in_sum, out_other, in_other, back_out, back_grad, grad_a, grad_b,
    packed_gates, rows_gates, send, recv, out_send, home_recv, local, stream_send, stream_recv, load,
    row_send, row_recv, row_local, back_send, back_recv, back_local, hop_send, hop_recv,
):
    n = lay.n
    me = lax.axis_index("sp")
    gain_one, shift_one, gain_two, shift_two = (vectors.at[i : i + 1] for i in range(4))
    planes = Planes(n_dp)
    is_short, seq, first_pair = lay.role(me)
    meet(planes.peers(n))
    stream = Weights(
        planes, (own_a, own_b, own_c, own_d), (all_a, all_b, all_c, all_d), stream_send, stream_recv
    )
    stream.begin((0, 1), planes.outer)
    stream.begin((2, 3), planes.inner)

    hat, _ = normed(tokens[...].astype(F32))
    first_norm[...] = (hat * gain_one[...] + shift_one[...]).astype(BF16)
    started = []
    for chunk in range(9):
        kind, third = divmod(chunk, 3)
        made = dot(first_norm[...], w_qkv[:, chunk * 2 * WIDE : (chunk + 1) * 2 * WIDE]).astype(BF16)
        made = made * BF16(HEAD_DIM**-0.5) if kind == 0 else made
        area = packed.at[pl.ds(kind * tokens.shape[0], tokens.shape[0]), pl.ds(third * 2 * WIDE, 2 * WIDE)]
        area[...] = made
        count = len(lay.owners())
        started += to_owners(
            lay,
            me,
            lambda pair: (pair % 2) * WIDE,
            lambda number: chunk * count + number,
            area,
            lambda start, rows: unit.at[kind, pl.ds(pl.multiple_of(start, 16), rows)],
            send,
            recv.at[kind],
            local,
            (2 * third, 2 * third + 1),
        )
    span = n * capacity
    width, hidden = grad_a.shape
    count = tokens.shape[0]
    place = slot_rows(lay, capacity, routes_t[...])

    def dispatch_copies(which, kind):
        source, target = ((packed, rows_in), (packed_grad, rows_grad), (packed_gates, rows_gates))[which]
        plane = jnp.where(planes.outer, planes.inward, planes.me) if kind == 0 else planes.me
        area = jnp.where(planes.outer, 1, 0) if kind == 0 else 2

        def block(buffer, number):
            if which == 2:
                return buffer.at[number]
            return buffer.at[pl.ds(pl.multiple_of(number * capacity, 16), capacity)]

        into = block(target, area * n + me)
        for step in range(n):
            to = lax.rem(me + step, n)
            piece = block(source, to * 2 + kind)
            far = remote(
                piece, into, row_send.at[which, kind, step], row_recv.at[which, area, me], {"sp": to, "dp": plane}
            )
            if step:
                yield True, far
                continue
            if kind == 0:
                yield planes.outer, far
            stays = planes.inner if kind == 0 else True
            yield stays, pltpu.make_async_copy(piece, into, row_local.at[which, kind])

    def each(copies, act):
        for condition, copy in copies:
            if condition is True:
                act(copy)
            else:
                pl.when(condition)(functools.partial(act, copy))

    def start(copy):
        copy.start()

    def end(copy):
        if copy.is_remote:
            copy.wait_send()
        else:
            copy.wait()

    def dispatch(which):
        for kind in range(2):
            each(dispatch_copies(which, kind), start)

    for first in range(0, 2 * span, ROWS):
        slots = first + lax.broadcasted_iota(jnp.int32, (ROWS, count), 0)
        chosen = hot(jnp.logical_or(slots == place[0], slots == place[1]))
        packed_grad[first : first + ROWS] = dot(chosen, cotangent[...]).astype(BF16)
    dispatch(1)
    for kind in range(3):
        wait_unit(lay, is_short, unit.at[kind], recv.at[kind])
    keep = lanes_first()
    lower = causal(BLOCK)

    def task(index, carry):
        start, block = lay.task(is_short, index)
        base = pl.multiple_of(start + block * BLOCK, BLOCK)
        queries = halves(unit[0, pl.ds(base, BLOCK)])

        def visit(place, state, diagonal):
            keys = unit[1, pl.ds(place, BLOCK)]
            values = unit[2, pl.ds(place, BLOCK)]
            result = []
            for (peak, total, summed), query in zip(state, queries):
                scores = dot_t(query, keys)
                if diagonal:
                    scores = jnp.where(lower, scores, NEGATIVE)
                new_peak = jnp.maximum(peak, jnp.max(scores, axis=1, keepdims=True))
                factor = jnp.exp(peak - new_peak)
                weight = jnp.exp(scores - new_peak)
                total = total * factor + jnp.sum(weight, axis=1, keepdims=True)
                summed = summed * factor + dot(weight.astype(BF16), values)
                result.append((new_peak, total, summed))
            return tuple(result)

        empty = (jnp.full((BLOCK, 1), NEGATIVE, F32), jnp.zeros((BLOCK, 1), F32), jnp.zeros((BLOCK, WIDE), F32))
        state = lax.fori_loop(
            0, block, lambda j, state: visit(pl.multiple_of(start + j * BLOCK, BLOCK), state, False), (empty, empty)
        )
        (peak_a, total_a, summed_a), (peak_b, total_b, summed_b) = visit(base, state, True)
        result = jnp.where(keep, summed_a / total_a, summed_b / total_b)
        attended[pl.ds(base, BLOCK)] = result
        staged_out[pl.ds(base, BLOCK)] = result.astype(BF16)
        log_total[pl.ds(base, BLOCK)] = jnp.where(keep, peak_a + jnp.log(total_a), peak_b + jnp.log(total_b))
        send_home(
            lay, me, is_short, seq, first_pair, base, block, start, staged_out, home, 0, out_send, home_recv, local
        )
        return carry

    lax.fori_loop(0, lay.tasks(is_short), task, 0)
    finish_sends(me, started)
    wait_home(lay, is_short, staged_out, out_send, 1, True)
    wait_home(lay, is_short, staged_out, home_recv, 1, False)

    stream.begin((0, 1), planes.inner)
    stream.pass_on((2, 3), 1, False)
    stream.pass_on((0, 1), 1, True)
    x1 = tokens[...].astype(F32) + dot(home[...], w_out[...])
    middle[...] = x1
    hat, _ = normed(x1)
    second = (hat * gain_two[...] + shift_two[...]).astype(BF16)
    second_norm[...] = second
    for first in range(0, 2 * span, ROWS):
        slots = first + lax.broadcasted_iota(jnp.int32, (ROWS, count), 0)
        chosen = hot(jnp.logical_or(slots == place[0], slots == place[1]))
        packed[first : first + ROWS] = dot(chosen, second).astype(BF16)
    dispatch(0)
    logits = dot(second, w_router[...])
    index = lax.broadcasted_iota(jnp.int32, logits.shape, 1)
    chosen = [jnp.sum(jnp.where(index == routes[:, c : c + 1], logits, 0.0), axis=1, keepdims=True) for c in range(2)]
    top = jnp.maximum(chosen[0], chosen[1])
    exped = [jnp.exp(value - top) for value in chosen]
    gates = [value / (exped[0] + exped[1]) for value in exped]
    lane = lax.broadcasted_iota(jnp.int32, gates_out.shape, 1)
    gates_out[...] = jnp.where(lane == 0, gates[0], gates[1])
    column, _ = slot_columns(lay, capacity, routes[...])
    for number in range(2 * n):
        held = [
            jnp.where(jnp.logical_and(lane < capacity, lane + number * capacity == column[c]), gates[c], 0.0)
            for c in range(2)
        ]
        packed_gates[number] = jnp.broadcast_to(jnp.sum(held[0] + held[1], axis=0, keepdims=True), (8, 128))
    dispatch(2)

    def arrived(which, area):
        buffer = (rows_in, rows_grad, rows_gates)[which]
        for src in range(n):
            piece = buffer.at[area * n + src] if which == 2 else buffer.at[pl.ds((area * n + src) * capacity, capacity)]
            wait = pltpu.make_async_copy(piece, piece, row_recv.at[which, area, src]).wait
            if area == 1:
                wait()
            else:
                pl.when(src != me)(wait)

    for which in (1, 0, 2):
        for kind in range(2):
            each(dispatch_copies(which, kind), end)
    stream.begin((2, 3), planes.outer)
    stream.pass_on((0, 1), 1, False)

    def take(area):
        for which in (1, 0, 2):
            arrived(which, area)
        one = lax.broadcasted_iota(jnp.int32, (capacity, 128), 0) == lax.broadcasted_iota(jnp.int32, (capacity, 128), 1)

        def gated(src, carry):
            gate = jnp.sum(jnp.where(one, rows_gates[area * n + src, 0:1], 0.0), axis=1, keepdims=True)
            part = pl.ds(pl.multiple_of((area * n + src) * capacity, 16), capacity)
            rows_grad[part] = (gate * rows_grad[part].astype(F32)).astype(BF16)
            return carry

        lax.fori_loop(0, n, gated, 0)

    def clear(sums, rows):
        def one(index, carry):
            part = pl.ds(pl.multiple_of(index * ROWS, ROWS), ROWS)
            for total in sums:
                total[part] = jnp.zeros((ROWS, width), F32)
            return carry

        lax.fori_loop(0, rows // ROWS, one, 0)

    def weight_grads(index):
        stores = [
            pltpu.make_async_copy(stage, whole.at[index], load.at[2 + i])
            for i, (stage, whole) in enumerate(((grad_a, first_grad), (grad_b, second_grad)))
        ]
        tall = 3 * WIDE
        for total in (span, 2 * span):

            @pl.when(planes.hosts == (total > span))
            def _():
                every_row = pl.ds(0, total)
                for col in range(0, width, tall):
                    part = pl.ds(col, tall)
                    grad_a[part] = t_dot(rows_in[every_row, part], packed_grad[every_row, :hidden]).astype(BF16)
                for col in range(0, hidden, tall):
                    part = pl.ds(col, tall)
                    grad_b[part] = t_dot(packed[every_row, part], rows_grad[every_row]).astype(BF16)

        for copy in stores:
            copy.start()
        for copy in stores:
            copy.wait()

    def work(trained, sums, first_row, rows, nearest, farthest):
        arrays = (0, 1) if trained else (2, 3)
        last = jnp.maximum(planes.me, n_dp - 1 - planes.me)
        every = (all_a, all_b) if trained else (all_c, all_d)
        own = (own_a, own_b) if trained else (own_c, own_d)

        def one(step, carry):
            distance, side = step // 2, lax.rem(step, 2)
            index = jnp.where(side == 0, planes.me - distance, planes.me + distance)
            real = jnp.logical_and(jnp.logical_and(index >= 0, index < n_dp), jnp.logical_or(side == 0, distance > 0))

            if trained:

                @pl.when(jnp.logical_and(side == 1, distance == 1))
                def _():
                    stream.pass_on((2, 3), 1, True)

            @pl.when(jnp.logical_and(side == 0, distance >= 3))
            def _():
                stream.pass_on(arrays, distance)

            @pl.when(real)
            def _():
                near = [pltpu.make_async_copy(own[i], (weight_a, weight_b)[i], load.at[i]) for i in range(2)]
                far = [pltpu.make_async_copy(every[i].at[index], (weight_a, weight_b)[i], load.at[i]) for i in range(2)]

                @pl.when(distance == 0)
                def _():
                    for copy in near:
                        copy.start()

                @pl.when(distance > 0)
                def _():
                    for copy in far:
                        copy.start()

                for copy in near:
                    copy.wait()

                def chunk(number, carry):
                    part = pl.ds(pl.multiple_of(number * ROWS, ROWS), ROWS)
                    here = pl.ds(pl.multiple_of(first_row + number * ROWS, ROWS), ROWS)
                    active, slope = gelu_parts(dot(rows_in[here], weight_a[...]))
                    active = active.astype(BF16)
                    back = (dot_t(rows_grad[here], weight_b[...]) * slope).astype(BF16)
                    if trained:
                        packed[part, :hidden] = active
                        packed_grad[part, :hidden] = back
                    sums[0][part] += dot(active, weight_b[...])
                    sums[1][part] += dot_t(back, weight_a[...])
                    return carry

                lax.fori_loop(0, rows // ROWS, chunk, 0)
                if trained:

                    @pl.when(distance < last)
                    def _():
                        weight_grads(index)

            return carry

        lax.fori_loop(2 * nearest, 2 * farthest + 2, one, 0)

    def turn(sums, first_row, base, rows):
        def one(number, carry):
            part = pl.ds(pl.multiple_of(base + number * ROWS, ROWS), ROWS)
            here = pl.ds(pl.multiple_of(first_row + number * ROWS, ROWS), ROWS)
            back_out[here] = sums[0][part].astype(BF16)
            back_grad[here] = sums[1][part].astype(BF16)
            return carry

        lax.fori_loop(0, rows // ROWS, one, 0)

    def back_copies(kind, guest, whiches=(0, 1)):
        area = 2 if kind else int(guest)
        plane = planes.guest if guest else planes.me
        for which in whiches:
            source, target = ((back_out, got), (back_grad, got_grad))[which]
            into = target.at[pl.ds(pl.multiple_of((me * 2 + kind) * capacity, 16), capacity)]
            for step in range(n):
                to = lax.rem(me + step, n)
                piece = source.at[pl.ds(pl.multiple_of((area * n + to) * capacity, 16), capacity)]
                if step or guest:
                    yield True, remote(
                        piece, into, back_send.at[which, area, step], back_recv.at[which, kind, me], {"sp": to, "dp": plane}
                    )
                else:
                    yield True, pltpu.make_async_copy(piece, into, back_local.at[which, kind])

    def hops(act):
        for up in (True, False):
            for array, (whole, hop) in enumerate(((first_grad, hop_a), (second_grad, hop_b))):

                @pl.when(planes.me == (1 if up else n_dp - 2))
                def _():
                    act(
                        remote(
                            whole.at[n_dp - 1 if up else 0], hop.at[int(up)], hop_send.at[int(up), array],
                            hop_recv.at[int(up), array], {"dp": planes.me + (1 if up else -1)},
                        )
                    )

    train_sums, frozen_sums = (out_sum, in_sum), (out_other, in_other)
    train_rows = jnp.where(planes.hosts, 2 * span, span)
    clear(frozen_sums, span)

    clear(train_sums, train_rows)

    @pl.when(planes.inner)
    def _():
        take(0)

        @pl.when(planes.hosts)
        def _():
            take(1)

        work(True, train_sums, 0, train_rows, 0, 1)
        stream.pass_on((0, 1), 2)
        work(True, train_sums, 0, train_rows, 2, n_dp - 1)

        @pl.when(planes.hosts)
        def _():
            turn(train_sums, span, span, span)
            each(back_copies(0, True, (0,)), start)

        turn(train_sums, 0, 0, span)
        each(back_copies(0, False), start)
        weight_grads(jnp.where(planes.me > n_dp - 1 - planes.me, 0, n_dp - 1))

    take(2)
    work(False, frozen_sums, 2 * span, span, 0, 1)
    stream.pass_on((2, 3), 2)

    hops(start)

    @pl.when(planes.hosts)
    def _():
        each(back_copies(0, True, (1,)), start)

    work(False, frozen_sums, 2 * span, span, 2, n_dp - 1)
    turn(frozen_sums, 2 * span, 0, span)
    each(back_copies(1, False), start)
    each(back_copies(1, False), end)

    @pl.when(planes.inner)
    def _():
        each(back_copies(0, False), end)

        @pl.when(planes.hosts)
        def _():
            each(back_copies(0, True), end)

    for kind in range(2):
        for which, buffer in enumerate((got, got_grad)):
            for src in range(n):
                piece = buffer.at[pl.ds((src * 2 + kind) * capacity, capacity)]
                comes = jnp.logical_or(src != me, planes.outer) if kind == 0 else src != me
                pl.when(comes)(pltpu.make_async_copy(piece, piece, back_recv.at[which, kind, src]).wait)
    stream.finish()
    hops(end)
    for up in (True, False):
        for array, hop in enumerate((hop_a, hop_b)):

            @pl.when(planes.me == (2 if up else n_dp - 3))
            def _():
                pltpu.make_async_copy(hop.at[int(up)], hop.at[int(up)], hop_recv.at[int(up), array]).wait()


ANY = pl.BlockSpec(memory_space=pl.ANY)


def layer(lay, capacity, n_dp, tokens, vectors, w_qkv, w_out, w_router, routes, cotangent, weights):
    count, width = tokens.shape
    n = lay.n
    owners = len(lay.owners())
    span = n * capacity
    shape = jax.ShapeDtypeStruct
    hidden = weights[0].shape[1]
    every = [shape((n_dp, *weight.shape), BF16) for weight in weights]
    return pl.pallas_call(
        functools.partial(layer_kernel, lay, capacity, n_dp),
        out_shape=(
            shape((count, width), BF16),
            shape((3, UNIT, WIDE), BF16),
            shape((UNIT, WIDE), F32),
            shape((UNIT, WIDE), F32),
            shape((count, width), BF16),
            shape((count, width), F32),
            shape((count, width), BF16),
            shape((count, 128), F32),
            shape((2 * span, width), BF16),
            shape((2 * span, width), BF16),
            every[0],
            every[1],
            *every,
            shape((2, *weights[0].shape), BF16),
            shape((2, *weights[1].shape), BF16),
        ),
        in_specs=[VMEM] * 8 + [ANY] * 4,
        out_specs=[VMEM] * 8 + [ANY] * 10,
        scratch_shapes=[
            pltpu.VMEM((UNIT, WIDE), BF16),
            pltpu.VMEM((2 * span, width), BF16),
            pltpu.VMEM((2 * span, width), BF16),
            pltpu.VMEM((3 * span, width), BF16),
            pltpu.VMEM((3 * span, width), BF16),
            pltpu.VMEM((width, hidden), BF16),
            pltpu.VMEM((hidden, width), BF16),
            pltpu.VMEM((2 * span, width), F32),
            pltpu.VMEM((2 * span, width), F32),
            pltpu.VMEM((span, width), F32),
            pltpu.VMEM((span, width), F32),
            pltpu.VMEM((3 * span, width), BF16),
            pltpu.VMEM((3 * span, width), BF16),
            pltpu.VMEM((width, hidden), BF16),
            pltpu.VMEM((hidden, width), BF16),
            pltpu.VMEM((2 * n, 8, 128), F32),
            pltpu.VMEM((3 * n, 8, 128), F32),
            DMA((9 * owners,)),
            DMA((3,)),
            DMA,
            DMA,
            DMA,
            DMA((2, 4, n_dp)),
            DMA((4, n_dp)),
            DMA((4,)),
            DMA((3, 2, n)),
            DMA((3, 3, n)),
            DMA((3, 2)),
            DMA((2, 3, n)),
            DMA((2, 2, n)),
            DMA((2, 2)),
            DMA((2, 2)),
            DMA((2, 2)),
        ],
        compiler_params=pltpu.CompilerParams(collective_id=0, has_side_effects=True, vmem_limit_bytes=LIMIT),
        cost_estimate=pl.CostEstimate(flops=50 * 10**9, bytes_accessed=100 * 2**20, transcendentals=10**7),
        name="layer",
    )(
        tokens, vectors, w_qkv, w_out, w_router, routes, routes.T, cotangent, *weights
    )


class Sum:
    def __init__(self, n_sp, n_dp, pieces, quantum, needed):
        self.n_sp, self.n_dp = n_sp, n_dp
        self.bits = n_sp.bit_length() - 1
        unit = math.lcm(16 * n_sp * n_dp, quantum)
        units = -(-needed // unit)
        pieces = min(pieces, units)
        sizes = [units // pieces + (p < units % pieces) for p in range(pieces)]
        self.pieces = [(unit * sum(sizes[:p]), unit * size) for p, size in enumerate(sizes)]
        self.rows = unit * units
        self.steps = 2 * self.bits + 2

    def order(self, piece):
        later = list(range(1, self.bits))
        return [0] + (later[::-1] if piece % 2 else later)

    def landing(self):
        places, start = [], 0
        for _, rows in self.pieces:
            places.append([])
            for step in range(self.bits + 1):
                rows = rows // 2 if step < self.bits else rows
                places[-1].append((start, rows))
                start += rows
        return places, start

    def bind(self, mine, landed, whole, send, recv):
        self.mine, self.landed, self.whole, self.send, self.recv = mine, landed, whole, send, recv
        self.me, self.plane = lax.axis_index("sp"), lax.axis_index("dp")
        self.places, _ = self.landing()
        self.starts = [[start] for start, _ in self.pieces]
        for piece, (_, rows) in enumerate(self.pieces):
            for bit in self.order(piece):
                rows //= 2
                value = (self.me // (1 << bit)) % 2
                self.starts[piece].append(self.starts[piece][-1] + value * rows)

    def partner(self, bit):
        value = (self.me // (1 << bit)) % 2
        return self.me + (1 - 2 * value) * (1 << bit)

    def peers(self):
        found = [(True, {"sp": self.partner(bit)}) for bit in range(self.bits)]
        return found + [(True, {"dp": lax.rem(self.plane + step, self.n_dp)}) for step in range(1, self.n_dp)]

    def cut(self, start, rows):
        return pl.ds(pl.multiple_of(start, 16), rows)

    def copies(self, piece, step):
        bits = self.bits
        rows = self.pieces[piece][1]
        if step < bits or step > bits + 1:
            level = step if step < bits else 2 * bits + 1 - step
            bit = self.order(piece)[level]
            half = rows >> (level + 1)
            held, kept = self.starts[piece][level], self.starts[piece][level + 1]
            if step < bits:
                start, _ = self.places[piece][step]
                source = self.mine.at[self.cut(2 * held + half - kept, half)]
                target = self.landed.at[pl.ds(start, half)]
            else:
                source = target = self.whole.at[self.cut(kept, half)]
            yield remote(source, target, self.send.at[piece, step, 0], self.recv.at[piece, step, 0], self.partner(bit))
            return
        block = (rows >> bits) // self.n_dp
        base = self.starts[piece][bits]
        start, _ = self.places[piece][bits]
        for far in range(1, self.n_dp):
            other = lax.rem(self.plane + far, self.n_dp)
            if step == bits:
                source = self.mine.at[self.cut(base + other * block, block)]
                target = self.landed.at[self.cut(start + self.plane * block, block)]
            else:
                source = target = self.whole.at[self.cut(base + self.plane * block, block)]
            yield remote(source, target, self.send.at[piece, step, far], self.recv.at[piece, step, far], {"dp": other})

    def start(self, piece, step):
        for copy in self.copies(piece, step):
            copy.start()

    def add(self, piece, step):
        for copy in self.copies(piece, step):
            copy.wait()
        bits, rows = self.bits, self.pieces[piece][1]
        if step > bits:
            return
        start, _ = self.places[piece][step]
        if step < bits:
            size, kept = rows >> (step + 1), self.starts[piece][step + 1]
            for first, count in blocks(size):

                def one(number, carry):
                    part = self.cut(kept + first + number * count[0], count[0])
                    here = self.cut(start + first + number * count[0], count[0])
                    self.mine[part] = (self.mine[part].astype(F32) + self.landed[here].astype(F32)).astype(BF16)
                    return carry

                lax.fori_loop(0, count[1], one, 0)
            return
        block = (rows >> bits) // self.n_dp
        own = self.cut(self.starts[piece][bits] + self.plane * block, block)
        total = self.mine[own].astype(F32)
        for far in range(1, self.n_dp):
            other = lax.rem(self.plane + far, self.n_dp)
            total = total + self.landed[self.cut(start + other * block, block)].astype(F32)
        self.whole[own] = total.astype(BF16)


def blocks(rows, size=512):
    found = []
    if rows >= size:
        found.append((0, (size, rows // size)))
    if rows % size:
        found.append((rows - rows % size, (rows % size, 1)))
    return found


def run_sum(total, ahead, ready, done):
    begun = [ahead] + [1 - piece for piece in range(1, len(total.pieces))]
    while any(step <= total.steps for step in begun):
        for piece, step in enumerate(begun):
            if 0 < step <= total.steps:
                total.add(piece, step - 1)
                if step == total.steps:
                    done(piece)
            if step == 0:
                ready(piece)
            if 0 <= step < total.steps:
                total.start(piece, step)
            begun[piece] += 1


class Gather:
    def __init__(self, n, own, hop, below, above, theirs, sums, stage, send, recv, load):
        self.n, self.own, self.hop, self.below, self.above, self.stage = n, own, hop, below, above, stage
        self.theirs, self.sums, self.send, self.recv, self.load = theirs, sums, send, recv, load
        self.me = lax.axis_index("dp")
        self.inner = jnp.logical_and(self.me >= 1, self.me <= n - 2)

    def copy(self, array, index, up, source):
        target = (self.below if up else self.above)[array].at[index]
        other = self.me + 1 if up else self.me - 1
        return remote(
            source, target, self.send.at[int(up), array, index], self.recv.at[int(up), array, index], {"dp": other}
        )

    def fetch(self, source, buffer, number):
        moved = pltpu.make_async_copy(source, buffer, self.load.at[number])
        moved.start()
        return moved

    def wanted(self, index, up):
        return jnp.logical_and(self.inner, index > self.me if up else index < self.me)

    def begins(self, up):
        return self.me == 1 if up else self.me == self.n - 2

    def hopped(self, index, up):
        if index not in (0, self.n - 1):
            return False
        return self.me == 2 if up else self.me == self.n - 3

    def begin(self, array, index, up):
        @pl.when(jnp.logical_and(self.wanted(index, up), self.begins(up)))
        def _():
            self.copy(array, index, up, self.own[array].at[index]).start()

    def came(self, array, index, up):
        buffer = (self.below if up else self.above)[array].at[index]
        pltpu.make_async_copy(buffer, buffer, self.recv.at[int(up), array, index]).wait()
        return buffer

    def pass_on(self, array, index, up):
        @pl.when(jnp.logical_and(self.wanted(index, up), jnp.logical_not(self.begins(up))))
        def _():
            total, theirs = self.sums[array].at[int(up)], self.theirs[array]
            here = self.fetch(self.own[array].at[index], total, 0)
            hopped = self.hopped(index, up)

            @pl.when(hopped)
            def _():
                self.fetch(self.hop[array].at[int(up)], theirs, 1).wait()

            @pl.when(jnp.logical_not(hopped))
            def _():
                self.fetch(self.came(array, index, up), theirs, 1).wait()

            here.wait()
            total[...] = (total[...].astype(F32) + theirs[...].astype(F32)).astype(BF16)
            self.copy(array, index, up, total).start()

    def finish(self, array, index, up):
        waits = self.wanted(index, up)
        if index in (0, self.n - 1):
            waits = jnp.logical_and(waits, jnp.logical_not(self.begins(up)))

        @pl.when(waits)
        def _():
            self.copy(array, index, up, self.sums[array].at[int(up)]).wait_send()

    def total(self, array, out):
        theirs = self.theirs[array]

        @pl.when(self.inner)
        def _():
            self.fetch(self.own[array].at[self.me], theirs, 0).wait()

        @pl.when(jnp.logical_not(self.inner))
        def _():
            theirs[...] = jnp.zeros_like(theirs)

        sides = ((True, self.me >= 2), (False, self.me <= self.n - 3))
        for up, comes in sides:

            @pl.when(comes)
            def _():
                self.fetch(self.came(array, self.me, up), self.sums[array].at[int(up)], 1).wait()

        rows, lanes = out.shape
        stores = []
        for number in range(lanes // WIDE):
            part = pl.ds(number * WIDE, WIDE)
            stage = self.stage.at[number % 2, pl.ds(0, rows), pl.ds(0, WIDE)]
            if number >= 2:
                stores[number - 2].wait()
            stage[...] = theirs[:, part].astype(F32)
            for up, comes in sides:

                @pl.when(comes)
                def _():
                    stage[...] += self.sums[array][int(up), :, part].astype(F32)

            stores.append(pltpu.make_async_copy(stage, out.at[:, part], self.load.at[3 + number % 2]))
            stores[number].start()
        for store in stores[-2:]:
            store.wait()


def gather_scratch(n, first, second):
    shapes = [first.shape[1:], second.shape[1:]]
    return [
        *(pltpu.VMEM(shape, BF16) for shape in shapes),
        *(pltpu.VMEM((2, *shape), BF16) for shape in shapes),
        DMA((2, 2, n)),
        DMA((2, 2, n)),
        DMA((5,)),
    ]


def back_kernel(
    lay, capacity, replicated,
    got, got_grad, middle, second_norm, gates, home_out, w_out, vectors, w_router, routes, cotangent,
    unit, attended, log_total, first_norm, tokens, w_qkv, first_own, second_own, hop_a, hop_b,
    block_out, tokens_grad, qkv_grad, out_proj_grad, router_out, vectors_out, first_total, second_total, below_a, below_b, above_a, above_b,
    grad_attended, grad_out, deltas, query_sum, staged, home, send, recv, out_send, home_recv, local,
    theirs_a, theirs_b, sums_a, sums_b, pass_send, pass_recv, load,
    grads, landed, summed, stage, sum_send, sum_recv,
):
    n_dp = first_own.shape[0]
    gather = Gather(
        n_dp, (first_own, second_own), (hop_a, hop_b), (below_a, below_b), (above_a, above_b), (theirs_a, theirs_b),
        (sums_a, sums_b), stage, pass_send, pass_recv, load,
    )
    gain_one, gain_two = vectors.at[0:1], vectors.at[2:3]
    replicated.bind(grads, landed, summed, sum_send, sum_recv)
    me = lax.axis_index("sp")
    is_short, seq, first_pair = lay.role(me)
    everywhere = [(True, {"dp": lax.rem(gather.me + step, n_dp)}) for step in range(1, n_dp)]
    meet(plane_peers(lay.n) + everywhere)
    kept = pltpu.make_async_copy(attended, deltas, load.at[2])
    kept.start()
    inside = [(up, index) for index in range(1, n_dp - 1) for up in (True, False)]
    ends = [(True, n_dp - 1), (False, 0)]
    for array in range(2):
        for up, index in inside:
            gather.begin(array, index, up)
    place, matches = slot_columns(lay, capacity, routes[...])
    slots = lax.broadcasted_iota(jnp.int32, (tokens.shape[0], got.shape[0]), 1)
    chosen = [hot(slots == place[c]) for c in range(2)]
    upstream = cotangent[...].astype(F32)
    gate = [gates[:, c : c + 1] for c in range(2)]
    total = middle[...]
    grad_gate = []
    for c in range(2):
        produced = dot(chosen[c], got[...])
        total = total + gate[c] * produced
        grad_gate.append(jnp.sum(upstream * produced, axis=1, keepdims=True))
    block_out[...] = total.astype(BF16)
    mean_grad = gate[0] * grad_gate[0] + gate[1] * grad_gate[1]
    grad_logits = sum(matches[c] * (gate[c] * (grad_gate[c] - mean_grad)) for c in range(2))
    high = grad_logits.astype(BF16)
    low = (grad_logits - high.astype(F32)).astype(BF16)
    router_grad = t_dot(second_norm[...], high) + t_dot(second_norm[...], low)
    grad_second = dot_t(high, w_router[...]) + dot_t(low, w_router[...])
    grad_second = grad_second + dot(chosen[0] + chosen[1], got_grad[...])
    hat, scale = normed(middle[...])
    gain_two_grad = jnp.sum(grad_second * hat, axis=0, keepdims=True)
    shift_two_grad = jnp.sum(grad_second, axis=0, keepdims=True)
    grad = upstream + norm_back(grad_second, gain_two[...], hat, scale)
    tokens_grad[...] = grad
    branch = grad.astype(BF16)
    grad_attended[...] = dot_t(branch, w_out[...]).astype(BF16)
    out_proj = t_dot(home_out[...], branch)
    width = w_out.shape[0]

    def put(column, value):
        for lane in range(0, value.shape[1], WIDE):
            grads[pl.ds((column + lane) // WIDE * width, width)] = value[:, lane : lane + WIDE].astype(BF16)

    put(0, out_proj)
    early = 4 if replicated.pieces[0][1] <= width // WIDE * width else 0
    if early:
        replicated.start(0, 0)
    started = to_owners(
        lay,
        me,
        lambda pair: pair * WIDE,
        lambda number: number,
        grad_attended,
        lambda start, rows: grad_out.at[pl.ds(pl.multiple_of(start, 16), rows)],
        send,
        recv,
        local,
        range(PAIRS),
    )
    for array in range(2):
        for up, index in ends:
            gather.pass_on(array, index, up)
    query_sum[...] = jnp.zeros_like(query_sum)
    keep = lanes_first()
    lower = causal(BLOCK)
    wait_unit(lay, is_short, grad_out, recv)
    kept.wait()

    def make_delta(index, carry):
        part = pl.ds(pl.multiple_of(index * BLOCK, BLOCK), BLOCK)
        first, second = halves(grad_out[part].astype(F32) * deltas[part])
        deltas[part] = jnp.where(
            keep, jnp.sum(first, axis=1, keepdims=True), jnp.sum(second, axis=1, keepdims=True)
        )
        return carry

    lax.fori_loop(0, lay.tasks(is_short), make_delta, 0)
    per = jnp.where(is_short, LEN_A // BLOCK, LEN_B // BLOCK)

    def task(index, carry):
        start, block = lay.task(is_short, index)
        base = pl.multiple_of(start + block * BLOCK, BLOCK)
        keys = unit[1, pl.ds(base, BLOCK)]
        values = unit[2, pl.ds(base, BLOCK)]
        key_both = jnp.concatenate(halves(keys), axis=0)

        def visit(place, state, diagonal):
            part = pl.ds(place, BLOCK)
            grad_key, grad_value = state
            queries = halves(unit[0, part])
            outs = halves(grad_out[part])
            weights, grads = [], []
            for which, (query, out) in enumerate(zip(queries, outs)):
                column = which * HEAD_DIM
                scores = dot_t(query, keys)
                if diagonal:
                    scores = jnp.where(lower, scores, NEGATIVE)
                weight = jnp.exp(scores - log_total[part, column : column + 1])
                grad = weight * (dot_t(out, values) - deltas[part, column : column + 1])
                weights.append(weight.astype(BF16))
                grads.append(grad.astype(BF16))
            grad_value = grad_value + t_dot(jnp.concatenate(weights, axis=0), jnp.concatenate(outs, axis=0))
            grad_key = grad_key + t_dot(jnp.concatenate(grads, axis=0), jnp.concatenate(queries, axis=0))
            query_sum[part] += dot(jnp.concatenate(grads, axis=1), key_both)
            return grad_key, grad_value

        zero = jnp.zeros((BLOCK, WIDE), F32)
        state = visit(base, (zero, zero), True)
        grad_key, grad_value = lax.fori_loop(
            block + 1, per, lambda i, state: visit(pl.multiple_of(start + i * BLOCK, BLOCK), state, False), state
        )
        part = pl.ds(base, BLOCK)
        staged[0, part] = (query_sum[part] * HEAD_DIM**-0.5).astype(BF16)
        staged[1, part] = grad_key.astype(BF16)
        staged[2, part] = grad_value.astype(BF16)
        for kind in range(3):
            send_home(
                lay, me, is_short, seq, first_pair, base, block, start, staged.at[kind], home, kind * PAIRS * WIDE,
                out_send.at[kind], home_recv.at[kind], local,
            )
        for step in range(1, early):

            @pl.when(index == 2 * step)
            def _():
                replicated.add(0, step - 1)
                replicated.start(0, step)

        return carry

    lax.fori_loop(0, lay.tasks(is_short), task, 0)
    for kind in range(3):
        wait_home(lay, is_short, staged.at[kind], home_recv.at[kind], 1, False)
    grad_first = dot_t(home[...], w_qkv[...])
    hat, scale = normed(tokens[...].astype(F32))
    gain_one_grad = jnp.sum(grad_first * hat, axis=0, keepdims=True)
    shift_one_grad = jnp.sum(grad_first, axis=0, keepdims=True)
    tokens_grad[...] += norm_back(grad_first, gain_one[...], hat, scale)
    parts = (gain_one_grad, shift_one_grad, gain_two_grad, shift_two_grad)
    grads[pl.ds(width // WIDE * width, width)] = router_grad.astype(BF16)
    rows = [part[:, lane : lane + WIDE] for part in parts for lane in range(0, width, WIDE)]
    rows.append(jnp.zeros((width - len(rows), WIDE), F32))
    grads[pl.ds(7 * width, width)] = jnp.concatenate(rows, axis=0).astype(BF16)
    first = 8
    last = first + 3 * PAIRS
    for spare in range(last, replicated.rows // width):
        grads[pl.ds(spare * width, width)] = jnp.zeros((width, WIDE), BF16)

    def ready(piece):
        start, rows = replicated.pieces[piece]
        for column in range(start // width, (start + rows) // width, 2):
            if first <= column < last:
                lanes = pl.ds((column - first) * WIDE, 2 * WIDE)
                put(column * WIDE, t_dot(first_norm[...], home[:, lanes]))

    stores = []

    def done(piece):
        start, rows = replicated.pieces[piece]
        for column in range(start // width, (start + rows) // width, 2):
            blocks = [summed.at[pl.ds((column + i) * width, width)] for i in range(2)]
            if column == 6:
                router_out[...] = blocks[0][...].astype(F32)
                vectors_out[...] = blocks[1][0:32].astype(F32)
            elif column < last:
                number = len(stores)
                if number >= 2:
                    stores[number - 2].wait()
                for i in range(2):
                    stage[number % 2, :, i * WIDE : (i + 1) * WIDE] = blocks[i][...].astype(F32)
                target, lane = (out_proj_grad, column * WIDE) if column < 6 else (qkv_grad, (column - first) * WIDE)
                stores.append(
                    pltpu.make_async_copy(stage.at[number % 2], target.at[:, pl.ds(lane, 2 * WIDE)], load.at[3 + number % 2])
                )
                stores[number].start()

    run_sum(replicated, early, ready, done)
    for store in stores[-2:]:
        store.wait()
    for array, out in enumerate((first_total, second_total)):
        for up, index in inside:
            gather.pass_on(array, index, up)
        for up, index in inside + ends:
            gather.finish(array, index, up)
        gather.total(array, out)
    finish_sends(me, started)
    for kind in range(3):
        wait_home(lay, is_short, staged.at[kind], out_send.at[kind], 1, True)


def backward(lay, capacity, values):
    count, width = values[2].shape
    owners = len(lay.owners())
    shape = jax.ShapeDtypeStruct
    slices = values[-4:-2]
    replicated = Sum(lay.n, slices[0].shape[0], 6, 2 * width, 26 * width)
    return pl.pallas_call(
        functools.partial(back_kernel, lay, capacity, replicated),
        out_shape=(
            shape((count, width), BF16), shape((count, width), F32),
            shape((width, 3 * width), F32), shape((width, width), F32), shape((width, WIDE), F32), shape((32, WIDE), F32),
            *(shape(g.shape[1:], F32) for g in slices), *(shape(g.shape, BF16) for g in slices * 2),
        ),
        in_specs=[VMEM] * 12 + [ANY] + [VMEM] * 4 + [ANY] * 4,
        out_specs=[VMEM] * 2 + [ANY] * 2 + [VMEM] * 2 + [ANY] * 6,
        scratch_shapes=[
            pltpu.VMEM((count, width), BF16),
            pltpu.VMEM((UNIT, WIDE), BF16),
            pltpu.VMEM((UNIT, WIDE), F32),
            pltpu.VMEM((UNIT, WIDE), F32),
            pltpu.VMEM((3, UNIT, WIDE), BF16),
            pltpu.VMEM((count, 3 * width), BF16),
            DMA((owners,)),
            DMA,
            DMA((3,)),
            DMA((3,)),
            DMA,
            *gather_scratch(slices[0].shape[0], *slices),
            pltpu.VMEM((replicated.rows, WIDE), BF16),
            pltpu.VMEM((replicated.landing()[1], WIDE), BF16),
            pltpu.VMEM((replicated.rows, WIDE), BF16),
            pltpu.VMEM((2, width, 2 * WIDE), F32),
            DMA((len(replicated.pieces), replicated.steps, slices[0].shape[0])),
            DMA((len(replicated.pieces), replicated.steps, slices[0].shape[0])),
        ],
        compiler_params=pltpu.CompilerParams(collective_id=1, has_side_effects=True, vmem_limit_bytes=LIMIT),
        cost_estimate=pl.CostEstimate(flops=16 * 10**9, bytes_accessed=60 * 2**20, transcendentals=5 * 10**6),
        name="backward",
    )(*values)


def shards(
    tokens, ln1_gain, ln1_shift, w_qkv, w_out, ln2_gain, ln2_shift, w_router,
    train_w1, train_w2, frozen_w1, frozen_w2, routes, cotangent,
):
    lay = Layout(lax.axis_size("sp"))
    n_dp = lax.axis_size("dp")
    tokens, routes, cotangent = tokens[0], routes[0], cotangent[0]
    count, width = tokens.shape
    capacity = 2 * count // lay.n
    experts = w_router.shape[1]
    router_wide = jnp.pad(w_router, ((0, 0), (0, 128 - experts)))
    vectors = jnp.stack([ln1_gain, ln1_shift, ln2_gain, ln2_shift])
    weights = [weight[0] for weight in (train_w1, train_w2, frozen_w1, frozen_w2)]
    (
        first_norm, unit, attended, log_total, home, middle, second, gates, got, got_grad, first_grad, second_grad,
        _, _, _, _, hop_a, hop_b,
    ) = layer(lay, capacity, n_dp, tokens, vectors, w_qkv, w_out, router_wide, routes, cotangent, weights)
    block_out, tokens_grad, qkv_grad, out_proj, router, vector_rows, first_total, second_total, *_ = backward(
        lay, capacity,
        (
            got, got_grad, middle, second, gates, home, w_out, vectors, router_wide, routes, cotangent,
            unit, attended, log_total, first_norm, tokens, w_qkv, first_grad, second_grad, hop_a, hop_b,
        ),
    )
    found = vector_rows[: 4 * width // WIDE].reshape(4, width)
    return (
        block_out[None],
        tokens_grad[None],
        found[0],
        found[1],
        qkv_grad,
        out_proj,
        found[2],
        found[3],
        router[:, :experts],
        first_total[None],
        second_total[None],
    )


def solution(mesh):
    in_specs = (
        P("dp", "sp", None), P(), P(), P(), P(), P(), P(), P(),
        P("sp", None, "dp"), P("sp", "dp", None), P("sp", None, "dp"), P("sp", "dp", None),
        P("dp", "sp", None), P("dp", "sp", None),
    )
    out_specs = (
        P("dp", "sp", None), P("dp", "sp", None), P(), P(), P(), P(), P(), P(), P(),
        P("sp", None, "dp"), P("sp", "dp", None),
    )
    return jax.shard_map(shards, mesh=mesh, in_specs=in_specs, out_specs=out_specs, check_vma=False)
```

```python
import functools
import math

import jax
import jax.numpy as jnp
from jax import lax
from jax.experimental import pallas as pl
from jax.experimental.pallas import tpu as pltpu
from jax.sharding import PartitionSpec as P

HEADS = 12
HEAD_DIM = 64
LEN_A = 1024
LEN_B = 2048
PAIRS = HEADS // 2
WIDE = 2 * HEAD_DIM
UNIT = 3 * LEN_A
BLOCK = 256
EPSILON = 1e-05
NEGATIVE = -1e30
MESH = pl.DeviceIdType.MESH
DMA = pltpu.SemaphoreType.DMA
F32 = jnp.float32
BF16 = jnp.bfloat16
VMEM = pl.BlockSpec(memory_space=pltpu.VMEM)


def dot(a, b):
    return jnp.dot(a, b, preferred_element_type=F32)


def dot_t(a, b):
    return lax.dot_general(a, b, (((1,), (1,)), ((), ())), preferred_element_type=F32)


def t_dot(a, b):
    return lax.dot_general(a, b, (((0,), (0,)), ((), ())), preferred_element_type=F32)


def normed(value):
    centre = jnp.mean(value, axis=-1, keepdims=True)
    centred = value - centre
    spread = jnp.mean(centred * centred, axis=-1, keepdims=True)
    scale = lax.rsqrt(spread + EPSILON)
    return centred * scale, scale


def norm_back(grad, gain, hat, scale):
    scaled = grad * gain
    first = jnp.mean(scaled, axis=-1, keepdims=True)
    second = jnp.mean(scaled * hat, axis=-1, keepdims=True)
    return (scaled - first - hat * second) * scale


class Layout:
    def __init__(self, n_sp):
        self.n = n_sp
        self.sequences = n_sp // 8
        self.short = LEN_A // n_sp
        self.long = LEN_B // n_sp
        self.split = self.sequences * self.short

    def owners(self):
        found = []
        for seq in range(self.sequences):
            for pair in range(PAIRS):
                number = seq * PAIRS + pair
                found.append((number + number // 3 + 1, True, self.split + seq * self.long, self.long, pair, 0))
                found.append((4 * (seq * 2 + pair // 3), False, seq * self.short, self.short, pair, (pair % 3) * LEN_A))
        return found

    def role(self, me):
        is_short = lax.rem(me, 4) == 0
        number = me - me // 4 - 1
        group = me // 4
        seq = jnp.where(is_short, group // 2, number // PAIRS)
        pair = jnp.where(is_short, 3 * lax.rem(group, 2), lax.rem(number, PAIRS))
        return is_short, seq, pair

    def task(self, is_short, index):
        per = LEN_A // BLOCK
        start = jnp.where(is_short, (index // per) * LEN_A, 0)
        block = jnp.where(is_short, lax.rem(index, per), index)
        return pl.multiple_of(start, BLOCK), block

    def tasks(self, is_short):
        return jnp.where(is_short, 3 * LEN_A // BLOCK, LEN_B // BLOCK)


def meet(peers):
    barrier = pltpu.get_barrier_semaphore()
    for wanted, device in peers:

        @pl.when(wanted)
        def _():
            pl.semaphore_signal(barrier, inc=1, device_id=device, device_id_type=MESH)

    pl.semaphore_wait(barrier, sum(jnp.asarray(wanted, jnp.int32) for wanted, _ in peers))


def plane_peers(n):
    me = lax.axis_index("sp")
    return [(True, {"sp": lax.rem(me + step, n)}) for step in range(1, n)]


def remote(source, target, send_sem, recv_sem, device):
    device = device if isinstance(device, dict) else {"sp": device}
    return pltpu.make_async_remote_copy(
        src_ref=source, dst_ref=target, send_sem=send_sem, recv_sem=recv_sem, device_id=device, device_id_type=MESH
    )


def lanes_first():
    return lax.broadcasted_iota(jnp.int32, (1, WIDE), 1) < HEAD_DIM


def halves(value):
    keep = lanes_first()
    zero = jnp.zeros_like(value)
    return jnp.where(keep, value, zero), jnp.where(keep, zero, value)


def causal(rows):
    return lax.broadcasted_iota(jnp.int32, (rows, rows), 0) >= lax.broadcasted_iota(jnp.int32, (rows, rows), 1)


def to_owners(lay, me, cols, slot, source, target, send_sems, recv_sem, local_sem, wanted):
    started = []
    for number, (owner, is_long, start, rows, pair, unit) in enumerate(lay.owners()):
        if pair not in wanted:
            continue
        piece = source.at[pl.ds(start, rows), pl.ds(cols(pair), WIDE)]
        place = target(unit + me * rows, rows)
        far = remote(piece, place, send_sems.at[slot(number)], recv_sem, owner)
        near = pltpu.make_async_copy(piece, place, local_sem)

        @pl.when(me != owner)
        def _():
            far.start()

        @pl.when(me == owner)
        def _():
            near.start()
            near.wait()

        started.append((owner, far))
    return started


def finish_sends(me, started):
    for owner, copy in started:

        @pl.when(me != owner)
        def _():
            copy.wait_send()


def wait_unit(lay, is_short, buffer, sem):
    for short, rows in ((True, 3 * (lay.n - 1) * lay.short), (False, (lay.n - 1) * lay.long)):

        @pl.when(is_short == short)
        def _():
            piece = buffer.at[pl.ds(0, rows)]
            pltpu.make_async_copy(piece, piece, sem).wait()


def send_home(lay, me, is_short, seq, first_pair, base, block, unit_start, source, target, base_col, send_sem, recv_sem, local_sem):
    for short, rows in ((True, lay.short), (False, lay.long)):

        @pl.when(is_short == short)
        def _():
            pair = first_pair + (unit_start // LEN_A if short else 0)
            column = pl.multiple_of(base_col + pair * WIDE, WIDE)
            first = pl.multiple_of(seq * rows + (0 if short else lay.split), 16)
            for part in range(BLOCK // rows):
                home = block * (BLOCK // rows) + part
                piece = source.at[pl.ds(pl.multiple_of(base + part * rows, 16), rows)]
                place = target.at[pl.ds(first, rows), pl.ds(column, WIDE)]

                @pl.when(home != me)
                def _():
                    remote(piece, place, send_sem, recv_sem, home).start()

                @pl.when(home == me)
                def _():
                    near = pltpu.make_async_copy(piece, place, local_sem)
                    near.start()
                    near.wait()


def wait_home(lay, is_short, scratch, sem, tensors, sent):
    for short in (True, False):
        own = 3 * lay.short if short else lay.long
        if sent:
            rows = (3 * LEN_A if short else LEN_B) - own
        else:
            rows = PAIRS * lay.sequences * (lay.short + lay.long) - own

        @pl.when(is_short == short)
        def _():
            for _ in range(tensors):
                piece = scratch.at[pl.ds(0, rows)]
                pltpu.make_async_copy(piece, piece, sem).wait()


class Planes:
    def __init__(self, n_dp):
        self.n = n_dp
        self.me = lax.axis_index("dp")
        self.outer = jnp.logical_or(self.me == 0, self.me == n_dp - 1)
        self.inner = jnp.logical_not(self.outer)
        self.inward = jnp.where(self.me == 0, 1, n_dp - 2)
        self.hosts = jnp.logical_or(self.me == 1, self.me == n_dp - 2)
        self.guest = jnp.where(self.me == 1, 0, n_dp - 1)

    def peers(self, n_sp):
        me = lax.axis_index("sp")
        found = plane_peers(n_sp)
        for sp in range(n_sp):
            found.append((self.outer, {"sp": sp, "dp": self.inward}))
            found.append((self.hosts, {"sp": sp, "dp": self.guest}))
        far = jnp.logical_and(self.inner, self.me + 1 < self.n - 1)
        found.append((far, {"sp": me, "dp": self.me + 1}))
        far = jnp.logical_and(self.inner, self.me - 1 > 0)
        found.append((far, {"sp": me, "dp": self.me - 1}))
        return found

    def takes(self, trained, up):
        other = self.me + 1 if up else self.me - 1
        low, high = (1, self.n - 2) if trained else (0, self.n - 1)
        return jnp.logical_and(other >= low, other <= high)


class Weights:
    def __init__(self, planes, own, every, send, recv):
        self.planes, self.own, self.every = planes, own, every
        self.send, self.recv = send, recv

    def copy(self, array, index, up, source):
        other = self.planes.me + 1 if up else self.planes.me - 1
        return remote(
            source, self.every[array].at[index], self.send.at[int(up), array, index], self.recv.at[array, index],
            {"dp": other},
        )

    def begin(self, arrays, wanted):
        me = self.planes.me
        for array in arrays:
            for up in (True, False):

                @pl.when(jnp.logical_and(wanted, self.planes.takes(array < 2, up)))
                def _():
                    self.copy(array, me, up, self.own[array]).start()

    def pairs(self, array, distance):
        me, n = self.planes.me, self.planes.n
        used = self.planes.inner if array < 2 else True
        for up in (True, False):
            index = me - distance if up else me + distance
            comes = jnp.logical_and(used, jnp.logical_and(index >= 0, index < n))
            yield comes, jnp.logical_and(comes, self.planes.takes(array < 2, up)), jnp.clip(index, 0, n - 1), up

    def pass_on(self, arrays, distance, of_ends=None):
        for array in arrays:
            for comes, goes, index, up in self.pairs(array, distance):
                if of_ends is not None:
                    end = jnp.logical_or(index == 0, index == self.planes.n - 1)
                    chosen = end if of_ends else jnp.logical_not(end)
                    comes, goes = jnp.logical_and(comes, chosen), jnp.logical_and(goes, chosen)

                @pl.when(comes)
                def _():
                    place = self.every[array].at[index]
                    pltpu.make_async_copy(place, place, self.recv.at[array, index]).wait()

                @pl.when(goes)
                def _():
                    self.copy(array, index, up, self.every[array].at[index]).start()

    def finish(self):
        for array in range(4):
            for distance in range(self.planes.n):
                for _, goes, index, up in self.pairs(array, distance):
                    goes = goes if distance else self.planes.takes(array < 2, up)

                    @pl.when(goes)
                    def _():
                        self.copy(array, index, up, self.every[array].at[index]).wait_send()


ROWS = 256
LIMIT = 60 * 2**20


def gelu_parts(value):
    root = 0.7978845608028654
    square = value * value
    bent = jnp.tanh(root * value * (1.0 + 0.044715 * square))
    half = 0.5 + 0.5 * bent
    slope = half + 0.5 * value * (1.0 - bent * bent) * (root + 3.0 * 0.044715 * root * square)
    return value * half, slope


def slot_rows(lay, capacity, routes_t):
    n = lay.n
    experts, count = 2 * n, routes_t.shape[1]
    index = lax.broadcasted_iota(jnp.int32, (experts, count), 0)
    matches = [(index == routes_t[c : c + 1]).astype(F32) for c in range(2)]
    earlier = (
        lax.broadcasted_iota(jnp.int32, (count, count), 0) < lax.broadcasted_iota(jnp.int32, (count, count), 1)
    ).astype(F32)
    rank = dot((matches[0] + matches[1]).astype(BF16), earlier.astype(BF16))
    place = rank + (((index % n) * 2 + index // n) * capacity).astype(F32)
    return [jnp.sum(m * place, axis=0, keepdims=True).astype(jnp.int32) for m in matches]


def slot_columns(lay, capacity, routes):
    n = lay.n
    count = routes.shape[0]
    index = lax.broadcasted_iota(jnp.int32, (count, 128), 1)
    matches = [(index == routes[:, c : c + 1]).astype(F32) for c in range(2)]
    earlier = (
        lax.broadcasted_iota(jnp.int32, (count, count), 0) > lax.broadcasted_iota(jnp.int32, (count, count), 1)
    ).astype(F32)
    rank = dot(earlier.astype(BF16), (matches[0] + matches[1]).astype(BF16))
    place = rank + (((index % n) * 2 + index // n) * capacity).astype(F32)
    return [jnp.sum(m * place, axis=1, keepdims=True).astype(jnp.int32) for m in matches], matches


def hot(condition):
    return condition.astype(F32).astype(BF16)


def layer_kernel(
    lay, capacity, n_dp,
    tokens, vectors, w_qkv, w_out, w_router, routes, routes_t, cotangent, own_a, own_b, own_c, own_d,
    first_norm, unit, attended, log_total, home, middle, second_norm, gates_out, got, got_grad, first_grad, second_grad,
    all_a, all_b, all_c, all_d, hop_a, hop_b,
    staged_out, packed, packed_grad, rows_in, rows_grad, weight_a, weight_b, out_sum, in_sum, out_other, in_other, back_out, back_grad, grad_a, grad_b,
    packed_gates, rows_gates, send, recv, out_send, home_recv, local, stream_send, stream_recv, load,
    row_send, row_recv, row_local, back_send, back_recv, back_local, hop_send, hop_recv,
):
    n = lay.n
    me = lax.axis_index("sp")
    gain_one, shift_one, gain_two, shift_two = (vectors.at[i : i + 1] for i in range(4))
    planes = Planes(n_dp)
    is_short, seq, first_pair = lay.role(me)
    meet(planes.peers(n))
    stream = Weights(
        planes, (own_a, own_b, own_c, own_d), (all_a, all_b, all_c, all_d), stream_send, stream_recv
    )
    stream.begin((2, 3), True)

    hat, _ = normed(tokens[...].astype(F32))
    first_norm[...] = (hat * gain_one[...] + shift_one[...]).astype(BF16)
    started = []
    for chunk in range(9):
        kind, third = divmod(chunk, 3)
        made = dot(first_norm[...], w_qkv[:, chunk * 2 * WIDE : (chunk + 1) * 2 * WIDE]).astype(BF16)
        made = made * BF16(HEAD_DIM**-0.5) if kind == 0 else made
        area = packed.at[pl.ds(kind * tokens.shape[0], tokens.shape[0]), pl.ds(third * 2 * WIDE, 2 * WIDE)]
        area[...] = made
        count = len(lay.owners())
        started += to_owners(
            lay,
            me,
            lambda pair: (pair % 2) * WIDE,
            lambda number: chunk * count + number,
            area,
            lambda start, rows: unit.at[kind, pl.ds(pl.multiple_of(start, 16), rows)],
            send,
            recv.at[kind],
            local,
            (2 * third, 2 * third + 1),
        )
    span = n * capacity
    width, hidden = grad_a.shape
    count = tokens.shape[0]
    place = slot_rows(lay, capacity, routes_t[...])

    def dispatch_copies(which, kind):
        source, target = ((packed, rows_in), (packed_grad, rows_grad), (packed_gates, rows_gates))[which]
        plane = jnp.where(planes.outer, planes.inward, planes.me) if kind == 0 else planes.me
        area = jnp.where(planes.outer, 1, 0) if kind == 0 else 2

        def block(buffer, number):
            if which == 2:
                return buffer.at[number]
            return buffer.at[pl.ds(pl.multiple_of(number * capacity, 16), capacity)]

        into = block(target, area * n + me)
        for step in range(n):
            to = lax.rem(me + step, n)
            piece = block(source, to * 2 + kind)
            far = remote(
                piece, into, row_send.at[which, kind, step], row_recv.at[which, area, me], {"sp": to, "dp": plane}
            )
            if step:
                yield True, far
                continue
            if kind == 0:
                yield planes.outer, far
            stays = planes.inner if kind == 0 else True
            yield stays, pltpu.make_async_copy(piece, into, row_local.at[which, kind])

    def each(copies, act):
        for condition, copy in copies:
            if condition is True:
                act(copy)
            else:
                pl.when(condition)(functools.partial(act, copy))

    def start(copy):
        copy.start()

    def end(copy):
        if copy.is_remote:
            copy.wait_send()
        else:
            copy.wait()

    def dispatch(which):
        for kind in range(2):
            each(dispatch_copies(which, kind), start)

    for first in range(0, 2 * span, ROWS):
        slots = first + lax.broadcasted_iota(jnp.int32, (ROWS, count), 0)
        chosen = hot(jnp.logical_or(slots == place[0], slots == place[1]))
        packed_grad[first : first + ROWS] = dot(chosen, cotangent[...]).astype(BF16)
    dispatch(1)
    for kind in range(3):
        wait_unit(lay, is_short, unit.at[kind], recv.at[kind])
    keep = lanes_first()
    lower = causal(BLOCK)

    def task(index, carry):
        start, block = lay.task(is_short, index)
        base = pl.multiple_of(start + block * BLOCK, BLOCK)
        queries = halves(unit[0, pl.ds(base, BLOCK)])

        def visit(place, state, diagonal):
            keys = unit[1, pl.ds(place, BLOCK)]
            values = unit[2, pl.ds(place, BLOCK)]
            result = []
            for (peak, total, summed), query in zip(state, queries):
                scores = dot_t(query, keys)
                if diagonal:
                    scores = jnp.where(lower, scores, NEGATIVE)
                new_peak = jnp.maximum(peak, jnp.max(scores, axis=1, keepdims=True))
                factor = jnp.exp(peak - new_peak)
                weight = jnp.exp(scores - new_peak)
                total = total * factor + jnp.sum(weight, axis=1, keepdims=True)
                summed = summed * factor + dot(weight.astype(BF16), values)
                result.append((new_peak, total, summed))
            return tuple(result)

        empty = (jnp.full((BLOCK, 1), NEGATIVE, F32), jnp.zeros((BLOCK, 1), F32), jnp.zeros((BLOCK, WIDE), F32))
        state = lax.fori_loop(
            0, block, lambda j, state: visit(pl.multiple_of(start + j * BLOCK, BLOCK), state, False), (empty, empty)
        )
        (peak_a, total_a, summed_a), (peak_b, total_b, summed_b) = visit(base, state, True)
        result = jnp.where(keep, summed_a / total_a, summed_b / total_b)
        attended[pl.ds(base, BLOCK)] = result
        staged_out[pl.ds(base, BLOCK)] = result.astype(BF16)
        log_total[pl.ds(base, BLOCK)] = jnp.where(keep, peak_a + jnp.log(total_a), peak_b + jnp.log(total_b))
        send_home(
            lay, me, is_short, seq, first_pair, base, block, start, staged_out, home, 0, out_send, home_recv, local
        )
        return carry

    lax.fori_loop(0, lay.tasks(is_short), task, 0)
    finish_sends(me, started)
    wait_home(lay, is_short, staged_out, out_send, 1, True)
    wait_home(lay, is_short, staged_out, home_recv, 1, False)

    stream.pass_on((2, 3), 1)
    stream.begin((0, 1), planes.inner)
    x1 = tokens[...].astype(F32) + dot(home[...], w_out[...])
    middle[...] = x1
    hat, _ = normed(x1)
    second = (hat * gain_two[...] + shift_two[...]).astype(BF16)
    second_norm[...] = second
    for first in range(0, 2 * span, ROWS):
        slots = first + lax.broadcasted_iota(jnp.int32, (ROWS, count), 0)
        chosen = hot(jnp.logical_or(slots == place[0], slots == place[1]))
        packed[first : first + ROWS] = dot(chosen, second).astype(BF16)
    dispatch(0)
    logits = dot(second, w_router[...])
    index = lax.broadcasted_iota(jnp.int32, logits.shape, 1)
    chosen = [jnp.sum(jnp.where(index == routes[:, c : c + 1], logits, 0.0), axis=1, keepdims=True) for c in range(2)]
    top = jnp.maximum(chosen[0], chosen[1])
    exped = [jnp.exp(value - top) for value in chosen]
    gates = [value / (exped[0] + exped[1]) for value in exped]
    lane = lax.broadcasted_iota(jnp.int32, gates_out.shape, 1)
    gates_out[...] = jnp.where(lane == 0, gates[0], gates[1])
    column, _ = slot_columns(lay, capacity, routes[...])
    for number in range(2 * n):
        held = [
            jnp.where(jnp.logical_and(lane < capacity, lane + number * capacity == column[c]), gates[c], 0.0)
            for c in range(2)
        ]
        packed_gates[number] = jnp.broadcast_to(jnp.sum(held[0] + held[1], axis=0, keepdims=True), (8, 128))
    dispatch(2)

    def arrived(which, area):
        buffer = (rows_in, rows_grad, rows_gates)[which]
        for src in range(n):
            piece = buffer.at[area * n + src] if which == 2 else buffer.at[pl.ds((area * n + src) * capacity, capacity)]
            wait = pltpu.make_async_copy(piece, piece, row_recv.at[which, area, src]).wait
            if area == 1:
                wait()
            else:
                pl.when(src != me)(wait)

    for which in (1, 0, 2):
        for kind in range(2):
            each(dispatch_copies(which, kind), end)
    stream.begin((0, 1), planes.outer)
    stream.pass_on((2, 3), 2)

    def take(area):
        for which in (1, 0, 2):
            arrived(which, area)
        one = lax.broadcasted_iota(jnp.int32, (capacity, 128), 0) == lax.broadcasted_iota(jnp.int32, (capacity, 128), 1)

        def gated(src, carry):
            gate = jnp.sum(jnp.where(one, rows_gates[area * n + src, 0:1], 0.0), axis=1, keepdims=True)
            part = pl.ds(pl.multiple_of((area * n + src) * capacity, 16), capacity)
            rows_grad[part] = (gate * rows_grad[part].astype(F32)).astype(BF16)
            return carry

        lax.fori_loop(0, n, gated, 0)

    def clear(sums, rows):
        def one(index, carry):
            part = pl.ds(pl.multiple_of(index * ROWS, ROWS), ROWS)
            for total in sums:
                total[part] = jnp.zeros((ROWS, width), F32)
            return carry

        lax.fori_loop(0, rows // ROWS, one, 0)

    last = jnp.maximum(planes.me, n_dp - 1 - planes.me)

    def weight_grads(index):
        stores = [
            pltpu.make_async_copy(stage, whole.at[index], load.at[2 + i])
            for i, (stage, whole) in enumerate(((grad_a, first_grad), (grad_b, second_grad)))
        ]
        tall = 3 * WIDE
        for total in (span, 2 * span):

            @pl.when(planes.hosts == (total > span))
            def _():
                every_row = pl.ds(0, total)
                for col in range(0, width, tall):
                    part = pl.ds(col, tall)
                    grad_a[part] = t_dot(rows_in[every_row, part], packed_grad[every_row, :hidden]).astype(BF16)
                for col in range(0, hidden, tall):
                    part = pl.ds(col, tall)
                    grad_b[part] = t_dot(packed[every_row, part], rows_grad[every_row]).astype(BF16)

        for copy in stores:
            copy.start()
        for copy in stores:
            copy.wait()

    def work(trained, sums, first_row, base, rows, nearest, farthest, passing=True):
        arrays = (0, 1) if trained else (2, 3)
        every = (all_a, all_b) if trained else (all_c, all_d)
        own = (own_a, own_b) if trained else (own_c, own_d)

        def one(step, carry):
            distance, side = step // 2, lax.rem(step, 2)
            index = jnp.where(side == 0, planes.me - distance, planes.me + distance)
            real = jnp.logical_and(jnp.logical_and(index >= 0, index < n_dp), jnp.logical_or(side == 0, distance > 0))

            @pl.when(jnp.logical_and(passing, jnp.logical_and(side == 0, distance >= 3)))
            def _():
                stream.pass_on(arrays, distance)

            @pl.when(real)
            def _():
                near = [pltpu.make_async_copy(own[i], (weight_a, weight_b)[i], load.at[i]) for i in range(2)]
                far = [pltpu.make_async_copy(every[i].at[index], (weight_a, weight_b)[i], load.at[i]) for i in range(2)]

                @pl.when(distance == 0)
                def _():
                    for copy in near:
                        copy.start()

                @pl.when(distance > 0)
                def _():
                    for copy in far:
                        copy.start()

                for copy in near:
                    copy.wait()

                def chunk(number, carry):
                    part = pl.ds(pl.multiple_of(base + number * ROWS, ROWS), ROWS)
                    here = pl.ds(pl.multiple_of(first_row + number * ROWS, ROWS), ROWS)
                    active, slope = gelu_parts(dot(rows_in[here], weight_a[...]))
                    active = active.astype(BF16)
                    back = (dot_t(rows_grad[here], weight_b[...]) * slope).astype(BF16)
                    if trained:
                        packed[part, :hidden] = active
                        packed_grad[part, :hidden] = back
                    sums[0][part] += dot(active, weight_b[...])
                    sums[1][part] += dot_t(back, weight_a[...])
                    return carry

                lax.fori_loop(0, rows // ROWS, chunk, 0)
                if trained:

                    @pl.when(distance < last)
                    def _():
                        weight_grads(index)

            return carry

        lax.fori_loop(2 * nearest, 2 * farthest + 2, one, 0)

    def turn(sums, first_row, base, rows):
        def one(number, carry):
            part = pl.ds(pl.multiple_of(base + number * ROWS, ROWS), ROWS)
            here = pl.ds(pl.multiple_of(first_row + number * ROWS, ROWS), ROWS)
            back_out[here] = sums[0][part].astype(BF16)
            back_grad[here] = sums[1][part].astype(BF16)
            return carry

        lax.fori_loop(0, rows // ROWS, one, 0)

    def back_copies(kind, guest, whiches=(0, 1)):
        area = 2 if kind else int(guest)
        plane = planes.guest if guest else planes.me
        for which in whiches:
            source, target = ((back_out, got), (back_grad, got_grad))[which]
            into = target.at[pl.ds(pl.multiple_of((me * 2 + kind) * capacity, 16), capacity)]
            for step in range(n):
                to = lax.rem(me + step, n)
                piece = source.at[pl.ds(pl.multiple_of((area * n + to) * capacity, 16), capacity)]
                if step or guest:
                    yield True, remote(
                        piece, into, back_send.at[which, area, step], back_recv.at[which, kind, me], {"sp": to, "dp": plane}
                    )
                else:
                    yield True, pltpu.make_async_copy(piece, into, back_local.at[which, kind])

    def hops(act):
        for up in (True, False):
            for array, (whole, hop) in enumerate(((first_grad, hop_a), (second_grad, hop_b))):

                @pl.when(planes.me == (1 if up else n_dp - 2))
                def _():
                    act(
                        remote(
                            whole.at[2 if up else n_dp - 3], hop.at[int(up)], hop_send.at[int(up), array],
                            hop_recv.at[int(up), array], {"dp": planes.me + (1 if up else -1)},
                        )
                    )

    train_sums, frozen_sums = (out_sum, in_sum), (out_other, in_other)
    train_rows = jnp.where(planes.hosts, 2 * span, span)
    clear(frozen_sums, span)

    clear(train_sums, train_rows)

    @pl.when(planes.inner)
    def _():
        take(0)

        @pl.when(planes.hosts)
        def _():
            take(1)

        work(True, train_sums, 0, 0, train_rows, 0, 0)

    take(2)
    work(False, frozen_sums, 2 * span, 0, span, 0, 1)
    stream.pass_on((0, 1), 1, True)
    work(False, frozen_sums, 2 * span, 0, span, 2, n_dp - 1)
    turn(frozen_sums, 2 * span, 0, span)
    each(back_copies(1, False), start)

    @pl.when(planes.inner)
    def _():
        stream.pass_on((0, 1), 1, False)
        work(True, train_sums, 0, 0, train_rows, 1, 1)
        stream.pass_on((0, 1), 2)
        hops(start)
        work(True, train_sums, 0, 0, train_rows, 2, last - 1)

        @pl.when(planes.hosts)
        def _():
            work(True, train_sums, span, span, span, last, last)
            turn(train_sums, span, span, span)
            each(back_copies(0, True), start)

        work(True, train_sums, 0, 0, span, last, last, jnp.logical_not(planes.hosts))
        turn(train_sums, 0, 0, span)
        each(back_copies(0, False), start)
        weight_grads(jnp.where(planes.me > n_dp - 1 - planes.me, 0, n_dp - 1))

    each(back_copies(1, False), end)

    @pl.when(planes.inner)
    def _():
        each(back_copies(0, False), end)

        @pl.when(planes.hosts)
        def _():
            each(back_copies(0, True), end)

    for kind in range(2):
        for which, buffer in enumerate((got, got_grad)):
            for src in range(n):
                piece = buffer.at[pl.ds((src * 2 + kind) * capacity, capacity)]
                comes = jnp.logical_or(src != me, planes.outer) if kind == 0 else src != me
                pl.when(comes)(pltpu.make_async_copy(piece, piece, back_recv.at[which, kind, src]).wait)
    stream.finish()
    hops(end)
    for up in (True, False):
        for array, hop in enumerate((hop_a, hop_b)):

            @pl.when(planes.me == (2 if up else n_dp - 3))
            def _():
                pltpu.make_async_copy(hop.at[int(up)], hop.at[int(up)], hop_recv.at[int(up), array]).wait()


ANY = pl.BlockSpec(memory_space=pl.ANY)


def layer(lay, capacity, n_dp, tokens, vectors, w_qkv, w_out, w_router, routes, cotangent, weights):
    count, width = tokens.shape
    n = lay.n
    owners = len(lay.owners())
    span = n * capacity
    shape = jax.ShapeDtypeStruct
    hidden = weights[0].shape[1]
    every = [shape((n_dp, *weight.shape), BF16) for weight in weights]
    return pl.pallas_call(
        functools.partial(layer_kernel, lay, capacity, n_dp),
        out_shape=(
            shape((count, width), BF16),
            shape((3, UNIT, WIDE), BF16),
            shape((UNIT, WIDE), F32),
            shape((UNIT, WIDE), F32),
            shape((count, width), BF16),
            shape((count, width), F32),
            shape((count, width), BF16),
            shape((count, 128), F32),
            shape((2 * span, width), BF16),
            shape((2 * span, width), BF16),
            every[0],
            every[1],
            *every,
            shape((2, *weights[0].shape), BF16),
            shape((2, *weights[1].shape), BF16),
        ),
        in_specs=[VMEM] * 8 + [ANY] * 4,
        out_specs=[VMEM] * 8 + [ANY] * 10,
        scratch_shapes=[
            pltpu.VMEM((UNIT, WIDE), BF16),
            pltpu.VMEM((2 * span, width), BF16),
            pltpu.VMEM((2 * span, width), BF16),
            pltpu.VMEM((3 * span, width), BF16),
            pltpu.VMEM((3 * span, width), BF16),
            pltpu.VMEM((width, hidden), BF16),
            pltpu.VMEM((hidden, width), BF16),
            pltpu.VMEM((2 * span, width), F32),
            pltpu.VMEM((2 * span, width), F32),
            pltpu.VMEM((span, width), F32),
            pltpu.VMEM((span, width), F32),
            pltpu.VMEM((3 * span, width), BF16),
            pltpu.VMEM((3 * span, width), BF16),
            pltpu.VMEM((width, hidden), BF16),
            pltpu.VMEM((hidden, width), BF16),
            pltpu.VMEM((2 * n, 8, 128), F32),
            pltpu.VMEM((3 * n, 8, 128), F32),
            DMA((9 * owners,)),
            DMA((3,)),
            DMA,
            DMA,
            DMA,
            DMA((2, 4, n_dp)),
            DMA((4, n_dp)),
            DMA((4,)),
            DMA((3, 2, n)),
            DMA((3, 3, n)),
            DMA((3, 2)),
            DMA((2, 3, n)),
            DMA((2, 2, n)),
            DMA((2, 2)),
            DMA((2, 2)),
            DMA((2, 2)),
        ],
        compiler_params=pltpu.CompilerParams(collective_id=0, has_side_effects=True, vmem_limit_bytes=LIMIT),
        cost_estimate=pl.CostEstimate(flops=50 * 10**9, bytes_accessed=100 * 2**20, transcendentals=10**7),
        name="layer",
    )(
        tokens, vectors, w_qkv, w_out, w_router, routes, routes.T, cotangent, *weights
    )


class Sum:
    def __init__(self, n_sp, n_dp, pieces, quantum, needed, first):
        self.n_sp, self.n_dp = n_sp, n_dp
        self.bits = n_sp.bit_length() - 1
        unit = math.lcm(16 * n_sp * n_dp, quantum)
        units = -(-needed // unit)
        sizes = [first // unit] if first >= unit else []
        left = units - sum(sizes)
        pieces = min(pieces, left)
        sizes += [left // pieces + (p < left % pieces) for p in range(pieces)]
        self.pieces = [(unit * sum(sizes[:p]), unit * size) for p, size in enumerate(sizes)]
        self.early = first >= unit
        self.rows = unit * units
        self.steps = 2 * self.bits + 2

    def order(self, piece):
        later = list(range(1, self.bits))
        return [0] + (later[::-1] if piece % 2 else later)

    def landing(self):
        places, start = [], 0
        for _, rows in self.pieces:
            places.append([])
            for step in range(self.bits + 1):
                rows = rows // 2 if step < self.bits else rows
                places[-1].append((start, rows))
                start += rows
        return places, start

    def bind(self, mine, landed, whole, send, recv):
        self.mine, self.landed, self.whole, self.send, self.recv = mine, landed, whole, send, recv
        self.me, self.plane = lax.axis_index("sp"), lax.axis_index("dp")
        self.places, _ = self.landing()
        self.starts = [[start] for start, _ in self.pieces]
        for piece, (_, rows) in enumerate(self.pieces):
            for bit in self.order(piece):
                rows //= 2
                value = (self.me // (1 << bit)) % 2
                self.starts[piece].append(self.starts[piece][-1] + value * rows)

    def partner(self, bit):
        value = (self.me // (1 << bit)) % 2
        return self.me + (1 - 2 * value) * (1 << bit)

    def peers(self):
        found = [(True, {"sp": self.partner(bit)}) for bit in range(self.bits)]
        return found + [(True, {"dp": lax.rem(self.plane + step, self.n_dp)}) for step in range(1, self.n_dp)]

    def cut(self, start, rows):
        return pl.ds(pl.multiple_of(start, 16), rows)

    def copies(self, piece, step):
        bits = self.bits
        rows = self.pieces[piece][1]
        if step < bits or step > bits + 1:
            level = step if step < bits else 2 * bits + 1 - step
            bit = self.order(piece)[level]
            half = rows >> (level + 1)
            held, kept = self.starts[piece][level], self.starts[piece][level + 1]
            if step < bits:
                start, _ = self.places[piece][step]
                source = self.mine.at[self.cut(2 * held + half - kept, half)]
                target = self.landed.at[pl.ds(start, half)]
            else:
                source = target = self.whole.at[self.cut(kept, half)]
            yield remote(source, target, self.send.at[piece, step, 0], self.recv.at[piece, step, 0], self.partner(bit))
            return
        block = (rows >> bits) // self.n_dp
        base = self.starts[piece][bits]
        start, _ = self.places[piece][bits]
        for far in range(1, self.n_dp):
            other = lax.rem(self.plane + far, self.n_dp)
            if step == bits:
                source = self.mine.at[self.cut(base + other * block, block)]
                target = self.landed.at[self.cut(start + self.plane * block, block)]
            else:
                source = target = self.whole.at[self.cut(base + self.plane * block, block)]
            yield remote(source, target, self.send.at[piece, step, far], self.recv.at[piece, step, far], {"dp": other})

    def start(self, piece, step):
        for copy in self.copies(piece, step):
            copy.start()

    def add(self, piece, step):
        for copy in self.copies(piece, step):
            copy.wait()
        bits, rows = self.bits, self.pieces[piece][1]
        if step > bits:
            return
        start, _ = self.places[piece][step]
        if step < bits:
            size, kept = rows >> (step + 1), self.starts[piece][step + 1]
            for first, count in blocks(size):

                def one(number, carry):
                    part = self.cut(kept + first + number * count[0], count[0])
                    here = self.cut(start + first + number * count[0], count[0])
                    self.mine[part] = (self.mine[part].astype(F32) + self.landed[here].astype(F32)).astype(BF16)
                    return carry

                lax.fori_loop(0, count[1], one, 0)
            return
        block = (rows >> bits) // self.n_dp
        own = self.cut(self.starts[piece][bits] + self.plane * block, block)
        total = self.mine[own].astype(F32)
        for far in range(1, self.n_dp):
            other = lax.rem(self.plane + far, self.n_dp)
            total = total + self.landed[self.cut(start + other * block, block)].astype(F32)
        self.whole[own] = total.astype(BF16)


def blocks(rows, size=512):
    found = []
    if rows >= size:
        found.append((0, (size, rows // size)))
    if rows % size:
        found.append((rows - rows % size, (rows % size, 1)))
    return found


def run_sum(total, ahead, ready, done, between):
    begun = [-(piece // 2) for piece in range(len(total.pieces) - total.early)]
    begun = [ahead] * total.early + begun
    rounds = 0
    while any(step <= total.steps for step in begun):
        for piece, step in enumerate(begun):
            if 0 < step <= total.steps:
                total.add(piece, step - 1)
                if step == total.steps:
                    done(piece)
            if step == 0:
                ready(piece)
            if 0 <= step < total.steps:
                total.start(piece, step)
            begun[piece] += 1
        between(rounds)
        rounds += 1


class Gather:
    def __init__(self, n, own, hop, below, above, theirs, sums, stage, send, recv, load):
        self.n, self.own, self.hop, self.below, self.above, self.stage = n, own, hop, below, above, stage
        self.theirs, self.sums, self.send, self.recv, self.load = theirs, sums, send, recv, load
        self.me = lax.axis_index("dp")
        self.inner = jnp.logical_and(self.me >= 1, self.me <= n - 2)

    def copy(self, array, index, up, source):
        target = (self.below if up else self.above)[array].at[index]
        other = self.me + 1 if up else self.me - 1
        return remote(
            source, target, self.send.at[int(up), array, index], self.recv.at[int(up), array, index], {"dp": other}
        )

    def fetch(self, source, buffer, number):
        moved = pltpu.make_async_copy(source, buffer, self.load.at[number])
        moved.start()
        return moved

    def wanted(self, index, up):
        return jnp.logical_and(self.inner, index > self.me if up else index < self.me)

    def begins(self, up):
        return self.me == 1 if up else self.me == self.n - 2

    def hopped(self, index, up):
        return index == (2 if up else self.n - 3)

    def begin(self, array, index, up):
        if self.hopped(index, up):
            return

        @pl.when(jnp.logical_and(self.wanted(index, up), self.begins(up)))
        def _():
            self.copy(array, index, up, self.own[array].at[index]).start()

    def came(self, array, index, up):
        buffer = (self.below if up else self.above)[array].at[index]
        pltpu.make_async_copy(buffer, buffer, self.recv.at[int(up), array, index]).wait()
        return buffer

    def pass_on(self, array, index, up):
        @pl.when(jnp.logical_and(self.wanted(index, up), jnp.logical_not(self.begins(up))))
        def _():
            total, theirs = self.sums[array].at[int(up)], self.theirs[array]
            here = self.fetch(self.own[array].at[index], total, 0)
            self.fetch(self.came(array, index, up), theirs, 1).wait()
            here.wait()
            total[...] = (total[...].astype(F32) + theirs[...].astype(F32)).astype(BF16)
            self.copy(array, index, up, total).start()

    def finish(self, array, index, up):
        waits = self.wanted(index, up)
        if self.hopped(index, up):
            waits = jnp.logical_and(waits, jnp.logical_not(self.begins(up)))

        @pl.when(waits)
        def _():
            self.copy(array, index, up, self.sums[array].at[int(up)]).wait_send()

    def total(self, array, out):
        theirs = self.theirs[array]

        @pl.when(self.inner)
        def _():
            self.fetch(self.own[array].at[self.me], theirs, 0).wait()

        @pl.when(jnp.logical_not(self.inner))
        def _():
            theirs[...] = jnp.zeros_like(theirs)

        sides = ((True, self.me >= 2), (False, self.me <= self.n - 3))
        for up, comes in sides:

            near = self.me == (2 if up else self.n - 3)

            @pl.when(jnp.logical_and(comes, near))
            def _():
                self.fetch(self.hop[array].at[int(up)], self.sums[array].at[int(up)], 1).wait()

            @pl.when(jnp.logical_and(comes, jnp.logical_not(near)))
            def _():
                self.fetch(self.came(array, self.me, up), self.sums[array].at[int(up)], 1).wait()

        rows, lanes = out.shape
        stores = []
        for number in range(lanes // WIDE):
            part = pl.ds(number * WIDE, WIDE)
            stage = self.stage.at[number % 2, pl.ds(0, rows), pl.ds(0, WIDE)]
            if number >= 2:
                stores[number - 2].wait()
            stage[...] = theirs[:, part].astype(F32)
            for up, comes in sides:

                @pl.when(comes)
                def _():
                    stage[...] += self.sums[array][int(up), :, part].astype(F32)

            stores.append(pltpu.make_async_copy(stage, out.at[:, part], self.load.at[3 + number % 2]))
            stores[number].start()
        for store in stores[-2:]:
            store.wait()


def gather_scratch(n, first, second):
    shapes = [first.shape[1:], second.shape[1:]]
    return [
        *(pltpu.VMEM(shape, BF16) for shape in shapes),
        *(pltpu.VMEM((2, *shape), BF16) for shape in shapes),
        DMA((2, 2, n)),
        DMA((2, 2, n)),
        DMA((5,)),
    ]


def back_kernel(
    lay, capacity, replicated,
    got, got_grad, middle, second_norm, gates, home_out, w_out, vectors, w_router, routes, cotangent,
    unit, attended, log_total, first_norm, tokens, w_qkv, first_own, second_own, hop_a, hop_b,
    block_out, tokens_grad, qkv_grad, out_proj_grad, router_out, vectors_out, first_total, second_total, below_a, below_b, above_a, above_b,
    grad_attended, grad_out, deltas, query_sum, staged, home, send, recv, out_send, home_recv, local,
    theirs_a, theirs_b, sums_a, sums_b, pass_send, pass_recv, load,
    grads, landed, summed, stage, sum_send, sum_recv, out_sems,
):
    n_dp = first_own.shape[0]
    gather = Gather(
        n_dp, (first_own, second_own), (hop_a, hop_b), (below_a, below_b), (above_a, above_b), (theirs_a, theirs_b),
        (sums_a, sums_b), stage, pass_send, pass_recv, load,
    )
    gain_one, gain_two = vectors.at[0:1], vectors.at[2:3]
    replicated.bind(grads, landed, summed, sum_send, sum_recv)
    me = lax.axis_index("sp")
    is_short, seq, first_pair = lay.role(me)
    everywhere = [(True, {"dp": lax.rem(gather.me + step, n_dp)}) for step in range(1, n_dp)]
    meet(plane_peers(lay.n) + everywhere)
    kept = pltpu.make_async_copy(attended, deltas, load.at[2])
    kept.start()
    inside = [(up, index) for index in range(1, n_dp - 1) for up in (True, False)]
    ends = [(True, n_dp - 1), (False, 0)]
    for up, index in ends:
        gather.begin(0, index, up)
    place, matches = slot_columns(lay, capacity, routes[...])
    slots = lax.broadcasted_iota(jnp.int32, (tokens.shape[0], got.shape[0]), 1)
    chosen = [hot(slots == place[c]) for c in range(2)]
    upstream = cotangent[...].astype(F32)
    gate = [gates[:, c : c + 1] for c in range(2)]
    total = middle[...]
    grad_gate = []
    for c in range(2):
        produced = dot(chosen[c], got[...])
        total = total + gate[c] * produced
        grad_gate.append(jnp.sum(upstream * produced, axis=1, keepdims=True))
    block_out[...] = total.astype(BF16)
    mean_grad = gate[0] * grad_gate[0] + gate[1] * grad_gate[1]
    grad_logits = sum(matches[c] * (gate[c] * (grad_gate[c] - mean_grad)) for c in range(2))
    high = grad_logits.astype(BF16)
    low = (grad_logits - high.astype(F32)).astype(BF16)
    router_grad = t_dot(second_norm[...], high) + t_dot(second_norm[...], low)
    grad_second = dot_t(high, w_router[...]) + dot_t(low, w_router[...])
    grad_second = grad_second + dot(chosen[0] + chosen[1], got_grad[...])
    hat, scale = normed(middle[...])
    gain_two_grad = jnp.sum(grad_second * hat, axis=0, keepdims=True)
    shift_two_grad = jnp.sum(grad_second, axis=0, keepdims=True)
    grad = upstream + norm_back(grad_second, gain_two[...], hat, scale)
    tokens_grad[...] = grad
    branch = grad.astype(BF16)
    grad_attended[...] = dot_t(branch, w_out[...]).astype(BF16)
    out_proj = t_dot(home_out[...], branch)
    width = w_out.shape[0]

    def put(column, value):
        for lane in range(0, value.shape[1], WIDE):
            grads[pl.ds((column + lane) // WIDE * width, width)] = value[:, lane : lane + WIDE].astype(BF16)

    put(0, out_proj)
    moments = (1, 2, 3, 5, 7)
    if replicated.early:
        replicated.start(0, 0)
    started = to_owners(
        lay,
        me,
        lambda pair: pair * WIDE,
        lambda number: number,
        grad_attended,
        lambda start, rows: grad_out.at[pl.ds(pl.multiple_of(start, 16), rows)],
        send,
        recv,
        local,
        range(PAIRS),
    )
    for up, index in ends:
        gather.begin(1, index, up)
    query_sum[...] = jnp.zeros_like(query_sum)
    keep = lanes_first()
    lower = causal(BLOCK)
    wait_unit(lay, is_short, grad_out, recv)
    kept.wait()

    def make_delta(index, carry):
        part = pl.ds(pl.multiple_of(index * BLOCK, BLOCK), BLOCK)
        first, second = halves(grad_out[part].astype(F32) * deltas[part])
        deltas[part] = jnp.where(
            keep, jnp.sum(first, axis=1, keepdims=True), jnp.sum(second, axis=1, keepdims=True)
        )
        return carry

    lax.fori_loop(0, lay.tasks(is_short), make_delta, 0)
    per = jnp.where(is_short, LEN_A // BLOCK, LEN_B // BLOCK)

    def task(index, carry):
        start, block = lay.task(is_short, index)
        base = pl.multiple_of(start + block * BLOCK, BLOCK)
        keys = unit[1, pl.ds(base, BLOCK)]
        values = unit[2, pl.ds(base, BLOCK)]
        key_both = jnp.concatenate(halves(keys), axis=0)

        def visit(place, state, diagonal):
            part = pl.ds(place, BLOCK)
            grad_key, grad_value = state
            queries = halves(unit[0, part])
            outs = halves(grad_out[part])
            weights, grads = [], []
            for which, (query, out) in enumerate(zip(queries, outs)):
                column = which * HEAD_DIM
                scores = dot_t(query, keys)
                if diagonal:
                    scores = jnp.where(lower, scores, NEGATIVE)
                weight = jnp.exp(scores - log_total[part, column : column + 1])
                grad = weight * (dot_t(out, values) - deltas[part, column : column + 1])
                weights.append(weight.astype(BF16))
                grads.append(grad.astype(BF16))
            grad_value = grad_value + t_dot(jnp.concatenate(weights, axis=0), jnp.concatenate(outs, axis=0))
            grad_key = grad_key + t_dot(jnp.concatenate(grads, axis=0), jnp.concatenate(queries, axis=0))
            query_sum[part] += dot(jnp.concatenate(grads, axis=1), key_both)
            return grad_key, grad_value

        zero = jnp.zeros((BLOCK, WIDE), F32)
        state = visit(base, (zero, zero), True)
        grad_key, grad_value = lax.fori_loop(
            block + 1, per, lambda i, state: visit(pl.multiple_of(start + i * BLOCK, BLOCK), state, False), state
        )
        part = pl.ds(base, BLOCK)
        staged[0, part] = (query_sum[part] * HEAD_DIM**-0.5).astype(BF16)
        staged[1, part] = grad_key.astype(BF16)
        staged[2, part] = grad_value.astype(BF16)
        for kind in range(3):
            send_home(
                lay, me, is_short, seq, first_pair, base, block, start, staged.at[kind], home, kind * PAIRS * WIDE,
                out_send.at[kind], home_recv.at[kind], local,
            )
        @pl.when(index == 1)
        def _():
            for up, which in ends:
                gather.pass_on(0, which, up)

        for step, moment in enumerate(moments if replicated.early else ()):

            @pl.when(index == moment)
            def _():
                replicated.add(0, step)
                replicated.start(0, step + 1)

        return carry

    lax.fori_loop(0, lay.tasks(is_short), task, 0)
    for up, index in ends:
        gather.pass_on(1, index, up)
    for array in range(2):
        for up, index in inside:
            gather.begin(array, index, up)
    for kind in range(3):
        wait_home(lay, is_short, staged.at[kind], home_recv.at[kind], 1, False)
    grad_first = dot_t(home[...], w_qkv[...])
    hat, scale = normed(tokens[...].astype(F32))
    gain_one_grad = jnp.sum(grad_first * hat, axis=0, keepdims=True)
    shift_one_grad = jnp.sum(grad_first, axis=0, keepdims=True)
    tokens_grad[...] += norm_back(grad_first, gain_one[...], hat, scale)
    parts = (gain_one_grad, shift_one_grad, gain_two_grad, shift_two_grad)
    grads[pl.ds(width // WIDE * width, width)] = router_grad.astype(BF16)
    rows = [part[:, lane : lane + WIDE] for part in parts for lane in range(0, width, WIDE)]
    rows.append(jnp.zeros((width - len(rows), WIDE), F32))
    grads[pl.ds(7 * width, width)] = jnp.concatenate(rows, axis=0).astype(BF16)
    first = 8
    last = first + 3 * PAIRS
    for spare in range(last, replicated.rows // width):
        grads[pl.ds(spare * width, width)] = jnp.zeros((width, WIDE), BF16)

    def ready(piece):
        start, rows = replicated.pieces[piece]
        for column in range(start // width, (start + rows) // width, 2):
            if first <= column < last:
                lanes = pl.ds((column - first) * WIDE, 2 * WIDE)
                put(column * WIDE, t_dot(first_norm[...], home[:, lanes]))

    stores = []

    def done(piece):
        start, rows = replicated.pieces[piece]
        for column in range(start // width, (start + rows) // width, 2):
            parts = [summed.at[pl.ds((column + i) * width, width)] for i in range(2)]
            if column == 6:
                router_out[...] = parts[0][...].astype(F32)
                vectors_out[...] = parts[1][0:32].astype(F32)
            elif column < last:
                for i in range(2):
                    target, lane = (out_proj_grad, column) if column < 6 else (qkv_grad, column - first)
                    lanes = pl.ds((lane + i) * WIDE, WIDE)
                    stores.append(pltpu.make_async_copy(parts[i], target.at[:, lanes], out_sems.at[len(stores)]))
                    stores[-1].start()

    def between(number):
        if number in (5, 6):
            array = number - 5
            for up, index in inside:
                gather.pass_on(array, index, up)
            for up, index in inside + ends:
                gather.finish(array, index, up)
            gather.total(array, (first_total, second_total)[array])

    run_sum(replicated, len(moments) + 1, ready, done, between)
    for store in stores:
        store.wait()
    finish_sends(me, started)
    for kind in range(3):
        wait_home(lay, is_short, staged.at[kind], out_send.at[kind], 1, True)


def backward(lay, capacity, values):
    count, width = values[2].shape
    owners = len(lay.owners())
    shape = jax.ShapeDtypeStruct
    slices = values[-4:-2]
    replicated = Sum(lay.n, slices[0].shape[0], 6, 2 * width, 26 * width, width // WIDE * width)
    return pl.pallas_call(
        functools.partial(back_kernel, lay, capacity, replicated),
        out_shape=(
            shape((count, width), BF16), shape((count, width), F32),
            shape((width, 3 * width), BF16), shape((width, width), BF16), shape((width, WIDE), F32), shape((32, WIDE), F32),
            *(shape(g.shape[1:], F32) for g in slices), *(shape(g.shape, BF16) for g in slices * 2),
        ),
        in_specs=[VMEM] * 12 + [ANY] + [VMEM] * 4 + [ANY] * 4,
        out_specs=[VMEM] * 2 + [ANY] * 2 + [VMEM] * 2 + [ANY] * 6,
        scratch_shapes=[
            pltpu.VMEM((count, width), BF16),
            pltpu.VMEM((UNIT, WIDE), BF16),
            pltpu.VMEM((UNIT, WIDE), F32),
            pltpu.VMEM((UNIT, WIDE), F32),
            pltpu.VMEM((3, UNIT, WIDE), BF16),
            pltpu.VMEM((count, 3 * width), BF16),
            DMA((owners,)),
            DMA,
            DMA((3,)),
            DMA((3,)),
            DMA,
            *gather_scratch(slices[0].shape[0], *slices),
            pltpu.VMEM((replicated.rows, WIDE), BF16),
            pltpu.VMEM((replicated.landing()[1], WIDE), BF16),
            pltpu.VMEM((replicated.rows, WIDE), BF16),
            pltpu.VMEM((2, width, WIDE), F32),
            DMA((len(replicated.pieces), replicated.steps, slices[0].shape[0])),
            DMA((len(replicated.pieces), replicated.steps, slices[0].shape[0])),
            DMA((4 * PAIRS,)),
        ],
        compiler_params=pltpu.CompilerParams(collective_id=1, has_side_effects=True, vmem_limit_bytes=LIMIT),
        cost_estimate=pl.CostEstimate(flops=16 * 10**9, bytes_accessed=60 * 2**20, transcendentals=5 * 10**6),
        name="backward",
    )(*values)


def shards(
    tokens, ln1_gain, ln1_shift, w_qkv, w_out, ln2_gain, ln2_shift, w_router,
    train_w1, train_w2, frozen_w1, frozen_w2, routes, cotangent,
):
    lay = Layout(lax.axis_size("sp"))
    n_dp = lax.axis_size("dp")
    tokens, routes, cotangent = tokens[0], routes[0], cotangent[0]
    count, width = tokens.shape
    capacity = 2 * count // lay.n
    experts = w_router.shape[1]
    router_wide = jnp.pad(w_router, ((0, 0), (0, 128 - experts)))
    vectors = jnp.stack([ln1_gain, ln1_shift, ln2_gain, ln2_shift])
    weights = [weight[0] for weight in (train_w1, train_w2, frozen_w1, frozen_w2)]
    (
        first_norm, unit, attended, log_total, home, middle, second, gates, got, got_grad, first_grad, second_grad,
        _, _, _, _, hop_a, hop_b,
    ) = layer(lay, capacity, n_dp, tokens, vectors, w_qkv, w_out, router_wide, routes, cotangent, weights)
    block_out, tokens_grad, qkv_grad, out_proj, router, vector_rows, first_total, second_total, *_ = backward(
        lay, capacity,
        (
            got, got_grad, middle, second, gates, home, w_out, vectors, router_wide, routes, cotangent,
            unit, attended, log_total, first_norm, tokens, w_qkv, first_grad, second_grad, hop_a, hop_b,
        ),
    )
    found = vector_rows[: 4 * width // WIDE].reshape(4, width)
    return (
        block_out[None],
        tokens_grad[None],
        found[0],
        found[1],
        qkv_grad.astype(F32),
        out_proj.astype(F32),
        found[2],
        found[3],
        router[:, :experts],
        first_total[None],
        second_total[None],
    )


def solution(mesh):
    in_specs = (
        P("dp", "sp", None), P(), P(), P(), P(), P(), P(), P(),
        P("sp", None, "dp"), P("sp", "dp", None), P("sp", None, "dp"), P("sp", "dp", None),
        P("dp", "sp", None), P("dp", "sp", None),
    )
    out_specs = (
        P("dp", "sp", None), P("dp", "sp", None), P(), P(), P(), P(), P(), P(), P(),
        P("sp", None, "dp"), P("sp", "dp", None),
    )
    return jax.shard_map(shards, mesh=mesh, in_specs=in_specs, out_specs=out_specs, check_vma=False)
```

```python
import functools
import math

import jax
import jax.numpy as jnp
from jax import lax
from jax.experimental import pallas as pl
from jax.experimental.pallas import tpu as pltpu
from jax.sharding import PartitionSpec as P

HEADS = 12
HEAD_DIM = 64
LEN_A = 1024
LEN_B = 2048
PAIRS = HEADS // 2
WIDE = 2 * HEAD_DIM
UNIT = 3 * LEN_A
BLOCK = 256
EPSILON = 1e-05
NEGATIVE = -1e30
MESH = pl.DeviceIdType.MESH
DMA = pltpu.SemaphoreType.DMA
F32 = jnp.float32
BF16 = jnp.bfloat16
VMEM = pl.BlockSpec(memory_space=pltpu.VMEM)


def dot(a, b):
    return jnp.dot(a, b, preferred_element_type=F32)


def dot_t(a, b):
    return lax.dot_general(a, b, (((1,), (1,)), ((), ())), preferred_element_type=F32)


def t_dot(a, b):
    return lax.dot_general(a, b, (((0,), (0,)), ((), ())), preferred_element_type=F32)


def normed(value):
    centre = jnp.mean(value, axis=-1, keepdims=True)
    centred = value - centre
    spread = jnp.mean(centred * centred, axis=-1, keepdims=True)
    scale = lax.rsqrt(spread + EPSILON)
    return centred * scale, scale


def norm_back(grad, gain, hat, scale):
    scaled = grad * gain
    first = jnp.mean(scaled, axis=-1, keepdims=True)
    second = jnp.mean(scaled * hat, axis=-1, keepdims=True)
    return (scaled - first - hat * second) * scale


class Layout:
    def __init__(self, n_sp):
        self.n = n_sp
        self.sequences = n_sp // 8
        self.short = LEN_A // n_sp
        self.long = LEN_B // n_sp
        self.split = self.sequences * self.short

    def owners(self):
        found = []
        for seq in range(self.sequences):
            for pair in range(PAIRS):
                number = seq * PAIRS + pair
                found.append((number + number // 3 + 1, True, self.split + seq * self.long, self.long, pair, 0))
                found.append((4 * (seq * 2 + pair // 3), False, seq * self.short, self.short, pair, (pair % 3) * LEN_A))
        return found

    def role(self, me):
        is_short = lax.rem(me, 4) == 0
        number = me - me // 4 - 1
        group = me // 4
        seq = jnp.where(is_short, group // 2, number // PAIRS)
        pair = jnp.where(is_short, 3 * lax.rem(group, 2), lax.rem(number, PAIRS))
        return is_short, seq, pair

    def task(self, is_short, index):
        per = LEN_A // BLOCK
        start = jnp.where(is_short, (index // per) * LEN_A, 0)
        block = jnp.where(is_short, lax.rem(index, per), index)
        return pl.multiple_of(start, BLOCK), block

    def tasks(self, is_short):
        return jnp.where(is_short, 3 * LEN_A // BLOCK, LEN_B // BLOCK)


def meet(peers):
    barrier = pltpu.get_barrier_semaphore()
    for wanted, device in peers:

        @pl.when(wanted)
        def _():
            pl.semaphore_signal(barrier, inc=1, device_id=device, device_id_type=MESH)

    pl.semaphore_wait(barrier, sum(jnp.asarray(wanted, jnp.int32) for wanted, _ in peers))


def plane_peers(n):
    me = lax.axis_index("sp")
    return [(True, {"sp": lax.rem(me + step, n)}) for step in range(1, n)]


def remote(source, target, send_sem, recv_sem, device):
    device = device if isinstance(device, dict) else {"sp": device}
    return pltpu.make_async_remote_copy(
        src_ref=source, dst_ref=target, send_sem=send_sem, recv_sem=recv_sem, device_id=device, device_id_type=MESH
    )


def lanes_first():
    return lax.broadcasted_iota(jnp.int32, (1, WIDE), 1) < HEAD_DIM


def halves(value):
    keep = lanes_first()
    zero = jnp.zeros_like(value)
    return jnp.where(keep, value, zero), jnp.where(keep, zero, value)


def causal(rows):
    return lax.broadcasted_iota(jnp.int32, (rows, rows), 0) >= lax.broadcasted_iota(jnp.int32, (rows, rows), 1)


def to_owners(lay, me, cols, slot, source, target, send_sems, recv_sem, local_sem, wanted):
    started = []
    for number, (owner, is_long, start, rows, pair, unit) in enumerate(lay.owners()):
        if pair not in wanted:
            continue
        piece = source.at[pl.ds(start, rows), pl.ds(cols(pair), WIDE)]
        place = target(unit + me * rows, rows)
        far = remote(piece, place, send_sems.at[slot(number)], recv_sem, owner)
        near = pltpu.make_async_copy(piece, place, local_sem)

        @pl.when(me != owner)
        def _():
            far.start()

        @pl.when(me == owner)
        def _():
            near.start()
            near.wait()

        started.append((owner, far))
    return started


def finish_sends(me, started):
    for owner, copy in started:

        @pl.when(me != owner)
        def _():
            copy.wait_send()


def wait_unit(lay, is_short, buffer, sem):
    for short, rows in ((True, 3 * (lay.n - 1) * lay.short), (False, (lay.n - 1) * lay.long)):

        @pl.when(is_short == short)
        def _():
            piece = buffer.at[pl.ds(0, rows)]
            pltpu.make_async_copy(piece, piece, sem).wait()


def send_home(lay, me, is_short, seq, first_pair, base, block, unit_start, source, target, base_col, send_sem, recv_sem, local_sem):
    for short, rows in ((True, lay.short), (False, lay.long)):

        @pl.when(is_short == short)
        def _():
            pair = first_pair + (unit_start // LEN_A if short else 0)
            column = pl.multiple_of(base_col + pair * WIDE, WIDE)
            first = pl.multiple_of(seq * rows + (0 if short else lay.split), 16)
            for part in range(BLOCK // rows):
                home = block * (BLOCK // rows) + part
                piece = source.at[pl.ds(pl.multiple_of(base + part * rows, 16), rows)]
                place = target.at[pl.ds(first, rows), pl.ds(column, WIDE)]

                @pl.when(home != me)
                def _():
                    remote(piece, place, send_sem, recv_sem, home).start()

                @pl.when(home == me)
                def _():
                    near = pltpu.make_async_copy(piece, place, local_sem)
                    near.start()
                    near.wait()


def wait_home(lay, is_short, scratch, sem, tensors, sent):
    for short in (True, False):
        own = 3 * lay.short if short else lay.long
        if sent:
            rows = (3 * LEN_A if short else LEN_B) - own
        else:
            rows = PAIRS * lay.sequences * (lay.short + lay.long) - own

        @pl.when(is_short == short)
        def _():
            for _ in range(tensors):
                piece = scratch.at[pl.ds(0, rows)]
                pltpu.make_async_copy(piece, piece, sem).wait()


class Planes:
    def __init__(self, n_dp):
        self.n = n_dp
        self.me = lax.axis_index("dp")
        self.outer = jnp.logical_or(self.me == 0, self.me == n_dp - 1)
        self.inner = jnp.logical_not(self.outer)
        self.inward = jnp.where(self.me == 0, 1, n_dp - 2)
        self.hosts = jnp.logical_or(self.me == 1, self.me == n_dp - 2)
        self.guest = jnp.where(self.me == 1, 0, n_dp - 1)

    def peers(self, n_sp):
        me = lax.axis_index("sp")
        found = plane_peers(n_sp)
        for sp in range(n_sp):
            found.append((self.outer, {"sp": sp, "dp": self.inward}))
            found.append((self.hosts, {"sp": sp, "dp": self.guest}))
        far = jnp.logical_and(self.inner, self.me + 1 < self.n - 1)
        found.append((far, {"sp": me, "dp": self.me + 1}))
        far = jnp.logical_and(self.inner, self.me - 1 > 0)
        found.append((far, {"sp": me, "dp": self.me - 1}))
        return found

    def takes(self, trained, up):
        other = self.me + 1 if up else self.me - 1
        low, high = (1, self.n - 2) if trained else (0, self.n - 1)
        return jnp.logical_and(other >= low, other <= high)


class Weights:
    def __init__(self, planes, own, every, send, recv):
        self.planes, self.own, self.every = planes, own, every
        self.send, self.recv = send, recv

    def copy(self, array, index, up, source):
        other = self.planes.me + 1 if up else self.planes.me - 1
        return remote(
            source, self.every[array].at[index], self.send.at[int(up), array, index], self.recv.at[array, index],
            {"dp": other},
        )

    def begin(self, arrays, wanted):
        me = self.planes.me
        for array in arrays:
            for up in (True, False):

                @pl.when(jnp.logical_and(wanted, self.planes.takes(array < 2, up)))
                def _():
                    self.copy(array, me, up, self.own[array]).start()

    def pairs(self, array, distance):
        me, n = self.planes.me, self.planes.n
        used = self.planes.inner if array < 2 else True
        for up in (True, False):
            index = me - distance if up else me + distance
            comes = jnp.logical_and(used, jnp.logical_and(index >= 0, index < n))
            yield comes, jnp.logical_and(comes, self.planes.takes(array < 2, up)), jnp.clip(index, 0, n - 1), up

    def pass_on(self, arrays, distance, of_ends=None):
        for array in arrays:
            for comes, goes, index, up in self.pairs(array, distance):
                if of_ends is not None:
                    end = jnp.logical_or(index == 0, index == self.planes.n - 1)
                    chosen = end if of_ends else jnp.logical_not(end)
                    comes, goes = jnp.logical_and(comes, chosen), jnp.logical_and(goes, chosen)

                @pl.when(comes)
                def _():
                    place = self.every[array].at[index]
                    pltpu.make_async_copy(place, place, self.recv.at[array, index]).wait()

                @pl.when(goes)
                def _():
                    self.copy(array, index, up, self.every[array].at[index]).start()

    def finish(self):
        for array in range(4):
            for distance in range(self.planes.n):
                for _, goes, index, up in self.pairs(array, distance):
                    goes = goes if distance else self.planes.takes(array < 2, up)

                    @pl.when(goes)
                    def _():
                        self.copy(array, index, up, self.every[array].at[index]).wait_send()


ROWS = 256
LIMIT = 60 * 2**20


def gelu_parts(value):
    root = 0.7978845608028654
    square = value * value
    bent = jnp.tanh(root * value * (1.0 + 0.044715 * square))
    half = 0.5 + 0.5 * bent
    slope = half + 0.5 * value * (1.0 - bent * bent) * (root + 3.0 * 0.044715 * root * square)
    return value * half, slope


def slot_rows(lay, capacity, routes_t):
    n = lay.n
    experts, count = 2 * n, routes_t.shape[1]
    index = lax.broadcasted_iota(jnp.int32, (experts, count), 0)
    matches = [(index == routes_t[c : c + 1]).astype(F32) for c in range(2)]
    earlier = (
        lax.broadcasted_iota(jnp.int32, (count, count), 0) < lax.broadcasted_iota(jnp.int32, (count, count), 1)
    ).astype(F32)
    rank = dot((matches[0] + matches[1]).astype(BF16), earlier.astype(BF16))
    place = rank + (((index % n) * 2 + index // n) * capacity).astype(F32)
    return [jnp.sum(m * place, axis=0, keepdims=True).astype(jnp.int32) for m in matches]


def upright(routes_t):
    tall = jnp.concatenate([routes_t.astype(F32), jnp.zeros((WIDE - 2, routes_t.shape[1]), F32)], axis=0)
    return jnp.transpose(tall).astype(jnp.int32)


def slot_columns(lay, capacity, routes):
    n = lay.n
    count = routes.shape[0]
    index = lax.broadcasted_iota(jnp.int32, (count, 128), 1)
    matches = [(index == routes[:, c : c + 1]).astype(F32) for c in range(2)]
    earlier = (
        lax.broadcasted_iota(jnp.int32, (count, count), 0) > lax.broadcasted_iota(jnp.int32, (count, count), 1)
    ).astype(F32)
    rank = dot(earlier.astype(BF16), (matches[0] + matches[1]).astype(BF16))
    place = rank + (((index % n) * 2 + index // n) * capacity).astype(F32)
    return [jnp.sum(m * place, axis=1, keepdims=True).astype(jnp.int32) for m in matches], matches


def hot(condition):
    return condition.astype(F32).astype(BF16)


def layer_kernel(
    lay, capacity, n_dp,
    tokens, vec_a, vec_b, vec_c, vec_d, w_router, routes_t, w_qkv_in, w_out_in, cotangent_in, own_a, own_b, own_c, own_d,
    first_norm_out, unit_out, attended_out, log_total_out, home_out, middle_out, second_out, gates_out, got, got_grad, first_grad, second_grad,
    all_a, all_b, all_c, all_d, hop_a, hop_b,
    staged_out, packed, packed_grad, rows_in, rows_grad, weight_a, weight_b, out_sum, in_sum, out_other, in_other, back_out, back_grad, grad_a, grad_b,
    packed_gates, rows_gates, send, recv, out_send, home_recv, local, stream_send, stream_recv, load,
    row_send, row_recv, row_local, back_send, back_recv, back_local, hop_send, hop_recv,
    first_norm, unit, attended, log_total, home, middle, second_norm, out_sems, w_qkv, w_out, cotangent, in_sems,
):
    n = lay.n
    me = lax.axis_index("sp")
    gain_one, shift_one, gain_two, shift_two = (vec[...].reshape(1, -1) for vec in (vec_a, vec_b, vec_c, vec_d))
    planes = Planes(n_dp)
    is_short, seq, first_pair = lay.role(me)
    entering = [
        pltpu.make_async_copy(source, target, in_sems.at[number])
        for number, (source, target) in enumerate(((w_qkv_in, w_qkv), (cotangent_in, cotangent), (w_out_in, w_out)))
    ]
    for copy in entering:
        copy.start()
    meet(planes.peers(n))
    stream = Weights(
        planes, (own_a, own_b, own_c, own_d), (all_a, all_b, all_c, all_d), stream_send, stream_recv
    )
    stream.begin((2, 3), True)

    hat, _ = normed(tokens[...].astype(F32))
    for copy in entering:
        copy.wait()
    first_norm[...] = (hat * gain_one + shift_one).astype(BF16)
    started = []
    for chunk in range(9):
        kind, third = divmod(chunk, 3)
        made = dot(first_norm[...], w_qkv[:, chunk * 2 * WIDE : (chunk + 1) * 2 * WIDE]).astype(BF16)
        made = made * BF16(HEAD_DIM**-0.5) if kind == 0 else made
        area = packed.at[pl.ds(kind * tokens.shape[0], tokens.shape[0]), pl.ds(third * 2 * WIDE, 2 * WIDE)]
        area[...] = made
        count = len(lay.owners())
        started += to_owners(
            lay,
            me,
            lambda pair: (pair % 2) * WIDE,
            lambda number: chunk * count + number,
            area,
            lambda start, rows: unit.at[kind, pl.ds(pl.multiple_of(start, 16), rows)],
            send,
            recv.at[kind],
            local,
            (2 * third, 2 * third + 1),
        )
    span = n * capacity
    width, hidden = grad_a.shape
    count = tokens.shape[0]
    place = slot_rows(lay, capacity, routes_t[...])

    def dispatch_copies(which, kind):
        source, target = ((packed, rows_in), (packed_grad, rows_grad), (packed_gates, rows_gates))[which]
        plane = jnp.where(planes.outer, planes.inward, planes.me) if kind == 0 else planes.me
        area = jnp.where(planes.outer, 1, 0) if kind == 0 else 2

        def block(buffer, number):
            if which == 2:
                return buffer.at[number]
            return buffer.at[pl.ds(pl.multiple_of(number * capacity, 16), capacity)]

        into = block(target, area * n + me)
        for step in range(n):
            to = lax.rem(me + step, n)
            piece = block(source, to * 2 + kind)
            far = remote(
                piece, into, row_send.at[which, kind, step], row_recv.at[which, area, me], {"sp": to, "dp": plane}
            )
            if step:
                yield True, far
                continue
            if kind == 0:
                yield planes.outer, far
            stays = planes.inner if kind == 0 else True
            yield stays, pltpu.make_async_copy(piece, into, row_local.at[which, kind])

    def each(copies, act):
        for condition, copy in copies:
            if condition is True:
                act(copy)
            else:
                pl.when(condition)(functools.partial(act, copy))

    def start(copy):
        copy.start()

    def end(copy):
        if copy.is_remote:
            copy.wait_send()
        else:
            copy.wait()

    def dispatch(which):
        for kind in range(2):
            each(dispatch_copies(which, kind), start)

    for first in range(0, 2 * span, ROWS):
        slots = first + lax.broadcasted_iota(jnp.int32, (ROWS, count), 0)
        chosen = hot(jnp.logical_or(slots == place[0], slots == place[1]))
        packed_grad[first : first + ROWS] = dot(chosen, cotangent[...]).astype(BF16)
    dispatch(1)
    for kind in range(3):
        wait_unit(lay, is_short, unit.at[kind], recv.at[kind])
    keep = lanes_first()
    lower = causal(BLOCK)

    def task(index, carry):
        start, block = lay.task(is_short, index)
        base = pl.multiple_of(start + block * BLOCK, BLOCK)
        queries = halves(unit[0, pl.ds(base, BLOCK)])

        def visit(place, state, diagonal):
            keys = unit[1, pl.ds(place, BLOCK)]
            values = unit[2, pl.ds(place, BLOCK)]
            result = []
            for (peak, total, summed), query in zip(state, queries):
                scores = dot_t(query, keys)
                if diagonal:
                    scores = jnp.where(lower, scores, NEGATIVE)
                new_peak = jnp.maximum(peak, jnp.max(scores, axis=1, keepdims=True))
                factor = jnp.exp(peak - new_peak)
                weight = jnp.exp(scores - new_peak)
                total = total * factor + jnp.sum(weight, axis=1, keepdims=True)
                summed = summed * factor + dot(weight.astype(BF16), values)
                result.append((new_peak, total, summed))
            return tuple(result)

        empty = (jnp.full((BLOCK, 1), NEGATIVE, F32), jnp.zeros((BLOCK, 1), F32), jnp.zeros((BLOCK, WIDE), F32))
        state = lax.fori_loop(
            0, block, lambda j, state: visit(pl.multiple_of(start + j * BLOCK, BLOCK), state, False), (empty, empty)
        )
        (peak_a, total_a, summed_a), (peak_b, total_b, summed_b) = visit(base, state, True)
        result = jnp.where(keep, summed_a / total_a, summed_b / total_b)
        attended[pl.ds(base, BLOCK)] = result
        staged_out[pl.ds(base, BLOCK)] = result.astype(BF16)
        log_total[pl.ds(base, BLOCK)] = jnp.where(keep, peak_a + jnp.log(total_a), peak_b + jnp.log(total_b))
        send_home(
            lay, me, is_short, seq, first_pair, base, block, start, staged_out, home, 0, out_send, home_recv, local
        )
        return carry

    lax.fori_loop(0, lay.tasks(is_short), task, 0)
    finish_sends(me, started)
    wait_home(lay, is_short, staged_out, out_send, 1, True)
    wait_home(lay, is_short, staged_out, home_recv, 1, False)

    stream.pass_on((2, 3), 1)
    stream.begin((0, 1), planes.inner)
    x1 = tokens[...].astype(F32) + dot(home[...], w_out[...])
    middle[...] = x1
    hat, _ = normed(x1)
    second = (hat * gain_two + shift_two).astype(BF16)
    second_norm[...] = second
    leaving = [
        pltpu.make_async_copy(source, target, out_sems.at[number])
        for number, (source, target) in enumerate(
            (
                (first_norm, first_norm_out), (unit, unit_out), (attended, attended_out), (log_total, log_total_out),
                (home, home_out), (middle, middle_out), (second_norm, second_out),
            )
        )
    ]
    for copy in leaving:
        copy.start()
    for first in range(0, 2 * span, ROWS):
        slots = first + lax.broadcasted_iota(jnp.int32, (ROWS, count), 0)
        chosen = hot(jnp.logical_or(slots == place[0], slots == place[1]))
        packed[first : first + ROWS] = dot(chosen, second).astype(BF16)
    dispatch(0)
    logits = dot_t(second, w_router[...])
    routes = upright(routes_t[...])
    index = lax.broadcasted_iota(jnp.int32, logits.shape, 1)
    chosen = [jnp.sum(jnp.where(index == routes[:, c : c + 1], logits, 0.0), axis=1, keepdims=True) for c in range(2)]
    top = jnp.maximum(chosen[0], chosen[1])
    exped = [jnp.exp(value - top) for value in chosen]
    gates = [value / (exped[0] + exped[1]) for value in exped]
    lane = lax.broadcasted_iota(jnp.int32, gates_out.shape, 1)
    gates_out[...] = jnp.where(lane == 0, gates[0], gates[1])
    column, _ = slot_columns(lay, capacity, routes)
    for number in range(2 * n):
        held = [
            jnp.where(jnp.logical_and(lane < capacity, lane + number * capacity == column[c]), gates[c], 0.0)
            for c in range(2)
        ]
        packed_gates[number] = jnp.broadcast_to(jnp.sum(held[0] + held[1], axis=0, keepdims=True), (8, 128))
    dispatch(2)

    def arrived(which, area):
        buffer = (rows_in, rows_grad, rows_gates)[which]
        for src in range(n):
            piece = buffer.at[area * n + src] if which == 2 else buffer.at[pl.ds((area * n + src) * capacity, capacity)]
            wait = pltpu.make_async_copy(piece, piece, row_recv.at[which, area, src]).wait
            if area == 1:
                wait()
            else:
                pl.when(src != me)(wait)

    for which in (1, 0, 2):
        for kind in range(2):
            each(dispatch_copies(which, kind), end)
    stream.begin((0, 1), planes.outer)
    stream.pass_on((2, 3), 2)

    def take(area):
        for which in (1, 0, 2):
            arrived(which, area)
        one = lax.broadcasted_iota(jnp.int32, (capacity, 128), 0) == lax.broadcasted_iota(jnp.int32, (capacity, 128), 1)

        def gated(src, carry):
            gate = jnp.sum(jnp.where(one, rows_gates[area * n + src, 0:1], 0.0), axis=1, keepdims=True)
            part = pl.ds(pl.multiple_of((area * n + src) * capacity, 16), capacity)
            rows_grad[part] = (gate * rows_grad[part].astype(F32)).astype(BF16)
            return carry

        lax.fori_loop(0, n, gated, 0)

    def clear(sums, rows):
        def one(index, carry):
            part = pl.ds(pl.multiple_of(index * ROWS, ROWS), ROWS)
            for total in sums:
                total[part] = jnp.zeros((ROWS, width), F32)
            return carry

        lax.fori_loop(0, rows // ROWS, one, 0)

    last = jnp.maximum(planes.me, n_dp - 1 - planes.me)

    def weight_grads(index):
        stores = [
            pltpu.make_async_copy(stage, whole.at[index], load.at[2 + i])
            for i, (stage, whole) in enumerate(((grad_a, first_grad), (grad_b, second_grad)))
        ]
        tall = 3 * WIDE
        for total in (span, 2 * span):

            @pl.when(planes.hosts == (total > span))
            def _():
                every_row = pl.ds(0, total)
                for col in range(0, width, tall):
                    part = pl.ds(col, tall)
                    grad_a[part] = t_dot(rows_in[every_row, part], packed_grad[every_row, :hidden]).astype(BF16)
                for col in range(0, hidden, tall):
                    part = pl.ds(col, tall)
                    grad_b[part] = t_dot(packed[every_row, part], rows_grad[every_row]).astype(BF16)

        for copy in stores:
            copy.start()
        for copy in stores:
            copy.wait()

    def work(trained, sums, first_row, base, rows, nearest, farthest, passing=True):
        arrays = (0, 1) if trained else (2, 3)
        every = (all_a, all_b) if trained else (all_c, all_d)
        own = (own_a, own_b) if trained else (own_c, own_d)

        def one(step, carry):
            distance, side = step // 2, lax.rem(step, 2)
            index = jnp.where(side == 0, planes.me - distance, planes.me + distance)
            real = jnp.logical_and(jnp.logical_and(index >= 0, index < n_dp), jnp.logical_or(side == 0, distance > 0))

            @pl.when(jnp.logical_and(passing, jnp.logical_and(side == 0, distance >= 3)))
            def _():
                stream.pass_on(arrays, distance)

            @pl.when(real)
            def _():
                near = [pltpu.make_async_copy(own[i], (weight_a, weight_b)[i], load.at[i]) for i in range(2)]
                far = [pltpu.make_async_copy(every[i].at[index], (weight_a, weight_b)[i], load.at[i]) for i in range(2)]

                @pl.when(distance == 0)
                def _():
                    for copy in near:
                        copy.start()

                @pl.when(distance > 0)
                def _():
                    for copy in far:
                        copy.start()

                for copy in near:
                    copy.wait()

                def chunk(number, carry):
                    part = pl.ds(pl.multiple_of(base + number * ROWS, ROWS), ROWS)
                    here = pl.ds(pl.multiple_of(first_row + number * ROWS, ROWS), ROWS)
                    active, slope = gelu_parts(dot(rows_in[here], weight_a[...]))
                    active = active.astype(BF16)
                    back = (dot_t(rows_grad[here], weight_b[...]) * slope).astype(BF16)
                    if trained:
                        packed[part, :hidden] = active
                        packed_grad[part, :hidden] = back
                    sums[0][part] += dot(active, weight_b[...])
                    sums[1][part] += dot_t(back, weight_a[...])
                    return carry

                lax.fori_loop(0, rows // ROWS, chunk, 0)
                if trained:

                    @pl.when(distance < last)
                    def _():
                        weight_grads(index)

            return carry

        lax.fori_loop(2 * nearest, 2 * farthest + 2, one, 0)

    def turn(sums, first_row, base, rows):
        def one(number, carry):
            part = pl.ds(pl.multiple_of(base + number * ROWS, ROWS), ROWS)
            here = pl.ds(pl.multiple_of(first_row + number * ROWS, ROWS), ROWS)
            back_out[here] = sums[0][part].astype(BF16)
            back_grad[here] = sums[1][part].astype(BF16)
            return carry

        lax.fori_loop(0, rows // ROWS, one, 0)

    def back_copies(kind, guest, whiches=(0, 1)):
        area = 2 if kind else int(guest)
        plane = planes.guest if guest else planes.me
        for which in whiches:
            source, target = ((back_out, got), (back_grad, got_grad))[which]
            into = target.at[pl.ds(pl.multiple_of((me * 2 + kind) * capacity, 16), capacity)]
            for step in range(n):
                to = lax.rem(me + step, n)
                piece = source.at[pl.ds(pl.multiple_of((area * n + to) * capacity, 16), capacity)]
                if step or guest:
                    yield True, remote(
                        piece, into, back_send.at[which, area, step], back_recv.at[which, kind, me], {"sp": to, "dp": plane}
                    )
                else:
                    yield True, pltpu.make_async_copy(piece, into, back_local.at[which, kind])

    def hops(act):
        for up in (True, False):
            for array, (whole, hop) in enumerate(((first_grad, hop_a), (second_grad, hop_b))):

                @pl.when(planes.me == (1 if up else n_dp - 2))
                def _():
                    act(
                        remote(
                            whole.at[2 if up else n_dp - 3], hop.at[int(up)], hop_send.at[int(up), array],
                            hop_recv.at[int(up), array], {"dp": planes.me + (1 if up else -1)},
                        )
                    )

    train_sums, frozen_sums = (out_sum, in_sum), (out_other, in_other)
    train_rows = jnp.where(planes.hosts, 2 * span, span)
    clear(frozen_sums, span)

    clear(train_sums, train_rows)

    @pl.when(planes.inner)
    def _():
        take(0)

        @pl.when(planes.hosts)
        def _():
            take(1)

        work(True, train_sums, 0, 0, train_rows, 0, 0)

    take(2)
    work(False, frozen_sums, 2 * span, 0, span, 0, 1)
    stream.pass_on((0, 1), 1, True)
    work(False, frozen_sums, 2 * span, 0, span, 2, n_dp - 1)
    turn(frozen_sums, 2 * span, 0, span)
    each(back_copies(1, False), start)

    @pl.when(planes.inner)
    def _():
        stream.pass_on((0, 1), 1, False)
        work(True, train_sums, 0, 0, train_rows, 1, 1)
        stream.pass_on((0, 1), 2)
        hops(start)
        work(True, train_sums, 0, 0, train_rows, 2, last - 1)

        @pl.when(planes.hosts)
        def _():
            work(True, train_sums, span, span, span, last, last)
            turn(train_sums, span, span, span)
            each(back_copies(0, True), start)

        work(True, train_sums, 0, 0, span, last, last, jnp.logical_not(planes.hosts))
        turn(train_sums, 0, 0, span)
        each(back_copies(0, False), start)
        weight_grads(jnp.where(planes.me > n_dp - 1 - planes.me, 0, n_dp - 1))

    each(back_copies(1, False), end)

    @pl.when(planes.inner)
    def _():
        each(back_copies(0, False), end)

        @pl.when(planes.hosts)
        def _():
            each(back_copies(0, True), end)

    for kind in range(2):
        for which, buffer in enumerate((got, got_grad)):
            for src in range(n):
                piece = buffer.at[pl.ds((src * 2 + kind) * capacity, capacity)]
                comes = jnp.logical_or(src != me, planes.outer) if kind == 0 else src != me
                pl.when(comes)(pltpu.make_async_copy(piece, piece, back_recv.at[which, kind, src]).wait)
    stream.finish()
    for copy in leaving:
        copy.wait()
    hops(end)
    for up in (True, False):
        for array, hop in enumerate((hop_a, hop_b)):

            @pl.when(planes.me == (2 if up else n_dp - 3))
            def _():
                pltpu.make_async_copy(hop.at[int(up)], hop.at[int(up)], hop_recv.at[int(up), array]).wait()


ANY = pl.BlockSpec(memory_space=pl.ANY)


def layer(lay, capacity, n_dp, tokens, vectors, w_router, routes_t, w_qkv, w_out, cotangent, weights):
    count, width = tokens.shape
    n = lay.n
    owners = len(lay.owners())
    span = n * capacity
    shape = jax.ShapeDtypeStruct
    hidden = weights[0].shape[1]
    every = [shape((n_dp, *weight.shape), BF16) for weight in weights]
    return pl.pallas_call(
        functools.partial(layer_kernel, lay, capacity, n_dp),
        out_shape=(
            shape((count, width), BF16),
            shape((3, UNIT, WIDE), BF16),
            shape((UNIT, WIDE), F32),
            shape((UNIT, WIDE), F32),
            shape((count, width), BF16),
            shape((count, width), F32),
            shape((count, width), BF16),
            shape((count, 128), F32),
            shape((2 * span, width), BF16),
            shape((2 * span, width), BF16),
            every[0],
            every[1],
            *every,
            shape((2, *weights[0].shape), BF16),
            shape((2, *weights[1].shape), BF16),
        ),
        in_specs=[VMEM] * 7 + [ANY] * 7,
        out_specs=[ANY] * 7 + [VMEM] + [ANY] * 10,
        scratch_shapes=[
            pltpu.VMEM((UNIT, WIDE), BF16),
            pltpu.VMEM((2 * span, width), BF16),
            pltpu.VMEM((2 * span, width), BF16),
            pltpu.VMEM((3 * span, width), BF16),
            pltpu.VMEM((3 * span, width), BF16),
            pltpu.VMEM((width, hidden), BF16),
            pltpu.VMEM((hidden, width), BF16),
            pltpu.VMEM((2 * span, width), F32),
            pltpu.VMEM((2 * span, width), F32),
            pltpu.VMEM((span, width), F32),
            pltpu.VMEM((span, width), F32),
            pltpu.VMEM((3 * span, width), BF16),
            pltpu.VMEM((3 * span, width), BF16),
            pltpu.VMEM((width, hidden), BF16),
            pltpu.VMEM((hidden, width), BF16),
            pltpu.VMEM((2 * n, 8, 128), F32),
            pltpu.VMEM((3 * n, 8, 128), F32),
            DMA((9 * owners,)),
            DMA((3,)),
            DMA,
            DMA,
            DMA,
            DMA((2, 4, n_dp)),
            DMA((4, n_dp)),
            DMA((4,)),
            DMA((3, 2, n)),
            DMA((3, 3, n)),
            DMA((3, 2)),
            DMA((2, 3, n)),
            DMA((2, 2, n)),
            DMA((2, 2)),
            DMA((2, 2)),
            DMA((2, 2)),
            pltpu.VMEM((count, width), BF16),
            pltpu.VMEM((3, UNIT, WIDE), BF16),
            pltpu.VMEM((UNIT, WIDE), F32),
            pltpu.VMEM((UNIT, WIDE), F32),
            pltpu.VMEM((count, width), BF16),
            pltpu.VMEM((count, width), F32),
            pltpu.VMEM((count, width), BF16),
            DMA((7,)),
            *(pltpu.VMEM(value.shape, BF16) for value in (w_qkv, w_out, cotangent)),
            DMA((3,)),
        ],
        compiler_params=pltpu.CompilerParams(collective_id=0, has_side_effects=True, vmem_limit_bytes=LIMIT),
        cost_estimate=pl.CostEstimate(flops=50 * 10**9, bytes_accessed=100 * 2**20, transcendentals=10**7),
        name="layer",
    )(
        tokens, *vectors, w_router, routes_t, w_qkv, w_out, cotangent, *weights
    )


class Sum:
    def __init__(self, n_sp, n_dp, pieces, quantum, needed, first):
        self.n_sp, self.n_dp = n_sp, n_dp
        self.bits = n_sp.bit_length() - 1
        unit = math.lcm(16 * n_sp * n_dp, quantum)
        units = -(-needed // unit)
        sizes = [first // unit] if first >= unit else []
        left = units - sum(sizes)
        pieces = min(pieces, left)
        sizes += [left // pieces + (p < left % pieces) for p in range(pieces)]
        self.pieces = [(unit * sum(sizes[:p]), unit * size) for p, size in enumerate(sizes)]
        self.early = first >= unit
        self.rows = unit * units
        self.steps = 2 * self.bits + 2

    def order(self, piece):
        later = list(range(1, self.bits))
        return [0] + (later[::-1] if piece % 2 else later)

    def landing(self):
        places, start = [], 0
        for _, rows in self.pieces:
            places.append([])
            for step in range(self.bits + 1):
                rows = rows // 2 if step < self.bits else rows
                places[-1].append((start, rows))
                start += rows
        return places, start

    def bind(self, mine, landed, whole, send, recv):
        self.mine, self.landed, self.whole, self.send, self.recv = mine, landed, whole, send, recv
        self.me, self.plane = lax.axis_index("sp"), lax.axis_index("dp")
        self.places, _ = self.landing()
        self.starts = [[start] for start, _ in self.pieces]
        for piece, (_, rows) in enumerate(self.pieces):
            for bit in self.order(piece):
                rows //= 2
                value = (self.me // (1 << bit)) % 2
                self.starts[piece].append(self.starts[piece][-1] + value * rows)

    def partner(self, bit):
        value = (self.me // (1 << bit)) % 2
        return self.me + (1 - 2 * value) * (1 << bit)

    def peers(self):
        found = [(True, {"sp": self.partner(bit)}) for bit in range(self.bits)]
        return found + [(True, {"dp": lax.rem(self.plane + step, self.n_dp)}) for step in range(1, self.n_dp)]

    def cut(self, start, rows):
        return pl.ds(pl.multiple_of(start, 16), rows)

    def copies(self, piece, step):
        bits = self.bits
        rows = self.pieces[piece][1]
        if step < bits or step > bits + 1:
            level = step if step < bits else 2 * bits + 1 - step
            bit = self.order(piece)[level]
            half = rows >> (level + 1)
            held, kept = self.starts[piece][level], self.starts[piece][level + 1]
            if step < bits:
                start, _ = self.places[piece][step]
                source = self.mine.at[self.cut(2 * held + half - kept, half)]
                target = self.landed.at[pl.ds(start, half)]
            else:
                source = target = self.whole.at[self.cut(kept, half)]
            yield remote(source, target, self.send.at[piece, step, 0], self.recv.at[piece, step, 0], self.partner(bit))
            return
        block = (rows >> bits) // self.n_dp
        base = self.starts[piece][bits]
        start, _ = self.places[piece][bits]
        for far in range(1, self.n_dp):
            other = lax.rem(self.plane + far, self.n_dp)
            if step == bits:
                source = self.mine.at[self.cut(base + other * block, block)]
                target = self.landed.at[self.cut(start + self.plane * block, block)]
            else:
                source = target = self.whole.at[self.cut(base + self.plane * block, block)]
            yield remote(source, target, self.send.at[piece, step, far], self.recv.at[piece, step, far], {"dp": other})

    def start(self, piece, step):
        for copy in self.copies(piece, step):
            copy.start()

    def add(self, piece, step):
        for copy in self.copies(piece, step):
            copy.wait()
        bits, rows = self.bits, self.pieces[piece][1]
        if step > bits:
            return
        start, _ = self.places[piece][step]
        if step < bits:
            size, kept = rows >> (step + 1), self.starts[piece][step + 1]
            for first, count in blocks(size):

                def one(number, carry):
                    part = self.cut(kept + first + number * count[0], count[0])
                    here = self.cut(start + first + number * count[0], count[0])
                    self.mine[part] = (self.mine[part].astype(F32) + self.landed[here].astype(F32)).astype(BF16)
                    return carry

                lax.fori_loop(0, count[1], one, 0)
            return
        block = (rows >> bits) // self.n_dp
        own = self.cut(self.starts[piece][bits] + self.plane * block, block)
        total = self.mine[own].astype(F32)
        for far in range(1, self.n_dp):
            other = lax.rem(self.plane + far, self.n_dp)
            total = total + self.landed[self.cut(start + other * block, block)].astype(F32)
        self.whole[own] = total.astype(BF16)


def blocks(rows, size=512):
    found = []
    if rows >= size:
        found.append((0, (size, rows // size)))
    if rows % size:
        found.append((rows - rows % size, (rows % size, 1)))
    return found


def run_sum(total, ahead, ready, done, between):
    begun = [-(piece // 2) for piece in range(len(total.pieces) - total.early)]
    begun = [ahead] * total.early + begun
    rounds = 0
    while any(step <= total.steps for step in begun):
        for piece, step in enumerate(begun):
            if 0 < step <= total.steps:
                total.add(piece, step - 1)
                if step == total.steps:
                    done(piece)
            if step == 0:
                ready(piece)
            if 0 <= step < total.steps:
                total.start(piece, step)
            begun[piece] += 1
        between(rounds)
        rounds += 1


class Gather:
    def __init__(self, n, own, hop, below, above, theirs, sums, stage, send, recv, load):
        self.n, self.own, self.hop, self.below, self.above, self.stage = n, own, hop, below, above, stage
        self.theirs, self.sums, self.send, self.recv, self.load = theirs, sums, send, recv, load
        self.me = lax.axis_index("dp")
        self.inner = jnp.logical_and(self.me >= 1, self.me <= n - 2)

    def copy(self, array, index, up, source):
        target = (self.below if up else self.above)[array].at[index]
        other = self.me + 1 if up else self.me - 1
        return remote(
            source, target, self.send.at[int(up), array, index], self.recv.at[int(up), array, index], {"dp": other}
        )

    def fetch(self, source, buffer, number):
        moved = pltpu.make_async_copy(source, buffer, self.load.at[number])
        moved.start()
        return moved

    def wanted(self, index, up):
        return jnp.logical_and(self.inner, index > self.me if up else index < self.me)

    def begins(self, up):
        return self.me == 1 if up else self.me == self.n - 2

    def hopped(self, index, up):
        return index == (2 if up else self.n - 3)

    def begin(self, array, index, up):
        if self.hopped(index, up):
            return

        @pl.when(jnp.logical_and(self.wanted(index, up), self.begins(up)))
        def _():
            self.copy(array, index, up, self.own[array].at[index]).start()

    def came(self, array, index, up):
        buffer = (self.below if up else self.above)[array].at[index]
        pltpu.make_async_copy(buffer, buffer, self.recv.at[int(up), array, index]).wait()
        return buffer

    def pass_on(self, array, index, up):
        @pl.when(jnp.logical_and(self.wanted(index, up), jnp.logical_not(self.begins(up))))
        def _():
            total, theirs = self.sums[array].at[int(up)], self.theirs[array]
            here = self.fetch(self.own[array].at[index], total, 0)
            self.fetch(self.came(array, index, up), theirs, 1).wait()
            here.wait()
            total[...] = (total[...].astype(F32) + theirs[...].astype(F32)).astype(BF16)
            self.copy(array, index, up, total).start()

    def finish(self, array, index, up):
        waits = self.wanted(index, up)
        if self.hopped(index, up):
            waits = jnp.logical_and(waits, jnp.logical_not(self.begins(up)))

        @pl.when(waits)
        def _():
            self.copy(array, index, up, self.sums[array].at[int(up)]).wait_send()

    def total(self, array, out):
        theirs = self.theirs[array]

        @pl.when(self.inner)
        def _():
            self.fetch(self.own[array].at[self.me], theirs, 0).wait()

        @pl.when(jnp.logical_not(self.inner))
        def _():
            theirs[...] = jnp.zeros_like(theirs)

        sides = ((True, self.me >= 2), (False, self.me <= self.n - 3))
        for up, comes in sides:

            near = self.me == (2 if up else self.n - 3)

            @pl.when(jnp.logical_and(comes, near))
            def _():
                self.fetch(self.hop[array].at[int(up)], self.sums[array].at[int(up)], 1).wait()

            @pl.when(jnp.logical_and(comes, jnp.logical_not(near)))
            def _():
                self.fetch(self.came(array, self.me, up), self.sums[array].at[int(up)], 1).wait()

        rows, lanes = out.shape
        stores = []
        for number in range(lanes // WIDE):
            part = pl.ds(number * WIDE, WIDE)
            stage = self.stage.at[number % 2, pl.ds(0, rows), pl.ds(0, WIDE)]
            if number >= 2:
                stores[number - 2].wait()
            stage[...] = theirs[:, part].astype(F32)
            for up, comes in sides:

                @pl.when(comes)
                def _():
                    stage[...] += self.sums[array][int(up), :, part].astype(F32)

            stores.append(pltpu.make_async_copy(stage, out.at[:, part], self.load.at[3 + number % 2]))
            stores[number].start()
        for store in stores[-2:]:
            store.wait()


def gather_scratch(n, first, second):
    shapes = [first.shape[1:], second.shape[1:]]
    return [
        *(pltpu.VMEM(shape, BF16) for shape in shapes),
        *(pltpu.VMEM((2, *shape), BF16) for shape in shapes),
        DMA((2, 2, n)),
        DMA((2, 2, n)),
        DMA((5,)),
    ]


def back_kernel(
    lay, capacity, replicated,
    got, got_grad, middle, second_norm, gates, home_out, w_out, vec_a, vec_b, w_router, routes_t, cotangent,
    unit_in, attended, log_total_in, first_norm_in, tokens, w_qkv_in, first_own, second_own, hop_a, hop_b,
    block_out, tokens_grad, qkv_grad, out_proj_grad, router_out, vectors_out, first_total, second_total, below_a, below_b, above_a, above_b,
    grad_attended, grad_out, deltas, query_sum, staged, home, send, recv, out_send, home_recv, local,
    theirs_a, theirs_b, sums_a, sums_b, pass_send, pass_recv, load,
    grads, landed, summed, stage, sum_send, sum_recv, out_sems, unit, log_total, first_norm, w_qkv, late_sems,
):
    n_dp = first_own.shape[0]
    gather = Gather(
        n_dp, (first_own, second_own), (hop_a, hop_b), (below_a, below_b), (above_a, above_b), (theirs_a, theirs_b),
        (sums_a, sums_b), stage, pass_send, pass_recv, load,
    )
    gain_one, gain_two = (vec[...].reshape(1, -1) for vec in (vec_a, vec_b))
    replicated.bind(grads, landed, summed, sum_send, sum_recv)
    me = lax.axis_index("sp")
    is_short, seq, first_pair = lay.role(me)
    everywhere = [(True, {"dp": lax.rem(gather.me + step, n_dp)}) for step in range(1, n_dp)]
    late = [
        pltpu.make_async_copy(source, target, late_sems.at[number])
        for number, (source, target) in enumerate(
            ((attended, deltas), (unit_in, unit), (log_total_in, log_total), (first_norm_in, first_norm), (w_qkv_in, w_qkv))
        )
    ]
    for copy in late:
        copy.start()
    meet(plane_peers(lay.n) + everywhere)
    inside = [(up, index) for index in range(1, n_dp - 1) for up in (True, False)]
    ends = [(True, n_dp - 1), (False, 0)]
    for up, index in ends:
        gather.begin(0, index, up)
    place, matches = slot_columns(lay, capacity, upright(routes_t[...]))
    slots = lax.broadcasted_iota(jnp.int32, (tokens.shape[0], got.shape[0]), 1)
    chosen = [hot(slots == place[c]) for c in range(2)]
    upstream = cotangent[...].astype(F32)
    gate = [gates[:, c : c + 1] for c in range(2)]
    total = middle[...]
    grad_gate = []
    for c in range(2):
        produced = dot(chosen[c], got[...])
        total = total + gate[c] * produced
        grad_gate.append(jnp.sum(upstream * produced, axis=1, keepdims=True))
    block_out[...] = total.astype(BF16)
    mean_grad = gate[0] * grad_gate[0] + gate[1] * grad_gate[1]
    grad_logits = sum(matches[c] * (gate[c] * (grad_gate[c] - mean_grad)) for c in range(2))
    high = grad_logits.astype(BF16)
    low = (grad_logits - high.astype(F32)).astype(BF16)
    experts = w_router.shape[0]
    grad_second = dot(high[:, :experts], w_router[...]) + dot(low[:, :experts], w_router[...])
    grad_second = grad_second + dot(chosen[0] + chosen[1], got_grad[...])
    hat, scale = normed(middle[...])
    grad = upstream + norm_back(grad_second, gain_two, hat, scale)
    tokens_grad[...] = grad
    branch = grad.astype(BF16)
    grad_attended[...] = dot_t(branch, w_out[...]).astype(BF16)
    width = w_out.shape[0]

    started = to_owners(
        lay,
        me,
        lambda pair: pair * WIDE,
        lambda number: number,
        grad_attended,
        lambda start, rows: grad_out.at[pl.ds(pl.multiple_of(start, 16), rows)],
        send,
        recv,
        local,
        range(PAIRS),
    )
    for up, index in ends:
        gather.begin(1, index, up)
    def put(column, value):
        for lane in range(0, value.shape[1], WIDE):
            grads[pl.ds((column + lane) // WIDE * width, width)] = value[:, lane : lane + WIDE].astype(BF16)

    put(0, t_dot(home_out[...], branch))
    moments = (1, 2, 3, 5, 7)
    if replicated.early:
        replicated.start(0, 0)
    router_grad = t_dot(second_norm[...], high) + t_dot(second_norm[...], low)
    gain_two_grad = jnp.sum(grad_second * hat, axis=0, keepdims=True)
    shift_two_grad = jnp.sum(grad_second, axis=0, keepdims=True)
    query_sum[...] = jnp.zeros_like(query_sum)
    keep = lanes_first()
    lower = causal(BLOCK)
    wait_unit(lay, is_short, grad_out, recv)
    for copy in late:
        copy.wait()

    def make_delta(index, carry):
        part = pl.ds(pl.multiple_of(index * BLOCK, BLOCK), BLOCK)
        first, second = halves(grad_out[part].astype(F32) * deltas[part])
        deltas[part] = jnp.where(
            keep, jnp.sum(first, axis=1, keepdims=True), jnp.sum(second, axis=1, keepdims=True)
        )
        return carry

    lax.fori_loop(0, lay.tasks(is_short), make_delta, 0)
    per = jnp.where(is_short, LEN_A // BLOCK, LEN_B // BLOCK)

    def task(index, carry):
        start, block = lay.task(is_short, index)
        base = pl.multiple_of(start + block * BLOCK, BLOCK)
        keys = unit[1, pl.ds(base, BLOCK)]
        values = unit[2, pl.ds(base, BLOCK)]
        key_both = jnp.concatenate(halves(keys), axis=0)

        def visit(place, state, diagonal):
            part = pl.ds(place, BLOCK)
            grad_key, grad_value = state
            queries = halves(unit[0, part])
            outs = halves(grad_out[part])
            weights, grads = [], []
            for which, (query, out) in enumerate(zip(queries, outs)):
                column = which * HEAD_DIM
                scores = dot_t(query, keys)
                if diagonal:
                    scores = jnp.where(lower, scores, NEGATIVE)
                weight = jnp.exp(scores - log_total[part, column : column + 1])
                grad = weight * (dot_t(out, values) - deltas[part, column : column + 1])
                weights.append(weight.astype(BF16))
                grads.append(grad.astype(BF16))
            grad_value = grad_value + t_dot(jnp.concatenate(weights, axis=0), jnp.concatenate(outs, axis=0))
            grad_key = grad_key + t_dot(jnp.concatenate(grads, axis=0), jnp.concatenate(queries, axis=0))
            query_sum[part] += dot(jnp.concatenate(grads, axis=1), key_both)
            return grad_key, grad_value

        zero = jnp.zeros((BLOCK, WIDE), F32)
        state = visit(base, (zero, zero), True)
        grad_key, grad_value = lax.fori_loop(
            block + 1, per, lambda i, state: visit(pl.multiple_of(start + i * BLOCK, BLOCK), state, False), state
        )
        part = pl.ds(base, BLOCK)
        staged[0, part] = (query_sum[part] * HEAD_DIM**-0.5).astype(BF16)
        staged[1, part] = grad_key.astype(BF16)
        staged[2, part] = grad_value.astype(BF16)
        for kind in range(3):
            send_home(
                lay, me, is_short, seq, first_pair, base, block, start, staged.at[kind], home, kind * PAIRS * WIDE,
                out_send.at[kind], home_recv.at[kind], local,
            )
        @pl.when(index == 1)
        def _():
            for up, which in ends:
                gather.pass_on(0, which, up)

        for step, moment in enumerate(moments if replicated.early else ()):

            @pl.when(index == moment)
            def _():
                replicated.add(0, step)
                replicated.start(0, step + 1)

        return carry

    lax.fori_loop(0, lay.tasks(is_short), task, 0)
    for up, index in ends:
        gather.pass_on(1, index, up)
    for array in range(2):
        for up, index in inside:
            gather.begin(array, index, up)
    for kind in range(3):
        wait_home(lay, is_short, staged.at[kind], home_recv.at[kind], 1, False)
    first, last = PAIRS, 4 * PAIRS

    def ready(piece):
        start, rows = replicated.pieces[piece]
        for column in range(start // width, (start + rows) // width, 2):
            if column == last:
                grads[pl.ds(column * width, width)] = router_grad.astype(BF16)
                parts = (*extra, gain_two_grad, shift_two_grad)
                rows = [part[:, lane : lane + WIDE] for part in parts for lane in range(0, width, WIDE)]
                rows.append(jnp.zeros((width - len(rows), WIDE), F32))
                grads[pl.ds((column + 1) * width, width)] = jnp.concatenate(rows, axis=0).astype(BF16)
            elif column > last:
                grads[pl.ds(column * width, 2 * width)] = jnp.zeros((2 * width, WIDE), BF16)
            elif first <= column:
                lanes = pl.ds((column - first) * WIDE, 2 * WIDE)
                put(column * WIDE, t_dot(first_norm[...], home[:, lanes]))

    stores, extra = [], []

    def done(piece):
        start, rows = replicated.pieces[piece]
        for column in range(start // width, (start + rows) // width, 2):
            parts = [summed.at[pl.ds((column + i) * width, width)] for i in range(2)]
            if column == last:
                router_out[...] = jnp.transpose(parts[0][...].astype(F32))[: router_out.shape[0]]
                vectors_out[...] = parts[1][0:32].astype(F32)
            elif column < last:
                for i in range(2):
                    target, lane = (out_proj_grad, column) if column < first else (qkv_grad, column - first)
                    lanes = pl.ds((lane + i) * WIDE, WIDE)
                    stores.append(pltpu.make_async_copy(parts[i], target.at[:, lanes], out_sems.at[len(stores)]))
                    stores[-1].start()

    def between(number):
        if number == 0:
            grad_first = dot_t(home[...], w_qkv[...])
            hat, scale = normed(tokens[...].astype(F32))
            extra.append(jnp.sum(grad_first * hat, axis=0, keepdims=True))
            extra.append(jnp.sum(grad_first, axis=0, keepdims=True))
            tokens_grad[...] += norm_back(grad_first, gain_one, hat, scale)
        if number in (6, 7):
            array = number - 6
            for up, index in inside:
                gather.pass_on(array, index, up)
            for up, index in inside + ends:
                gather.finish(array, index, up)
            gather.total(array, (first_total, second_total)[array])

    run_sum(replicated, len(moments) + 1, ready, done, between)
    for store in stores:
        store.wait()
    finish_sends(me, started)
    for kind in range(3):
        wait_home(lay, is_short, staged.at[kind], out_send.at[kind], 1, True)


def backward(lay, capacity, values):
    count, width = values[2].shape
    owners = len(lay.owners())
    shape = jax.ShapeDtypeStruct
    slices = values[-4:-2]
    late = [values[number] for number in (12, 14, 15, 17)]
    replicated = Sum(lay.n, slices[0].shape[0], 6, 2 * width, 26 * width, width // WIDE * width)
    return pl.pallas_call(
        functools.partial(back_kernel, lay, capacity, replicated),
        out_shape=(
            shape((count, width), BF16), shape((count, width), F32),
            shape((width, 3 * width), BF16), shape((width, width), BF16), shape(values[9].shape, F32), shape((32, WIDE), F32),
            *(shape(g.shape[1:], F32) for g in slices), *(shape(g.shape, BF16) for g in slices * 2),
        ),
        in_specs=[VMEM] * 12 + [ANY] * 4 + [VMEM] + [ANY] * 5,
        out_specs=[VMEM] * 2 + [ANY] * 2 + [VMEM] * 2 + [ANY] * 6,
        scratch_shapes=[
            pltpu.VMEM((count, width), BF16),
            pltpu.VMEM((UNIT, WIDE), BF16),
            pltpu.VMEM((UNIT, WIDE), F32),
            pltpu.VMEM((UNIT, WIDE), F32),
            pltpu.VMEM((3, UNIT, WIDE), BF16),
            pltpu.VMEM((count, 3 * width), BF16),
            DMA((owners,)),
            DMA,
            DMA((3,)),
            DMA((3,)),
            DMA,
            *gather_scratch(slices[0].shape[0], *slices),
            pltpu.VMEM((replicated.rows, WIDE), BF16),
            pltpu.VMEM((replicated.landing()[1], WIDE), BF16),
            pltpu.VMEM((replicated.rows, WIDE), BF16),
            pltpu.VMEM((2, width, WIDE), F32),
            DMA((len(replicated.pieces), replicated.steps, slices[0].shape[0])),
            DMA((len(replicated.pieces), replicated.steps, slices[0].shape[0])),
            DMA((4 * PAIRS,)),
            *(pltpu.VMEM(value.shape, value.dtype) for value in late),
            DMA((5,)),
        ],
        compiler_params=pltpu.CompilerParams(collective_id=1, has_side_effects=True, vmem_limit_bytes=LIMIT),
        cost_estimate=pl.CostEstimate(flops=16 * 10**9, bytes_accessed=60 * 2**20, transcendentals=5 * 10**6),
        name="backward",
    )(*values)


def shards(
    tokens, ln1_gain, ln1_shift, w_qkv, w_out, ln2_gain, ln2_shift, w_router,
    train_w1, train_w2, frozen_w1, frozen_w2, routes, cotangent,
):
    lay = Layout(lax.axis_size("sp"))
    n_dp = lax.axis_size("dp")
    tokens, routes, cotangent = tokens[0], routes[0], cotangent[0]
    count, width = tokens.shape
    capacity = 2 * count // lay.n
    router_t, routes_t = w_router.T, routes.T
    weights = [weight[0] for weight in (train_w1, train_w2, frozen_w1, frozen_w2)]
    (
        first_norm, unit, attended, log_total, home, middle, second, gates, got, got_grad, first_grad, second_grad,
        _, _, _, _, hop_a, hop_b,
    ) = layer(
        lay, capacity, n_dp, tokens, (ln1_gain, ln1_shift, ln2_gain, ln2_shift), router_t, routes_t, w_qkv, w_out, cotangent,
        weights,
    )
    block_out, tokens_grad, qkv_grad, out_proj, router, vector_rows, first_total, second_total, *_ = backward(
        lay, capacity,
        (
            got, got_grad, middle, second, gates, home, w_out, ln1_gain, ln2_gain, router_t, routes_t, cotangent,
            unit, attended, log_total, first_norm, tokens, w_qkv, first_grad, second_grad, hop_a, hop_b,
        ),
    )
    found = vector_rows[: 4 * width // WIDE].reshape(4, width)
    return (
        block_out[None],
        tokens_grad[None],
        found[0],
        found[1],
        qkv_grad.astype(F32),
        out_proj.astype(F32),
        found[2],
        found[3],
        router.T,
        first_total[None],
        second_total[None],
    )


def solution(mesh):
    in_specs = (
        P("dp", "sp", None), P(), P(), P(), P(), P(), P(), P(),
        P("sp", None, "dp"), P("sp", "dp", None), P("sp", None, "dp"), P("sp", "dp", None),
        P("dp", "sp", None), P("dp", "sp", None),
    )
    out_specs = (
        P("dp", "sp", None), P("dp", "sp", None), P(), P(), P(), P(), P(), P(), P(),
        P("sp", None, "dp"), P("sp", "dp", None),
    )
    return jax.shard_map(shards, mesh=mesh, in_specs=in_specs, out_specs=out_specs, check_vma=False)
```

```python
import functools
import math

import jax
import jax.numpy as jnp
from jax import lax
from jax.experimental import pallas as pl
from jax.experimental.pallas import tpu as pltpu
from jax.sharding import PartitionSpec as P

HEADS = 12
HEAD_DIM = 64
LEN_A = 1024
LEN_B = 2048
PAIRS = HEADS // 2
WIDE = 2 * HEAD_DIM
UNIT = 3 * LEN_A
BLOCK = 256
EPSILON = 1e-05
NEGATIVE = -1e30
MESH = pl.DeviceIdType.MESH
DMA = pltpu.SemaphoreType.DMA
F32 = jnp.float32
BF16 = jnp.bfloat16
VMEM = pl.BlockSpec(memory_space=pltpu.VMEM)


def dot(a, b):
    return jnp.dot(a, b, preferred_element_type=F32)


def dot_t(a, b):
    return lax.dot_general(a, b, (((1,), (1,)), ((), ())), preferred_element_type=F32)


def t_dot(a, b):
    return lax.dot_general(a, b, (((0,), (0,)), ((), ())), preferred_element_type=F32)


def normed(value):
    centre = jnp.mean(value, axis=-1, keepdims=True)
    centred = value - centre
    spread = jnp.mean(centred * centred, axis=-1, keepdims=True)
    scale = lax.rsqrt(spread + EPSILON)
    return centred * scale, scale


def norm_back(grad, gain, hat, scale):
    scaled = grad * gain
    first = jnp.mean(scaled, axis=-1, keepdims=True)
    second = jnp.mean(scaled * hat, axis=-1, keepdims=True)
    return (scaled - first - hat * second) * scale


class Layout:
    def __init__(self, n_sp):
        self.n = n_sp
        self.sequences = n_sp // 8
        self.short = LEN_A // n_sp
        self.long = LEN_B // n_sp
        self.split = self.sequences * self.short

    def owners(self):
        found = []
        for seq in range(self.sequences):
            for pair in range(PAIRS):
                number = seq * PAIRS + pair
                found.append((number + number // 3 + 1, True, self.split + seq * self.long, self.long, pair, 0))
                found.append((4 * (seq * 2 + pair // 3), False, seq * self.short, self.short, pair, (pair % 3) * LEN_A))
        return found

    def role(self, me):
        is_short = lax.rem(me, 4) == 0
        number = me - me // 4 - 1
        group = me // 4
        seq = jnp.where(is_short, group // 2, number // PAIRS)
        pair = jnp.where(is_short, 3 * lax.rem(group, 2), lax.rem(number, PAIRS))
        return is_short, seq, pair

    def task(self, is_short, index):
        per = LEN_A // BLOCK
        start = jnp.where(is_short, (index // per) * LEN_A, 0)
        block = jnp.where(is_short, lax.rem(index, per), index)
        return pl.multiple_of(start, BLOCK), block

    def tasks(self, is_short):
        return jnp.where(is_short, 3 * LEN_A // BLOCK, LEN_B // BLOCK)


def meet(peers):
    barrier = pltpu.get_barrier_semaphore()
    for wanted, device in peers:

        @pl.when(wanted)
        def _():
            pl.semaphore_signal(barrier, inc=1, device_id=device, device_id_type=MESH)

    pl.semaphore_wait(barrier, sum(jnp.asarray(wanted, jnp.int32) for wanted, _ in peers))


def plane_peers(n):
    me = lax.axis_index("sp")
    return [(True, {"sp": lax.rem(me + step, n)}) for step in range(1, n)]


def remote(source, target, send_sem, recv_sem, device):
    device = device if isinstance(device, dict) else {"sp": device}
    return pltpu.make_async_remote_copy(
        src_ref=source, dst_ref=target, send_sem=send_sem, recv_sem=recv_sem, device_id=device, device_id_type=MESH
    )


def lanes_first():
    return lax.broadcasted_iota(jnp.int32, (1, WIDE), 1) < HEAD_DIM


def halves(value):
    keep = lanes_first()
    zero = jnp.zeros_like(value)
    return jnp.where(keep, value, zero), jnp.where(keep, zero, value)


def causal(rows):
    return lax.broadcasted_iota(jnp.int32, (rows, rows), 0) >= lax.broadcasted_iota(jnp.int32, (rows, rows), 1)


def to_owners(lay, me, cols, slot, source, target, send_sems, recv_sem, local_sem, wanted):
    started = []
    for number, (owner, is_long, start, rows, pair, unit) in enumerate(lay.owners()):
        if pair not in wanted:
            continue
        piece = source.at[pl.ds(start, rows), pl.ds(cols(pair), WIDE)]
        place = target(unit + me * rows, rows)
        far = remote(piece, place, send_sems.at[slot(number)], recv_sem, owner)
        near = pltpu.make_async_copy(piece, place, local_sem)

        @pl.when(me != owner)
        def _():
            far.start()

        @pl.when(me == owner)
        def _():
            near.start()
            near.wait()

        started.append((owner, far))
    return started


def finish_sends(me, started):
    for owner, copy in started:

        @pl.when(me != owner)
        def _():
            copy.wait_send()


def wait_unit(lay, is_short, buffer, sem):
    for short, rows in ((True, 3 * (lay.n - 1) * lay.short), (False, (lay.n - 1) * lay.long)):

        @pl.when(is_short == short)
        def _():
            piece = buffer.at[pl.ds(0, rows)]
            pltpu.make_async_copy(piece, piece, sem).wait()


def send_home(lay, me, is_short, seq, first_pair, base, block, unit_start, source, target, base_col, send_sem, recv_sem, local_sem):
    for short, rows in ((True, lay.short), (False, lay.long)):

        @pl.when(is_short == short)
        def _():
            pair = first_pair + (unit_start // LEN_A if short else 0)
            column = pl.multiple_of(base_col + pair * WIDE, WIDE)
            first = pl.multiple_of(seq * rows + (0 if short else lay.split), 16)
            for part in range(BLOCK // rows):
                home = block * (BLOCK // rows) + part
                piece = source.at[pl.ds(pl.multiple_of(base + part * rows, 16), rows)]
                place = target.at[pl.ds(first, rows), pl.ds(column, WIDE)]

                @pl.when(home != me)
                def _():
                    remote(piece, place, send_sem, recv_sem, home).start()

                @pl.when(home == me)
                def _():
                    near = pltpu.make_async_copy(piece, place, local_sem)
                    near.start()
                    near.wait()


def wait_home(lay, is_short, scratch, sem, tensors, sent):
    for short in (True, False):
        own = 3 * lay.short if short else lay.long
        if sent:
            rows = (3 * LEN_A if short else LEN_B) - own
        else:
            rows = PAIRS * lay.sequences * (lay.short + lay.long) - own

        @pl.when(is_short == short)
        def _():
            for _ in range(tensors):
                piece = scratch.at[pl.ds(0, rows)]
                pltpu.make_async_copy(piece, piece, sem).wait()


class Planes:
    def __init__(self, n_dp):
        self.n = n_dp
        self.me = lax.axis_index("dp")
        self.outer = jnp.logical_or(self.me == 0, self.me == n_dp - 1)
        self.inner = jnp.logical_not(self.outer)
        self.inward = jnp.where(self.me == 0, 1, n_dp - 2)
        self.hosts = jnp.logical_or(self.me == 1, self.me == n_dp - 2)
        self.guest = jnp.where(self.me == 1, 0, n_dp - 1)

    def peers(self, n_sp):
        me = lax.axis_index("sp")
        found = plane_peers(n_sp)
        for sp in range(n_sp):
            found.append((self.outer, {"sp": sp, "dp": self.inward}))
            found.append((self.hosts, {"sp": sp, "dp": self.guest}))
        far = jnp.logical_and(self.inner, self.me + 1 < self.n - 1)
        found.append((far, {"sp": me, "dp": self.me + 1}))
        far = jnp.logical_and(self.inner, self.me - 1 > 0)
        found.append((far, {"sp": me, "dp": self.me - 1}))
        return found

    def takes(self, trained, up):
        other = self.me + 1 if up else self.me - 1
        low, high = (1, self.n - 2) if trained else (0, self.n - 1)
        return jnp.logical_and(other >= low, other <= high)


class Weights:
    def __init__(self, planes, own, every, send, recv):
        self.planes, self.own, self.every = planes, own, every
        self.send, self.recv = send, recv

    def copy(self, array, index, up, source):
        other = self.planes.me + 1 if up else self.planes.me - 1
        return remote(
            source, self.every[array].at[index], self.send.at[int(up), array, index], self.recv.at[array, index],
            {"dp": other},
        )

    def begin(self, arrays, wanted):
        me = self.planes.me
        for array in arrays:
            for up in (True, False):

                @pl.when(jnp.logical_and(wanted, self.planes.takes(array < 2, up)))
                def _():
                    self.copy(array, me, up, self.own[array]).start()

    def pairs(self, array, distance):
        me, n = self.planes.me, self.planes.n
        used = self.planes.inner if array < 2 else True
        for up in (True, False):
            index = me - distance if up else me + distance
            comes = jnp.logical_and(used, jnp.logical_and(index >= 0, index < n))
            yield comes, jnp.logical_and(comes, self.planes.takes(array < 2, up)), jnp.clip(index, 0, n - 1), up

    def pass_on(self, arrays, distance, of_ends=None):
        for array in arrays:
            for comes, goes, index, up in self.pairs(array, distance):
                if of_ends is not None:
                    end = jnp.logical_or(index == 0, index == self.planes.n - 1)
                    chosen = end if of_ends else jnp.logical_not(end)
                    comes, goes = jnp.logical_and(comes, chosen), jnp.logical_and(goes, chosen)

                @pl.when(comes)
                def _():
                    place = self.every[array].at[index]
                    pltpu.make_async_copy(place, place, self.recv.at[array, index]).wait()

                @pl.when(goes)
                def _():
                    self.copy(array, index, up, self.every[array].at[index]).start()

    def finish(self):
        for array in range(4):
            for distance in range(self.planes.n):
                for _, goes, index, up in self.pairs(array, distance):
                    goes = goes if distance else self.planes.takes(array < 2, up)

                    @pl.when(goes)
                    def _():
                        self.copy(array, index, up, self.every[array].at[index]).wait_send()


ROWS = 256
LIMIT = 60 * 2**20


def gelu_parts(value):
    root = 0.7978845608028654
    square = value * value
    bent = jnp.tanh(root * value * (1.0 + 0.044715 * square))
    half = 0.5 + 0.5 * bent
    slope = half + 0.5 * value * (1.0 - bent * bent) * (root + 3.0 * 0.044715 * root * square)
    return value * half, slope


def slot_rows(lay, capacity, routes_t):
    n = lay.n
    experts, count = 2 * n, routes_t.shape[1]
    index = lax.broadcasted_iota(jnp.int32, (experts, count), 0)
    matches = [(index == routes_t[c : c + 1]).astype(F32) for c in range(2)]
    earlier = (
        lax.broadcasted_iota(jnp.int32, (count, count), 0) < lax.broadcasted_iota(jnp.int32, (count, count), 1)
    ).astype(F32)
    rank = dot((matches[0] + matches[1]).astype(BF16), earlier.astype(BF16))
    place = rank + (((index % n) * 2 + index // n) * capacity).astype(F32)
    return [jnp.sum(m * place, axis=0, keepdims=True).astype(jnp.int32) for m in matches]


def upright(routes_t):
    tall = jnp.concatenate([routes_t.astype(F32), jnp.zeros((WIDE - 2, routes_t.shape[1]), F32)], axis=0)
    return jnp.transpose(tall).astype(jnp.int32)


def slot_columns(lay, capacity, routes):
    n = lay.n
    count = routes.shape[0]
    index = lax.broadcasted_iota(jnp.int32, (count, 128), 1)
    matches = [(index == routes[:, c : c + 1]).astype(F32) for c in range(2)]
    earlier = (
        lax.broadcasted_iota(jnp.int32, (count, count), 0) > lax.broadcasted_iota(jnp.int32, (count, count), 1)
    ).astype(F32)
    rank = dot(earlier.astype(BF16), (matches[0] + matches[1]).astype(BF16))
    place = rank + (((index % n) * 2 + index // n) * capacity).astype(F32)
    return [jnp.sum(m * place, axis=1, keepdims=True).astype(jnp.int32) for m in matches], matches


def hot(condition):
    return condition.astype(F32).astype(BF16)


def layer_kernel(
    lay, capacity, n_dp,
    tokens, vec_a, vec_b, vec_c, vec_d, w_router, routes_t, w_qkv_in, w_out_in, cotangent_in, own_a, own_b, own_c, own_d,
    first_norm_out, unit_out, attended_out, log_total_out, home_out, middle_out, second_out, gates_out, got, got_grad, first_grad, second_grad,
    all_a, all_b, all_c, all_d, hop_a, hop_b,
    staged_out, packed, packed_grad, rows_in, rows_grad, weight_a, weight_b, out_sum, in_sum, out_other, in_other, back_out, back_grad, grad_a, grad_b,
    packed_gates, rows_gates, send, recv, out_send, home_recv, local, stream_send, stream_recv, load,
    row_send, row_recv, row_local, back_send, back_recv, back_local, hop_send, hop_recv,
    first_norm, unit, attended, log_total, home, middle, second_norm, out_sems, w_qkv, w_out, cotangent, in_sems,
):
    n = lay.n
    me = lax.axis_index("sp")
    gain_one, shift_one, gain_two, shift_two = (vec[...].reshape(1, -1) for vec in (vec_a, vec_b, vec_c, vec_d))
    planes = Planes(n_dp)
    is_short, seq, first_pair = lay.role(me)
    entering = [
        pltpu.make_async_copy(source, target, in_sems.at[number])
        for number, (source, target) in enumerate(((w_qkv_in, w_qkv), (cotangent_in, cotangent), (w_out_in, w_out)))
    ]
    for copy in entering:
        copy.start()
    meet(planes.peers(n))
    stream = Weights(
        planes, (own_a, own_b, own_c, own_d), (all_a, all_b, all_c, all_d), stream_send, stream_recv
    )
    stream.begin((2, 3), True)

    hat, _ = normed(tokens[...].astype(F32))
    for copy in entering:
        copy.wait()
    first_norm[...] = (hat * gain_one + shift_one).astype(BF16)
    started = []
    for chunk in range(9):
        kind, third = divmod(chunk, 3)
        made = dot(first_norm[...], w_qkv[:, chunk * 2 * WIDE : (chunk + 1) * 2 * WIDE]).astype(BF16)
        made = made * BF16(HEAD_DIM**-0.5) if kind == 0 else made
        area = packed.at[pl.ds(kind * tokens.shape[0], tokens.shape[0]), pl.ds(third * 2 * WIDE, 2 * WIDE)]
        area[...] = made
        count = len(lay.owners())
        started += to_owners(
            lay,
            me,
            lambda pair: (pair % 2) * WIDE,
            lambda number: chunk * count + number,
            area,
            lambda start, rows: unit.at[kind, pl.ds(pl.multiple_of(start, 16), rows)],
            send,
            recv.at[kind],
            local,
            (2 * third, 2 * third + 1),
        )
    span = n * capacity
    width, hidden = grad_a.shape
    count = tokens.shape[0]
    place = slot_rows(lay, capacity, routes_t[...])

    def dispatch_copies(which, kind):
        source, target = ((packed, rows_in), (packed_grad, rows_grad), (packed_gates, rows_gates))[which]
        plane = jnp.where(planes.outer, planes.inward, planes.me) if kind == 0 else planes.me
        area = jnp.where(planes.outer, 1, 0) if kind == 0 else 2

        def block(buffer, number):
            if which == 2:
                return buffer.at[number]
            return buffer.at[pl.ds(pl.multiple_of(number * capacity, 16), capacity)]

        into = block(target, area * n + me)
        for step in range(n):
            to = lax.rem(me + step, n)
            piece = block(source, to * 2 + kind)
            far = remote(
                piece, into, row_send.at[which, kind, step], row_recv.at[which, area, me], {"sp": to, "dp": plane}
            )
            if step:
                yield True, far
                continue
            if kind == 0:
                yield planes.outer, far
            stays = planes.inner if kind == 0 else True
            yield stays, pltpu.make_async_copy(piece, into, row_local.at[which, kind])

    def each(copies, act):
        for condition, copy in copies:
            if condition is True:
                act(copy)
            else:
                pl.when(condition)(functools.partial(act, copy))

    def start(copy):
        copy.start()

    def end(copy):
        if copy.is_remote:
            copy.wait_send()
        else:
            copy.wait()

    def dispatch(which):
        for kind in range(2):
            each(dispatch_copies(which, kind), start)

    for first in range(0, 2 * span, ROWS):
        slots = first + lax.broadcasted_iota(jnp.int32, (ROWS, count), 0)
        chosen = hot(jnp.logical_or(slots == place[0], slots == place[1]))
        packed_grad[first : first + ROWS] = dot(chosen, cotangent[...]).astype(BF16)
    dispatch(1)
    for kind in range(3):
        wait_unit(lay, is_short, unit.at[kind], recv.at[kind])
    keep = lanes_first()
    lower = causal(BLOCK)

    def task(index, carry):
        start, block = lay.task(is_short, index)
        base = pl.multiple_of(start + block * BLOCK, BLOCK)
        queries = halves(unit[0, pl.ds(base, BLOCK)])

        def visit(place, state, diagonal):
            keys = unit[1, pl.ds(place, BLOCK)]
            values = unit[2, pl.ds(place, BLOCK)]
            result = []
            for (peak, total, summed), query in zip(state, queries):
                scores = dot_t(query, keys)
                if diagonal:
                    scores = jnp.where(lower, scores, NEGATIVE)
                new_peak = jnp.maximum(peak, jnp.max(scores, axis=1, keepdims=True))
                factor = jnp.exp(peak - new_peak)
                weight = jnp.exp(scores - new_peak)
                total = total * factor + jnp.sum(weight, axis=1, keepdims=True)
                summed = summed * factor + dot(weight.astype(BF16), values)
                result.append((new_peak, total, summed))
            return tuple(result)

        empty = (jnp.full((BLOCK, 1), NEGATIVE, F32), jnp.zeros((BLOCK, 1), F32), jnp.zeros((BLOCK, WIDE), F32))
        state = lax.fori_loop(
            0, block, lambda j, state: visit(pl.multiple_of(start + j * BLOCK, BLOCK), state, False), (empty, empty)
        )
        (peak_a, total_a, summed_a), (peak_b, total_b, summed_b) = visit(base, state, True)
        result = jnp.where(keep, summed_a / total_a, summed_b / total_b)
        attended[pl.ds(base, BLOCK)] = result
        staged_out[pl.ds(base, BLOCK)] = result.astype(BF16)
        log_total[pl.ds(base, BLOCK)] = jnp.where(keep, peak_a + jnp.log(total_a), peak_b + jnp.log(total_b))
        send_home(
            lay, me, is_short, seq, first_pair, base, block, start, staged_out, home, 0, out_send, home_recv, local
        )
        return carry

    lax.fori_loop(0, lay.tasks(is_short), task, 0)
    finish_sends(me, started)
    wait_home(lay, is_short, staged_out, out_send, 1, True)
    wait_home(lay, is_short, staged_out, home_recv, 1, False)

    stream.pass_on((2, 3), 1)
    stream.begin((0, 1), planes.inner)
    x1 = tokens[...].astype(F32) + dot(home[...], w_out[...])
    middle[...] = x1
    hat, _ = normed(x1)
    second = (hat * gain_two + shift_two).astype(BF16)
    second_norm[...] = second
    leaving = [
        pltpu.make_async_copy(source, target, out_sems.at[number])
        for number, (source, target) in enumerate(
            (
                (first_norm, first_norm_out), (unit, unit_out), (attended, attended_out), (log_total, log_total_out),
                (home, home_out), (middle, middle_out), (second_norm, second_out),
            )
        )
    ]
    for copy in leaving:
        copy.start()
    for first in range(0, 2 * span, ROWS):
        slots = first + lax.broadcasted_iota(jnp.int32, (ROWS, count), 0)
        chosen = hot(jnp.logical_or(slots == place[0], slots == place[1]))
        packed[first : first + ROWS] = dot(chosen, second).astype(BF16)
    dispatch(0)
    logits = dot_t(second, w_router[...])
    routes = upright(routes_t[...])
    index = lax.broadcasted_iota(jnp.int32, logits.shape, 1)
    chosen = [jnp.sum(jnp.where(index == routes[:, c : c + 1], logits, 0.0), axis=1, keepdims=True) for c in range(2)]
    top = jnp.maximum(chosen[0], chosen[1])
    exped = [jnp.exp(value - top) for value in chosen]
    gates = [value / (exped[0] + exped[1]) for value in exped]
    lane = lax.broadcasted_iota(jnp.int32, gates_out.shape, 1)
    gates_out[...] = jnp.where(lane == 0, gates[0], gates[1])
    column, _ = slot_columns(lay, capacity, routes)
    for number in range(2 * n):
        held = [
            jnp.where(jnp.logical_and(lane < capacity, lane + number * capacity == column[c]), gates[c], 0.0)
            for c in range(2)
        ]
        packed_gates[number] = jnp.broadcast_to(jnp.sum(held[0] + held[1], axis=0, keepdims=True), (8, 128))
    dispatch(2)

    def arrived(which, area):
        buffer = (rows_in, rows_grad, rows_gates)[which]
        for src in range(n):
            piece = buffer.at[area * n + src] if which == 2 else buffer.at[pl.ds((area * n + src) * capacity, capacity)]
            wait = pltpu.make_async_copy(piece, piece, row_recv.at[which, area, src]).wait
            if area == 1:
                wait()
            else:
                pl.when(src != me)(wait)

    for which in (1, 0, 2):
        for kind in range(2):
            each(dispatch_copies(which, kind), end)
    stream.begin((0, 1), planes.outer)
    stream.pass_on((2, 3), 2)

    def take(area):
        for which in (1, 0, 2):
            arrived(which, area)
        one = lax.broadcasted_iota(jnp.int32, (capacity, 128), 0) == lax.broadcasted_iota(jnp.int32, (capacity, 128), 1)

        def gated(src, carry):
            gate = jnp.sum(jnp.where(one, rows_gates[area * n + src, 0:1], 0.0), axis=1, keepdims=True)
            part = pl.ds(pl.multiple_of((area * n + src) * capacity, 16), capacity)
            rows_grad[part] = (gate * rows_grad[part].astype(F32)).astype(BF16)
            return carry

        lax.fori_loop(0, n, gated, 0)

    def clear(sums, rows):
        def one(index, carry):
            part = pl.ds(pl.multiple_of(index * ROWS, ROWS), ROWS)
            for total in sums:
                total[part] = jnp.zeros((ROWS, width), F32)
            return carry

        lax.fori_loop(0, rows // ROWS, one, 0)

    last = jnp.maximum(planes.me, n_dp - 1 - planes.me)

    def weight_grads(index):
        stores = [
            pltpu.make_async_copy(stage, whole.at[index], load.at[2 + i])
            for i, (stage, whole) in enumerate(((grad_a, first_grad), (grad_b, second_grad)))
        ]
        tall = 3 * WIDE
        for total in (span, 2 * span):

            @pl.when(planes.hosts == (total > span))
            def _():
                every_row = pl.ds(0, total)
                for col in range(0, width, tall):
                    part = pl.ds(col, tall)
                    grad_a[part] = t_dot(rows_in[every_row, part], packed_grad[every_row, :hidden]).astype(BF16)
                for col in range(0, hidden, tall):
                    part = pl.ds(col, tall)
                    grad_b[part] = t_dot(packed[every_row, part], rows_grad[every_row]).astype(BF16)

        for copy in stores:
            copy.start()
        for copy in stores:
            copy.wait()

    def work(trained, sums, first_row, base, rows, nearest, farthest, passing=True):
        arrays = (0, 1) if trained else (2, 3)
        every = (all_a, all_b) if trained else (all_c, all_d)
        own = (own_a, own_b) if trained else (own_c, own_d)

        def one(step, carry):
            distance, side = step // 2, lax.rem(step, 2)
            index = jnp.where(side == 0, planes.me - distance, planes.me + distance)
            real = jnp.logical_and(jnp.logical_and(index >= 0, index < n_dp), jnp.logical_or(side == 0, distance > 0))

            @pl.when(jnp.logical_and(passing, jnp.logical_and(side == 0, distance >= 3)))
            def _():
                stream.pass_on(arrays, distance)

            @pl.when(real)
            def _():
                near = [pltpu.make_async_copy(own[i], (weight_a, weight_b)[i], load.at[i]) for i in range(2)]
                far = [pltpu.make_async_copy(every[i].at[index], (weight_a, weight_b)[i], load.at[i]) for i in range(2)]

                @pl.when(distance == 0)
                def _():
                    for copy in near:
                        copy.start()

                @pl.when(distance > 0)
                def _():
                    for copy in far:
                        copy.start()

                for copy in near:
                    copy.wait()

                def chunk(number, carry):
                    part = pl.ds(pl.multiple_of(base + number * ROWS, ROWS), ROWS)
                    here = pl.ds(pl.multiple_of(first_row + number * ROWS, ROWS), ROWS)
                    active, slope = gelu_parts(dot(rows_in[here], weight_a[...]))
                    active = active.astype(BF16)
                    back = (dot_t(rows_grad[here], weight_b[...]) * slope).astype(BF16)
                    if trained:
                        packed[part, :hidden] = active
                        packed_grad[part, :hidden] = back
                    sums[0][part] += dot(active, weight_b[...])
                    sums[1][part] += dot_t(back, weight_a[...])
                    return carry

                lax.fori_loop(0, rows // ROWS, chunk, 0)
                if trained:

                    @pl.when(distance < last)
                    def _():
                        weight_grads(index)

            return carry

        lax.fori_loop(2 * nearest, 2 * farthest + 2, one, 0)

    def turn(sums, first_row, base, rows):
        def one(number, carry):
            part = pl.ds(pl.multiple_of(base + number * ROWS, ROWS), ROWS)
            here = pl.ds(pl.multiple_of(first_row + number * ROWS, ROWS), ROWS)
            back_out[here] = sums[0][part].astype(BF16)
            back_grad[here] = sums[1][part].astype(BF16)
            return carry

        lax.fori_loop(0, rows // ROWS, one, 0)

    def back_copies(kind, guest, whiches=(0, 1)):
        area = 2 if kind else int(guest)
        plane = planes.guest if guest else planes.me
        for which in whiches:
            source, target = ((back_out, got), (back_grad, got_grad))[which]
            into = target.at[pl.ds(pl.multiple_of((me * 2 + kind) * capacity, 16), capacity)]
            for step in range(n):
                to = lax.rem(me + step, n)
                piece = source.at[pl.ds(pl.multiple_of((area * n + to) * capacity, 16), capacity)]
                if step or guest:
                    yield True, remote(
                        piece, into, back_send.at[which, area, step], back_recv.at[which, kind, me], {"sp": to, "dp": plane}
                    )
                else:
                    yield True, pltpu.make_async_copy(piece, into, back_local.at[which, kind])

    def hops(act):
        for up in (True, False):
            for array, (whole, hop) in enumerate(((first_grad, hop_a), (second_grad, hop_b))):

                @pl.when(planes.me == (1 if up else n_dp - 2))
                def _():
                    act(
                        remote(
                            whole.at[2 if up else n_dp - 3], hop.at[int(up)], hop_send.at[int(up), array],
                            hop_recv.at[int(up), array], {"dp": planes.me + (1 if up else -1)},
                        )
                    )

    train_sums, frozen_sums = (out_sum, in_sum), (out_other, in_other)
    train_rows = jnp.where(planes.hosts, 2 * span, span)
    clear(frozen_sums, span)

    clear(train_sums, train_rows)

    @pl.when(planes.inner)
    def _():
        take(0)

        @pl.when(planes.hosts)
        def _():
            take(1)

        work(True, train_sums, 0, 0, train_rows, 0, 0)

    take(2)
    work(False, frozen_sums, 2 * span, 0, span, 0, 1)
    stream.pass_on((0, 1), 1, True)
    work(False, frozen_sums, 2 * span, 0, span, 2, n_dp - 1)
    turn(frozen_sums, 2 * span, 0, span)
    each(back_copies(1, False), start)

    @pl.when(planes.inner)
    def _():
        stream.pass_on((0, 1), 1, False)
        work(True, train_sums, 0, 0, train_rows, 1, 1)
        stream.pass_on((0, 1), 2)
        hops(start)
        work(True, train_sums, 0, 0, train_rows, 2, last - 1)

        @pl.when(planes.hosts)
        def _():
            work(True, train_sums, span, span, span, last, last)
            turn(train_sums, span, span, span)
            each(back_copies(0, True), start)

        work(True, train_sums, 0, 0, span, last, last, jnp.logical_not(planes.hosts))
        turn(train_sums, 0, 0, span)
        each(back_copies(0, False), start)
        weight_grads(jnp.where(planes.me > n_dp - 1 - planes.me, 0, n_dp - 1))

    each(back_copies(1, False), end)

    @pl.when(planes.inner)
    def _():
        each(back_copies(0, False), end)

        @pl.when(planes.hosts)
        def _():
            each(back_copies(0, True), end)

    for kind in range(2):
        for which, buffer in enumerate((got, got_grad)):
            for src in range(n):
                piece = buffer.at[pl.ds((src * 2 + kind) * capacity, capacity)]
                comes = jnp.logical_or(src != me, planes.outer) if kind == 0 else src != me
                pl.when(comes)(pltpu.make_async_copy(piece, piece, back_recv.at[which, kind, src]).wait)
    stream.finish()
    for copy in leaving:
        copy.wait()
    hops(end)
    for up in (True, False):
        for array, hop in enumerate((hop_a, hop_b)):

            @pl.when(planes.me == (2 if up else n_dp - 3))
            def _():
                pltpu.make_async_copy(hop.at[int(up)], hop.at[int(up)], hop_recv.at[int(up), array]).wait()


ANY = pl.BlockSpec(memory_space=pl.ANY)


def layer(lay, capacity, n_dp, tokens, vectors, w_router, routes_t, w_qkv, w_out, cotangent, weights):
    count, width = tokens.shape
    n = lay.n
    owners = len(lay.owners())
    span = n * capacity
    shape = jax.ShapeDtypeStruct
    hidden = weights[0].shape[1]
    every = [shape((n_dp, *weight.shape), BF16) for weight in weights]
    return pl.pallas_call(
        functools.partial(layer_kernel, lay, capacity, n_dp),
        out_shape=(
            shape((count, width), BF16),
            shape((3, UNIT, WIDE), BF16),
            shape((UNIT, WIDE), F32),
            shape((UNIT, WIDE), F32),
            shape((count, width), BF16),
            shape((count, width), F32),
            shape((count, width), BF16),
            shape((count, 128), F32),
            shape((2 * span, width), BF16),
            shape((2 * span, width), BF16),
            every[0],
            every[1],
            *every,
            shape((2, *weights[0].shape), BF16),
            shape((2, *weights[1].shape), BF16),
        ),
        in_specs=[VMEM] * 7 + [ANY] * 7,
        out_specs=[ANY] * 7 + [VMEM] + [ANY] * 10,
        scratch_shapes=[
            pltpu.VMEM((UNIT, WIDE), BF16),
            pltpu.VMEM((2 * span, width), BF16),
            pltpu.VMEM((2 * span, width), BF16),
            pltpu.VMEM((3 * span, width), BF16),
            pltpu.VMEM((3 * span, width), BF16),
            pltpu.VMEM((width, hidden), BF16),
            pltpu.VMEM((hidden, width), BF16),
            pltpu.VMEM((2 * span, width), F32),
            pltpu.VMEM((2 * span, width), F32),
            pltpu.VMEM((span, width), F32),
            pltpu.VMEM((span, width), F32),
            pltpu.VMEM((3 * span, width), BF16),
            pltpu.VMEM((3 * span, width), BF16),
            pltpu.VMEM((width, hidden), BF16),
            pltpu.VMEM((hidden, width), BF16),
            pltpu.VMEM((2 * n, 8, 128), F32),
            pltpu.VMEM((3 * n, 8, 128), F32),
            DMA((9 * owners,)),
            DMA((3,)),
            DMA,
            DMA,
            DMA,
            DMA((2, 4, n_dp)),
            DMA((4, n_dp)),
            DMA((4,)),
            DMA((3, 2, n)),
            DMA((3, 3, n)),
            DMA((3, 2)),
            DMA((2, 3, n)),
            DMA((2, 2, n)),
            DMA((2, 2)),
            DMA((2, 2)),
            DMA((2, 2)),
            pltpu.VMEM((count, width), BF16),
            pltpu.VMEM((3, UNIT, WIDE), BF16),
            pltpu.VMEM((UNIT, WIDE), F32),
            pltpu.VMEM((UNIT, WIDE), F32),
            pltpu.VMEM((count, width), BF16),
            pltpu.VMEM((count, width), F32),
            pltpu.VMEM((count, width), BF16),
            DMA((7,)),
            *(pltpu.VMEM(value.shape, BF16) for value in (w_qkv, w_out, cotangent)),
            DMA((3,)),
        ],
        compiler_params=pltpu.CompilerParams(collective_id=0, has_side_effects=True, vmem_limit_bytes=LIMIT),
        cost_estimate=pl.CostEstimate(flops=50 * 10**9, bytes_accessed=100 * 2**20, transcendentals=10**7),
        name="layer",
    )(
        tokens, *vectors, w_router, routes_t, w_qkv, w_out, cotangent, *weights
    )


class Sum:
    def __init__(self, n_sp, n_dp, pieces, quantum, needed, first):
        self.n_sp, self.n_dp = n_sp, n_dp
        self.bits = n_sp.bit_length() - 1
        unit = math.lcm(16 * n_sp * n_dp, quantum)
        units = -(-needed // unit)
        sizes = [first // unit] if first >= unit else []
        left = units - sum(sizes)
        pieces = min(pieces, left)
        sizes += [left // pieces + (p < left % pieces) for p in range(pieces)]
        self.pieces = [(unit * sum(sizes[:p]), unit * size) for p, size in enumerate(sizes)]
        self.early = first >= unit
        self.rows = unit * units
        self.steps = 2 * self.bits + 2

    def order(self, piece):
        later = list(range(1, self.bits))
        return [0] + (later[::-1] if piece % 2 else later)

    def landing(self):
        places, start = [], 0
        for _, rows in self.pieces:
            places.append([])
            for step in range(self.bits + 1):
                rows = rows // 2 if step < self.bits else rows
                places[-1].append((start, rows))
                start += rows
        return places, start

    def bind(self, mine, landed, whole, send, recv):
        self.mine, self.landed, self.whole, self.send, self.recv = mine, landed, whole, send, recv
        self.me, self.plane = lax.axis_index("sp"), lax.axis_index("dp")
        self.places, _ = self.landing()
        self.starts = [[start] for start, _ in self.pieces]
        for piece, (_, rows) in enumerate(self.pieces):
            for bit in self.order(piece):
                rows //= 2
                value = (self.me // (1 << bit)) % 2
                self.starts[piece].append(self.starts[piece][-1] + value * rows)

    def partner(self, bit):
        value = (self.me // (1 << bit)) % 2
        return self.me + (1 - 2 * value) * (1 << bit)

    def peers(self):
        found = [(True, {"sp": self.partner(bit)}) for bit in range(self.bits)]
        return found + [(True, {"dp": lax.rem(self.plane + step, self.n_dp)}) for step in range(1, self.n_dp)]

    def cut(self, start, rows):
        return pl.ds(pl.multiple_of(start, 16), rows)

    def copies(self, piece, step):
        bits = self.bits
        rows = self.pieces[piece][1]
        if step < bits or step > bits + 1:
            level = step if step < bits else 2 * bits + 1 - step
            bit = self.order(piece)[level]
            half = rows >> (level + 1)
            held, kept = self.starts[piece][level], self.starts[piece][level + 1]
            if step < bits:
                start, _ = self.places[piece][step]
                source = self.mine.at[self.cut(2 * held + half - kept, half)]
                target = self.landed.at[pl.ds(start, half)]
            else:
                source = target = self.whole.at[self.cut(kept, half)]
            yield remote(source, target, self.send.at[piece, step, 0], self.recv.at[piece, step, 0], self.partner(bit))
            return
        block = (rows >> bits) // self.n_dp
        base = self.starts[piece][bits]
        start, _ = self.places[piece][bits]
        for far in range(1, self.n_dp):
            other = lax.rem(self.plane + far, self.n_dp)
            if step == bits:
                source = self.mine.at[self.cut(base + other * block, block)]
                target = self.landed.at[self.cut(start + self.plane * block, block)]
            else:
                source = target = self.whole.at[self.cut(base + self.plane * block, block)]
            yield remote(source, target, self.send.at[piece, step, far], self.recv.at[piece, step, far], {"dp": other})

    def start(self, piece, step):
        for copy in self.copies(piece, step):
            copy.start()

    def add(self, piece, step):
        for copy in self.copies(piece, step):
            copy.wait()
        bits, rows = self.bits, self.pieces[piece][1]
        if step > bits:
            return
        start, _ = self.places[piece][step]
        if step < bits:
            size, kept = rows >> (step + 1), self.starts[piece][step + 1]
            for first, count in blocks(size):

                def one(number, carry):
                    part = self.cut(kept + first + number * count[0], count[0])
                    here = self.cut(start + first + number * count[0], count[0])
                    self.mine[part] = (self.mine[part].astype(F32) + self.landed[here].astype(F32)).astype(BF16)
                    return carry

                lax.fori_loop(0, count[1], one, 0)
            return
        block = (rows >> bits) // self.n_dp
        own = self.cut(self.starts[piece][bits] + self.plane * block, block)
        total = self.mine[own].astype(F32)
        for far in range(1, self.n_dp):
            other = lax.rem(self.plane + far, self.n_dp)
            total = total + self.landed[self.cut(start + other * block, block)].astype(F32)
        self.whole[own] = total.astype(BF16)


def blocks(rows, size=512):
    found = []
    if rows >= size:
        found.append((0, (size, rows // size)))
    if rows % size:
        found.append((rows - rows % size, (rows % size, 1)))
    return found


def run_sum(total, ahead, ready, done, between):
    begun = [-(piece // 2) for piece in range(len(total.pieces) - total.early)]
    begun = [ahead] * total.early + begun
    rounds = 0
    while any(step <= total.steps for step in begun):
        for piece, step in enumerate(begun):
            if 0 < step <= total.steps:
                total.add(piece, step - 1)
                if step == total.steps:
                    done(piece)
            if step == 0:
                ready(piece)
            if 0 <= step < total.steps:
                total.start(piece, step)
            begun[piece] += 1
        between(rounds)
        rounds += 1


class Gather:
    def __init__(self, n, own, hop, below, above, theirs, sums, send, recv, load):
        self.n, self.own, self.hop, self.below, self.above = n, own, hop, below, above
        self.theirs, self.sums, self.send, self.recv, self.load = theirs, sums, send, recv, load
        self.me = lax.axis_index("dp")
        self.inner = jnp.logical_and(self.me >= 1, self.me <= n - 2)

    def copy(self, array, index, up, source):
        target = (self.below if up else self.above)[array].at[index]
        other = self.me + 1 if up else self.me - 1
        return remote(
            source, target, self.send.at[int(up), array, index], self.recv.at[int(up), array, index], {"dp": other}
        )

    def fetch(self, source, buffer, number):
        moved = pltpu.make_async_copy(source, buffer, self.load.at[number])
        moved.start()
        return moved

    def wanted(self, index, up):
        return jnp.logical_and(self.inner, index > self.me if up else index < self.me)

    def begins(self, up):
        return self.me == 1 if up else self.me == self.n - 2

    def hopped(self, index, up):
        return index == (2 if up else self.n - 3)

    def begin(self, array, index, up):
        if self.hopped(index, up):
            return

        @pl.when(jnp.logical_and(self.wanted(index, up), self.begins(up)))
        def _():
            self.copy(array, index, up, self.own[array].at[index]).start()

    def came(self, array, index, up):
        buffer = (self.below if up else self.above)[array].at[index]
        pltpu.make_async_copy(buffer, buffer, self.recv.at[int(up), array, index]).wait()
        return buffer

    def pass_on(self, array, index, up):
        @pl.when(jnp.logical_and(self.wanted(index, up), jnp.logical_not(self.begins(up))))
        def _():
            total, theirs = self.sums[array].at[int(up)], self.theirs[array]
            here = self.fetch(self.own[array].at[index], total, 0)
            self.fetch(self.came(array, index, up), theirs, 1).wait()
            here.wait()
            total[...] = (total[...].astype(F32) + theirs[...].astype(F32)).astype(BF16)
            self.copy(array, index, up, total).start()

    def finish(self, array, index, up):
        waits = self.wanted(index, up)
        if self.hopped(index, up):
            waits = jnp.logical_and(waits, jnp.logical_not(self.begins(up)))

        @pl.when(waits)
        def _():
            self.copy(array, index, up, self.sums[array].at[int(up)]).wait_send()

    def arrived(self, array):
        for up, comes in ((True, self.me > 2), (False, self.me < self.n - 3)):

            @pl.when(comes)
            def _():
                self.came(array, self.me, up)


def gather_scratch(n, first, second):
    shapes = [first.shape[1:], second.shape[1:]]
    return [
        *(pltpu.VMEM(shape, BF16) for shape in shapes),
        *(pltpu.VMEM((2, *shape), BF16) for shape in shapes),
        DMA((2, 2, n)),
        DMA((2, 2, n)),
        DMA((5,)),
    ]


def back_kernel(
    lay, capacity, replicated,
    got, got_grad, middle, second_norm, gates, home_out, w_out, vec_a, vec_b, w_router, routes_t, cotangent,
    unit_in, attended, log_total_in, first_norm_in, tokens, w_qkv_in, first_own, second_own, hop_a, hop_b,
    block_out, tokens_grad, qkv_grad, out_proj_grad, router_out, vectors_out, below_a, below_b, above_a, above_b,
    grad_attended, grad_out, deltas, query_sum, staged, home, send, recv, out_send, home_recv, local,
    theirs_a, theirs_b, sums_a, sums_b, pass_send, pass_recv, load,
    grads, landed, summed, sum_send, sum_recv, out_sems, unit, log_total, first_norm, w_qkv, late_sems,
):
    n_dp = first_own.shape[0]
    gather = Gather(
        n_dp, (first_own, second_own), (hop_a, hop_b), (below_a, below_b), (above_a, above_b), (theirs_a, theirs_b),
        (sums_a, sums_b), pass_send, pass_recv, load,
    )
    gain_one, gain_two = (vec[...].reshape(1, -1) for vec in (vec_a, vec_b))
    replicated.bind(grads, landed, summed, sum_send, sum_recv)
    me = lax.axis_index("sp")
    is_short, seq, first_pair = lay.role(me)
    everywhere = [(True, {"dp": lax.rem(gather.me + step, n_dp)}) for step in range(1, n_dp)]
    late = [
        pltpu.make_async_copy(source, target, late_sems.at[number])
        for number, (source, target) in enumerate(
            ((attended, deltas), (unit_in, unit), (log_total_in, log_total), (first_norm_in, first_norm), (w_qkv_in, w_qkv))
        )
    ]
    for copy in late:
        copy.start()
    meet(plane_peers(lay.n) + everywhere)
    inside = [(up, index) for index in range(1, n_dp - 1) for up in (True, False)]
    ends = [(True, n_dp - 1), (False, 0)]
    for up, index in ends:
        gather.begin(0, index, up)
    place, matches = slot_columns(lay, capacity, upright(routes_t[...]))
    slots = lax.broadcasted_iota(jnp.int32, (tokens.shape[0], got.shape[0]), 1)
    chosen = [hot(slots == place[c]) for c in range(2)]
    upstream = cotangent[...].astype(F32)
    gate = [gates[:, c : c + 1] for c in range(2)]
    total = middle[...]
    grad_gate = []
    for c in range(2):
        produced = dot(chosen[c], got[...])
        total = total + gate[c] * produced
        grad_gate.append(jnp.sum(upstream * produced, axis=1, keepdims=True))
    block_out[...] = total.astype(BF16)
    mean_grad = gate[0] * grad_gate[0] + gate[1] * grad_gate[1]
    grad_logits = sum(matches[c] * (gate[c] * (grad_gate[c] - mean_grad)) for c in range(2))
    high = grad_logits.astype(BF16)
    low = (grad_logits - high.astype(F32)).astype(BF16)
    experts = w_router.shape[0]
    grad_second = dot(high[:, :experts], w_router[...]) + dot(low[:, :experts], w_router[...])
    grad_second = grad_second + dot(chosen[0] + chosen[1], got_grad[...])
    hat, scale = normed(middle[...])
    grad = upstream + norm_back(grad_second, gain_two, hat, scale)
    tokens_grad[...] = grad
    branch = grad.astype(BF16)
    grad_attended[...] = dot_t(branch, w_out[...]).astype(BF16)
    width = w_out.shape[0]

    started = to_owners(
        lay,
        me,
        lambda pair: pair * WIDE,
        lambda number: number,
        grad_attended,
        lambda start, rows: grad_out.at[pl.ds(pl.multiple_of(start, 16), rows)],
        send,
        recv,
        local,
        range(PAIRS),
    )
    for up, index in ends:
        gather.begin(1, index, up)
    def put(column, value):
        for lane in range(0, value.shape[1], WIDE):
            grads[pl.ds((column + lane) // WIDE * width, width)] = value[:, lane : lane + WIDE].astype(BF16)

    put(0, t_dot(home_out[...], branch))
    moments = (2, 3, 5, 6, 7)
    if replicated.early:
        replicated.start(0, 0)
    router_grad = t_dot(second_norm[...], high) + t_dot(second_norm[...], low)
    gain_two_grad = jnp.sum(grad_second * hat, axis=0, keepdims=True)
    shift_two_grad = jnp.sum(grad_second, axis=0, keepdims=True)
    query_sum[...] = jnp.zeros_like(query_sum)
    keep = lanes_first()
    lower = causal(BLOCK)
    wait_unit(lay, is_short, grad_out, recv)
    for copy in late:
        copy.wait()

    def make_delta(index, carry):
        part = pl.ds(pl.multiple_of(index * BLOCK, BLOCK), BLOCK)
        first, second = halves(grad_out[part].astype(F32) * deltas[part])
        deltas[part] = jnp.where(
            keep, jnp.sum(first, axis=1, keepdims=True), jnp.sum(second, axis=1, keepdims=True)
        )
        return carry

    lax.fori_loop(0, lay.tasks(is_short), make_delta, 0)
    per = jnp.where(is_short, LEN_A // BLOCK, LEN_B // BLOCK)

    def task(index, carry):
        start, block = lay.task(is_short, index)
        base = pl.multiple_of(start + block * BLOCK, BLOCK)
        keys = unit[1, pl.ds(base, BLOCK)]
        values = unit[2, pl.ds(base, BLOCK)]
        key_both = jnp.concatenate(halves(keys), axis=0)

        def visit(place, state, diagonal):
            part = pl.ds(place, BLOCK)
            grad_key, grad_value = state
            queries = halves(unit[0, part])
            outs = halves(grad_out[part])
            weights, grads = [], []
            for which, (query, out) in enumerate(zip(queries, outs)):
                column = which * HEAD_DIM
                scores = dot_t(query, keys)
                if diagonal:
                    scores = jnp.where(lower, scores, NEGATIVE)
                weight = jnp.exp(scores - log_total[part, column : column + 1])
                grad = weight * (dot_t(out, values) - deltas[part, column : column + 1])
                weights.append(weight.astype(BF16))
                grads.append(grad.astype(BF16))
            grad_value = grad_value + t_dot(jnp.concatenate(weights, axis=0), jnp.concatenate(outs, axis=0))
            grad_key = grad_key + t_dot(jnp.concatenate(grads, axis=0), jnp.concatenate(queries, axis=0))
            query_sum[part] += dot(jnp.concatenate(grads, axis=1), key_both)
            return grad_key, grad_value

        zero = jnp.zeros((BLOCK, WIDE), F32)
        state = visit(base, (zero, zero), True)
        grad_key, grad_value = lax.fori_loop(
            block + 1, per, lambda i, state: visit(pl.multiple_of(start + i * BLOCK, BLOCK), state, False), state
        )
        part = pl.ds(base, BLOCK)
        staged[0, part] = (query_sum[part] * HEAD_DIM**-0.5).astype(BF16)
        staged[1, part] = grad_key.astype(BF16)
        staged[2, part] = grad_value.astype(BF16)
        for kind in range(3):
            send_home(
                lay, me, is_short, seq, first_pair, base, block, start, staged.at[kind], home, kind * PAIRS * WIDE,
                out_send.at[kind], home_recv.at[kind], local,
            )
        @pl.when(index == 1)
        def _():
            for up, which in ends:
                gather.pass_on(0, which, up)

        for step, moment in enumerate(moments if replicated.early else ()):

            @pl.when(index == moment)
            def _():
                replicated.add(0, step)
                replicated.start(0, step + 1)

        return carry

    lax.fori_loop(0, lay.tasks(is_short), task, 0)
    for up, index in ends:
        gather.pass_on(1, index, up)
    for array in range(2):
        for up, index in inside:
            gather.begin(array, index, up)
    for kind in range(3):
        wait_home(lay, is_short, staged.at[kind], home_recv.at[kind], 1, False)
    first, last = PAIRS, 4 * PAIRS

    def ready(piece):
        start, rows = replicated.pieces[piece]
        for column in range(start // width, (start + rows) // width, 2):
            if column == last:
                grads[pl.ds(column * width, width)] = router_grad.astype(BF16)
                parts = (*extra, gain_two_grad, shift_two_grad)
                rows = [part[:, lane : lane + WIDE] for part in parts for lane in range(0, width, WIDE)]
                rows.append(jnp.zeros((width - len(rows), WIDE), F32))
                grads[pl.ds((column + 1) * width, width)] = jnp.concatenate(rows, axis=0).astype(BF16)
            elif column > last:
                grads[pl.ds(column * width, 2 * width)] = jnp.zeros((2 * width, WIDE), BF16)
            elif first <= column:
                lanes = pl.ds((column - first) * WIDE, 2 * WIDE)
                put(column * WIDE, t_dot(first_norm[...], home[:, lanes]))

    stores, extra = [], []

    def done(piece):
        start, rows = replicated.pieces[piece]
        for column in range(start // width, (start + rows) // width, 2):
            parts = [summed.at[pl.ds((column + i) * width, width)] for i in range(2)]
            if column == last:
                router_out[...] = jnp.transpose(parts[0][...].astype(F32))[: router_out.shape[0]]
                vectors_out[...] = parts[1][0:32].astype(F32)
            elif column < last:
                for i in range(2):
                    target, lane = (out_proj_grad, column) if column < first else (qkv_grad, column - first)
                    lanes = pl.ds((lane + i) * WIDE, WIDE)
                    stores.append(pltpu.make_async_copy(parts[i], target.at[:, lanes], out_sems.at[len(stores)]))
                    stores[-1].start()

    def between(number):
        if number == 0:
            grad_first = dot_t(home[...], w_qkv[...])
            hat, scale = normed(tokens[...].astype(F32))
            extra.append(jnp.sum(grad_first * hat, axis=0, keepdims=True))
            extra.append(jnp.sum(grad_first, axis=0, keepdims=True))
            tokens_grad[...] += norm_back(grad_first, gain_one, hat, scale)
        if number in (7, 8):
            array = number - 7
            for up, index in inside:
                gather.pass_on(array, index, up)
            for up, index in inside + ends:
                gather.finish(array, index, up)
            gather.arrived(array)

    run_sum(replicated, len(moments) + 1, ready, done, between)
    for store in stores:
        store.wait()
    finish_sends(me, started)
    for kind in range(3):
        wait_home(lay, is_short, staged.at[kind], out_send.at[kind], 1, True)


def backward(lay, capacity, values):
    count, width = values[2].shape
    owners = len(lay.owners())
    shape = jax.ShapeDtypeStruct
    slices = values[-4:-2]
    late = [values[number] for number in (12, 14, 15, 17)]
    replicated = Sum(lay.n, slices[0].shape[0], 6, 2 * width, 26 * width, width // WIDE * width)
    return pl.pallas_call(
        functools.partial(back_kernel, lay, capacity, replicated),
        out_shape=(
            shape((count, width), BF16), shape((count, width), F32),
            shape((width, 3 * width), BF16), shape((width, width), BF16), shape(values[9].shape, F32), shape((32, WIDE), F32),
            *(shape(g.shape, BF16) for g in slices * 2),
        ),
        in_specs=[VMEM] * 12 + [ANY] * 4 + [VMEM] + [ANY] * 5,
        out_specs=[VMEM] * 2 + [ANY] * 2 + [VMEM] * 2 + [ANY] * 4,
        scratch_shapes=[
            pltpu.VMEM((count, width), BF16),
            pltpu.VMEM((UNIT, WIDE), BF16),
            pltpu.VMEM((UNIT, WIDE), F32),
            pltpu.VMEM((UNIT, WIDE), F32),
            pltpu.VMEM((3, UNIT, WIDE), BF16),
            pltpu.VMEM((count, 3 * width), BF16),
            DMA((owners,)),
            DMA,
            DMA((3,)),
            DMA((3,)),
            DMA,
            *gather_scratch(slices[0].shape[0], *slices),
            pltpu.VMEM((replicated.rows, WIDE), BF16),
            pltpu.VMEM((replicated.landing()[1], WIDE), BF16),
            pltpu.VMEM((replicated.rows, WIDE), BF16),
            DMA((len(replicated.pieces), replicated.steps, slices[0].shape[0])),
            DMA((len(replicated.pieces), replicated.steps, slices[0].shape[0])),
            DMA((4 * PAIRS,)),
            *(pltpu.VMEM(value.shape, value.dtype) for value in late),
            DMA((5,)),
        ],
        compiler_params=pltpu.CompilerParams(collective_id=1, has_side_effects=True, vmem_limit_bytes=LIMIT),
        cost_estimate=pl.CostEstimate(flops=16 * 10**9, bytes_accessed=60 * 2**20, transcendentals=5 * 10**6),
        name="backward",
    )(*values)


def shards(
    tokens, ln1_gain, ln1_shift, w_qkv, w_out, ln2_gain, ln2_shift, w_router,
    train_w1, train_w2, frozen_w1, frozen_w2, routes, cotangent,
):
    lay = Layout(lax.axis_size("sp"))
    n_dp = lax.axis_size("dp")
    tokens, routes, cotangent = tokens[0], routes[0], cotangent[0]
    count, width = tokens.shape
    capacity = 2 * count // lay.n
    router_t, routes_t = w_router.T, routes.T
    weights = [weight[0] for weight in (train_w1, train_w2, frozen_w1, frozen_w2)]
    (
        first_norm, unit, attended, log_total, home, middle, second, gates, got, got_grad, first_grad, second_grad,
        _, _, _, _, hop_a, hop_b,
    ) = layer(
        lay, capacity, n_dp, tokens, (ln1_gain, ln1_shift, ln2_gain, ln2_shift), router_t, routes_t, w_qkv, w_out, cotangent,
        weights,
    )
    block_out, tokens_grad, qkv_grad, out_proj, router, vector_rows, below_a, below_b, above_a, above_b = backward(
        lay, capacity,
        (
            got, got_grad, middle, second, gates, home, w_out, ln1_gain, ln2_gain, router_t, routes_t, cotangent,
            unit, attended, log_total, first_norm, tokens, w_qkv, first_grad, second_grad, hop_a, hop_b,
        ),
    )
    plane = lax.axis_index("dp")

    def total(own, hop, below, above):
        at = lambda whole: lax.dynamic_index_in_dim(whole, plane, 0, keepdims=False).astype(F32)
        inner = jnp.logical_and(plane >= 1, plane <= n_dp - 2)
        up = jnp.where(plane == 2, hop[1].astype(F32), jnp.where(plane > 2, at(below), 0.0))
        down = jnp.where(plane == n_dp - 3, hop[0].astype(F32), jnp.where(plane < n_dp - 3, at(above), 0.0))
        return jnp.where(inner, at(own), 0.0) + up + down

    found = vector_rows[: 4 * width // WIDE].reshape(4, width)
    return (
        block_out[None],
        tokens_grad[None],
        found[0],
        found[1],
        qkv_grad.astype(F32),
        out_proj.astype(F32),
        found[2],
        found[3],
        router.T,
        total(first_grad, hop_a, below_a, above_a)[None],
        total(second_grad, hop_b, below_b, above_b)[None],
    )


def solution(mesh):
    in_specs = (
        P("dp", "sp", None), P(), P(), P(), P(), P(), P(), P(),
        P("sp", None, "dp"), P("sp", "dp", None), P("sp", None, "dp"), P("sp", "dp", None),
        P("dp", "sp", None), P("dp", "sp", None),
    )
    out_specs = (
        P("dp", "sp", None), P("dp", "sp", None), P(), P(), P(), P(), P(), P(), P(),
        P("sp", None, "dp"), P("sp", "dp", None),
    )
    return jax.shard_map(shards, mesh=mesh, in_specs=in_specs, out_specs=out_specs, check_vma=False)
```
